512 devices in a mesh: user: 128 (over z, y, core), head: 4 (over x).
Axes of the slice: x: 4, y: 8, z: 8, core: 2. Of those that a mesh axis runs over, the one named last changes fastest.
Arguments:
- events: bfloat16 [65536, 1024], P('user', 'head'), may hold values from -6 to 6
- norm_gain: float32 [1024], replicated, may hold values from 0.1 to 1.9
- w_uvqk: bfloat16 [1024, 4, 1024], P(None, None, 'head'), may hold values from -0.1875 to 0.1875
- w_out: bfloat16 [1024, 1024], P('head'), may hold values from -0.1875 to 0.1875
- cache_keys: bfloat16 [1024, 512, 1024], P('user', None, 'head'), may hold values from -6 to 6
- cache_values: bfloat16 [1024, 512, 1024], P('user', None, 'head'), may hold values from -6 to 6
- lengths: int32 [1024], P('user'), may hold values from 1 to 4, as said below
- swap_offset: int32 [1024], P('user'), may hold values from -1 to 1, as said below
Outputs:
- mixed: bfloat16 [65536, 1024], P('user', 'head')
The draws below stay inside these ranges and needn't reach their ends.
Inputs may be any that keep to these rules, and one draw needn't show every extreme that they name: The cached user holds lengths * 128 used positions of its 512; some user has 4 blocks. `swap_offset`: for slot d * 8 + j, the offset is 0 or +1 where d - j is even and 0 or -1 where d - j is odd (device indices along user taken around the cycle); a slot with +1 and the slot of the same index j on the next device, which then has -1, trade their users. Every device has at least one slot with +1 and at least one with -1.
All inputs are finite; a program needn't handle non-finite values.
Results may differ from the reference program's by a relative error of at most 0.0055.
Values may be sent and summed in bfloat16 or wider, within the bound.
No kernel may reach another device: no remote copies, remote signals or barrier semaphores. Data moves between devices by JAX's collectives and lax.ppermute only.
A program may use at most 64 MiB of HBM per device.

```python
import jax
import jax.numpy as jnp
from jax import lax

D = 1024
HEAD = 64
NEW = 64
BLOCK = 128
MAXB = 4
U_DEV = 8
CAP = 512
USERS = 1024
N_USER = 128


def draw_layout(key):
    user_total = U_DEV * N_USER
    lengths = jax.random.randint(jax.random.fold_in(key, 11), (user_total,), 1, MAXB + 1)
    longest = jax.random.randint(jax.random.fold_in(key, 12), (), 0, user_total)
    lengths = jnp.where(jnp.arange(user_total) == longest, MAXB, lengths).astype(jnp.int32)
    length_grid = lengths.reshape(N_USER, U_DEV)
    device_load = jnp.sum(length_grid, axis=1)
    device = jnp.arange(N_USER)[:, None]
    column = jnp.arange(U_DEV)[None, :]
    goes_right = (device - column) % 2 == 0
    partner_len = jnp.where(goes_right, jnp.roll(length_grid, -1, axis=0), jnp.roll(length_grid, 1, axis=0))
    partner_load = jnp.where(goes_right, jnp.roll(device_load, -1)[:, None], jnp.roll(device_load, 1)[:, None])
    own_load = device_load[:, None]
    trading = (length_grid > partner_len) & (own_load > partner_load) | (length_grid < partner_len) & (own_load < partner_load)
    picked = jax.random.randint(jax.random.fold_in(key, 13), (N_USER,), 0, U_DEV // 2)
    forced_col = (jnp.arange(N_USER) % 2 + 2 * picked)[:, None]
    forced_prev = jnp.roll(forced_col, 1, axis=0)
    always = jnp.where(goes_right, column == forced_col, column == forced_prev)
    trading = trading | always
    offset = jnp.where(trading, jnp.where(goes_right, 1, -1), 0).astype(jnp.int32)
    return (lengths, offset.reshape(user_total))


def draw_lengths(key, part):
    lengths, offset = draw_layout(key)
    return lengths


def draw_swap_offset(key, part):
    lengths, offset = draw_layout(key)
    return offset


def levels(key, dims, cuts, low, top_value):
    loudness = 1.0
    for dim, blocks in cuts:
        heights = jax.random.uniform(jax.random.fold_in(jax.random.fold_in(key, 6), dim), (blocks,), jnp.float32, low / len(cuts), top_value / len(cuts))
        loudness = loudness * jnp.repeat(jnp.exp(heights), dims[dim] // blocks).reshape((-1,) + (1,) * (len(dims) - 1 - dim))
    return loudness


def noise(stream_key, extent, scale, reach, pieces=(), held_as=jnp.bfloat16):
    loudness = levels(stream_key, extent, pieces, -0.22, 0.18) if pieces else 1.0
    result = jax.random.normal(stream_key, extent, jnp.float32) * scale * loudness
    return jnp.minimum(jnp.maximum(result, -reach), reach).astype(held_as)


def setup_inputs(seed: int = 0) -> dict:
    splits = jax.random.split(jax.random.key(seed), 9)
    return {
        "events": noise(splits[0], (USERS * NEW, D), 1.0, 6.0, ((0, 128), (1, 4))),
        "norm_gain": jnp.clip(1.0 + 0.18 * jax.random.normal(splits[1], (D,), jnp.float32), 0.1, 1.9),
        "w_uvqk": noise(splits[2], (D, 4, D), D ** -0.5, 0.1875, ((2, 4),)),
        "w_out": noise(splits[3], (D, D), D ** -0.5, 0.1875, ((0, 4),)),
        "cache_keys": noise(splits[4], (USERS, CAP, D), 1.0, 6.0, ((0, 128), (2, 4))),
        "cache_values": noise(splits[5], (USERS, CAP, D), 1.0, 6.0, ((0, 128), (2, 4))),
        "lengths": draw_lengths(jax.random.fold_in(splits[8], 71), 0),
        "swap_offset": draw_swap_offset(jax.random.fold_in(splits[8], 71), 0),
    }


def layer_norm(values, epsilon):
    average = lax.optimization_barrier(jnp.mean(values, axis=-1, keepdims=True))
    centred = values - average
    spread = lax.optimization_barrier(jnp.mean(centred * centred, axis=-1, keepdims=True))
    return centred * lax.rsqrt(spread + epsilon)

def rounded(values):
    return lax.optimization_barrier(values.astype(jnp.bfloat16)).astype(jnp.float32)

def reference(events, norm_gain, w_uvqk, w_out, cache_keys, cache_values, lengths, swap_offset):
    head_count = D // HEAD
    score_scale = HEAD ** (-0.5)
    residual = events.astype(jnp.float32)
    normed = (layer_norm(residual, 1e-05) * norm_gain.astype(jnp.float32)).astype(jnp.bfloat16)
    projected = jnp.dot(normed, w_uvqk.reshape(D, 4 * D), preferred_element_type=jnp.float32)
    branches = lax.optimization_barrier(jax.nn.silu(projected).astype(jnp.bfloat16))
    branches = branches.reshape(USERS, NEW, 4, head_count, HEAD)
    slot_ids = jnp.arange(USERS, dtype=jnp.int32)
    slot_device = slot_ids // U_DEV
    home_user = (slot_device + swap_offset) % N_USER * U_DEV + slot_ids % U_DEV
    position = jnp.arange(CAP, dtype=jnp.int32)
    causal = jnp.arange(NEW)[:, None] >= jnp.arange(NEW)[None, :]

    def serve(slot_item):
        slot_index, slot_rows = slot_item
        source = home_user[slot_index]
        key_heads = cache_keys[source].astype(jnp.float32).reshape(CAP, head_count, HEAD)
        value_heads = cache_values[source].astype(jnp.float32).reshape(CAP, head_count, HEAD)
        slot_float = slot_rows.astype(jnp.float32)
        gate_u = slot_float[:, 0]
        fresh_values = slot_float[:, 1]
        queries = slot_float[:, 2]
        fresh_keys = slot_float[:, 3]
        scores = jnp.einsum('nhe,che->hnc', queries, key_heads) * score_scale
        live_mask = position < lengths[source] * BLOCK
        weight = rounded(jnp.where(live_mask[None, None, :], jax.nn.silu(scores), 0.0))
        attended = jnp.einsum('hnc,che->nhe', weight, value_heads)
        fresh_scores = jnp.einsum('nhe,mhe->hnm', queries, fresh_keys) * score_scale
        fresh_weight = rounded(jnp.where(causal[None], jax.nn.silu(fresh_scores), 0.0))
        attended = attended + jnp.einsum('hnm,mhe->nhe', fresh_weight, fresh_values)
        gated = (layer_norm(attended, 1e-05) * gate_u).astype(jnp.bfloat16)
        return gated.reshape(NEW, D)
    gated = lax.map(serve, (slot_ids, branches))
    partial_terms = jnp.dot(gated.reshape(USERS * NEW, D), w_out, preferred_element_type=jnp.float32)
    return (residual + partial_terms).astype(jnp.bfloat16)
```

```python
import functools

import jax
import jax.numpy as jnp
from jax import lax
from jax.experimental import pallas as pl
from jax.experimental.pallas import tpu as pltpu
from jax.sharding import PartitionSpec as P

HEAD = 64
BLOCK = 128
NT = (((1,), (1,)), ((), ()))
NN = (((1,), (0,)), ((), ()))


def project_kernel(rows, x_ref, gain_ref, w_ref, out_ref):
    parts, total, width = x_ref.shape
    gain = gain_ref[...]
    features = parts * width

    def step(i, carry):
        at = pl.ds(pl.multiple_of(i * rows, rows), rows)
        x = jnp.concatenate([x_ref[p, at, :] for p in range(parts)], axis=1).astype(jnp.float32)
        average = jnp.sum(x, axis=-1, keepdims=True) * (1.0 / features)
        centred = x - average
        spread = jnp.sum(centred * centred, axis=-1, keepdims=True) * (1.0 / features)
        normed = (centred * lax.rsqrt(spread + 1e-05) * gain).astype(jnp.bfloat16)
        half = lax.dot_general(normed, w_ref[...], NN, preferred_element_type=jnp.float32) * 0.5
        out_ref[at, :] = (half + half * jnp.tanh(half)).astype(jnp.bfloat16)
        return carry

    lax.fori_loop(0, total // rows, step, 0)


def project(x4, gain, w):
    parts, total, width = x4.shape
    rows = 128
    return pl.pallas_call(
        functools.partial(project_kernel, rows),
        out_shape=jax.ShapeDtypeStruct((total, w.shape[1]), jnp.bfloat16),
        in_specs=[pl.BlockSpec(memory_space=pltpu.VMEM)] * 3,
        out_specs=pl.BlockSpec(memory_space=pltpu.VMEM),
        compiler_params=pltpu.CompilerParams(vmem_limit_bytes=24 * 2**20),
        cost_estimate=pl.CostEstimate(
            flops=2 * total * w.shape[0] * w.shape[1],
            bytes_accessed=2 * (w.size + 2 * x4.size),
            transcendentals=total * w.shape[1],
        ),
    )(x4, gain, w)


def attend_kernel(
    lengths, offsets, b_ref, keys, values, even, odd, w_ref, out_ref, kv, gated, sems
):
    slots, cap, width = keys.shape
    new = b_ref.shape[0] // slots
    heads = width // HEAD
    half_slots = slots // 2

    def copies(j, k_src, v_src):
        return (
            pltpu.make_async_copy(k_src, kv.at[2 * j], sems.at[2 * j]),
            pltpu.make_async_copy(v_src, kv.at[2 * j + 1], sems.at[2 * j + 1]),
        )

    for j in range(slots):
        moved = odd if j % 2 else even

        @pl.when(offsets[j] == 0)
        def _():
            for c in copies(j, keys.at[j], values.at[j]):
                c.start()

        @pl.when(offsets[j] != 0)
        def _():
            for c in copies(j, moved.at[j // 2], moved.at[half_slots + j // 2]):
                c.start()

    lane_head = lax.broadcasted_iota(jnp.int32, (new, width), 1) // HEAD
    position = lax.broadcasted_iota(jnp.int32, (1, cap), 1)
    row = lax.broadcasted_iota(jnp.int32, (heads * new, new), 0) % new
    causal = row >= lax.broadcasted_iota(jnp.int32, (heads * new, new), 1)
    pair_lane = lax.broadcasted_iota(jnp.int32, (new, 2 * HEAD), 1) // HEAD

    for j in range(slots):
        for c in copies(j, keys.at[j], values.at[j]):
            c.wait()
        at = slice(j * new, (j + 1) * new)
        gate = b_ref[at, :width].astype(jnp.float32)
        fresh_values = b_ref[at, width : 2 * width]
        queries = b_ref[at, 2 * width : 3 * width] * jnp.bfloat16(0.5 * HEAD**-0.5)
        fresh_keys = b_ref[at, 3 * width :]
        zero = jnp.zeros_like(queries)
        spread_q = jnp.concatenate(
            [jnp.where(lane_head == h, queries, zero) for h in range(heads)], axis=0
        )
        half = lax.dot_general(spread_q, kv[2 * j], NT, preferred_element_type=jnp.float32)
        used = jnp.where(offsets[j] == 0, lengths[j] * BLOCK, cap)
        weight = jnp.where(position < used, half + half * jnp.tanh(half), 0.0).astype(jnp.bfloat16)
        total = lax.dot_general(weight, kv[2 * j + 1], NN, preferred_element_type=jnp.float32)
        half = lax.dot_general(spread_q, fresh_keys, NT, preferred_element_type=jnp.float32)
        weight = jnp.where(causal, half + half * jnp.tanh(half), 0.0).astype(jnp.bfloat16)
        total = total + lax.dot_general(
            weight, fresh_values, NN, preferred_element_type=jnp.float32
        )
        for pair in range(heads // 2):
            lanes = slice(2 * HEAD * pair, 2 * HEAD * (pair + 1))
            result = jnp.zeros((new, 2 * HEAD), jnp.float32)
            for side in range(2):
                h = 2 * pair + side
                mine = pair_lane == side
                x = jnp.where(mine, total[h * new : (h + 1) * new, lanes], 0.0)
                average = jnp.sum(x, axis=-1, keepdims=True) * (1.0 / HEAD)
                centred = jnp.where(mine, x - average, 0.0)
                spread = jnp.sum(centred * centred, axis=-1, keepdims=True) * (1.0 / HEAD)
                result = result + centred * lax.rsqrt(spread + 1e-05)
            gated[at, lanes] = (result * gate[:, lanes]).astype(jnp.bfloat16)

    for p in range(out_ref.shape[0]):
        out_ref[p] = lax.dot_general(
            gated[...],
            w_ref[:, p * width : (p + 1) * width],
            NN,
            preferred_element_type=jnp.float32,
        ).astype(jnp.bfloat16)


def attend(lengths, offsets, branches, keys, values, even, odd, w_out):
    slots, cap, width = keys.shape
    rows = branches.shape[0]
    parts = w_out.shape[1] // width
    smem = pl.BlockSpec(memory_space=pltpu.SMEM)
    vmem = pl.BlockSpec(memory_space=pltpu.VMEM)
    hbm = pl.BlockSpec(memory_space=pl.ANY)
    return pl.pallas_call(
        attend_kernel,
        out_shape=jax.ShapeDtypeStruct((parts, rows, width), jnp.bfloat16),
        in_specs=[smem, smem, vmem, hbm, hbm, hbm, hbm, vmem],
        out_specs=vmem,
        scratch_shapes=[
            pltpu.VMEM((2 * slots, cap, width), jnp.bfloat16),
            pltpu.VMEM((rows, width), jnp.bfloat16),
            pltpu.SemaphoreType.DMA((2 * slots,)),
        ],
        compiler_params=pltpu.CompilerParams(vmem_limit_bytes=32 * 2**20),
        cost_estimate=pl.CostEstimate(
            flops=4 * rows * width * (cap + rows // slots) * (width // HEAD),
            bytes_accessed=4 * slots * cap * width + 4 * rows * width * parts,
            transcendentals=rows * (width // HEAD) * cap,
        ),
    )(lengths, offsets, branches, keys, values, even, odd, w_out)


def on_device(events, norm_gain, w_uvqk, w_out, cache_keys, cache_values, lengths, swap_offset):
    slots, cap, width = cache_keys.shape
    users = lax.axis_size("user")
    heads = lax.axis_size("head")

    live = jnp.arange(cap, dtype=jnp.int32)[None, :] < (lengths * BLOCK)[:, None]
    live_values = jnp.where(live[:, :, None], cache_values, jnp.zeros_like(cache_values))

    def payload(side):
        return jnp.concatenate(
            [
                a.reshape(slots // 2, 2, cap, width)[:, side]
                for a in (cache_keys, live_values)
            ],
            axis=0,
        )

    odd = lax.ppermute(
        payload(1), "user", [(i, (((i + 1) ^ 1) - 1) % users) for i in range(users)]
    )
    even = lax.ppermute(payload(0), "user", [(i, i ^ 1) for i in range(users)])

    gathered = lax.all_to_all(
        jnp.broadcast_to(events[None], (heads,) + events.shape), "head", 0, 0
    )
    w = w_uvqk.reshape(w_uvqk.shape[0], 4 * width)
    branches = project(gathered, norm_gain[None, :], w)
    partial_terms = attend(
        lengths, swap_offset, branches, cache_keys, cache_values, even, odd, w_out
    )
    terms = lax.all_to_all(partial_terms, "head", 0, 0)
    summed = jnp.sum(terms.astype(jnp.float32), axis=0)
    return (events.astype(jnp.float32) + summed).astype(jnp.bfloat16)


def solution(mesh):
    return jax.shard_map(
        on_device,
        mesh=mesh,
        in_specs=(
            P("user", "head"),
            P(),
            P(None, None, "head"),
            P("head", None),
            P("user", None, "head"),
            P("user", None, "head"),
            P("user"),
            P("user"),
        ),
        out_specs=P("user", "head"),
        check_vma=False,
    )
```

```python
import functools

import jax
import jax.numpy as jnp
from jax import lax
from jax.experimental import pallas as pl
from jax.experimental.pallas import tpu as pltpu
from jax.sharding import PartitionSpec as P

HEAD = 64
BLOCK = 128
NT = (((1,), (1,)), ((), ()))
NN = (((1,), (0,)), ((), ()))
VMEM = pl.BlockSpec(memory_space=pltpu.VMEM)
SMEM = pl.BlockSpec(memory_space=pltpu.SMEM)
HBM = pl.BlockSpec(memory_space=pltpu.HBM)
ANY = pl.BlockSpec(memory_space=pl.ANY)


def gather_pack_kernel(side, lengths, events, keys, values, pay_ref, all_ref, sems):
    half_slots = keys.shape[0] // 2
    parts = all_ref.shape[0]
    value_copies, others = [], []
    for s in range(half_slots):
        j = 2 * s + side
        value_copies.append(
            pltpu.make_async_copy(values.at[j], pay_ref.at[half_slots + s], sems.at[s])
        )
        others.append(pltpu.make_async_copy(keys.at[j], pay_ref.at[s], sems.at[half_slots + s]))
    for p in range(parts):
        others.append(
            pltpu.make_async_copy(events, all_ref.at[p], sems.at[2 * half_slots + p])
        )
    for c in value_copies + others:
        c.start()
    clear_dead(side, lengths, value_copies, pay_ref)
    for c in others:
        c.wait()


def pack_kernel(side, lengths, keys, values, pay_ref, sems):
    half_slots = keys.shape[0] // 2
    value_copies, others = [], []
    for s in range(half_slots):
        j = 2 * s + side
        value_copies.append(
            pltpu.make_async_copy(values.at[j], pay_ref.at[half_slots + s], sems.at[s])
        )
        others.append(pltpu.make_async_copy(keys.at[j], pay_ref.at[s], sems.at[half_slots + s]))
    for c in value_copies + others:
        c.start()
    clear_dead(side, lengths, value_copies, pay_ref)
    for c in others:
        c.wait()


def clear_dead(side, lengths, value_copies, pay_ref):
    half_slots, cap, width = pay_ref.shape[0] // 2, pay_ref.shape[1], pay_ref.shape[2]
    for s in range(half_slots):
        value_copies[s].wait()
        for block in range(1, cap // BLOCK):

            @pl.when(lengths[2 * s + side] <= block)
            def _():
                pay_ref[half_slots + s, block * BLOCK : (block + 1) * BLOCK, :] = jnp.zeros(
                    (BLOCK, width), pay_ref.dtype
                )


def gather_pack(side, parts, lengths, events, keys, values):
    slots, cap, width = keys.shape
    return pl.pallas_call(
        functools.partial(gather_pack_kernel, side),
        out_shape=(
            jax.ShapeDtypeStruct((slots, cap, width), keys.dtype),
            jax.ShapeDtypeStruct((parts,) + events.shape, events.dtype),
        ),
        in_specs=[SMEM, HBM, HBM, HBM],
        out_specs=(VMEM, VMEM),
        scratch_shapes=[pltpu.SemaphoreType.DMA((slots + parts,))],
        compiler_params=pltpu.CompilerParams(vmem_limit_bytes=6 * 2**20),
        cost_estimate=pl.CostEstimate(
            flops=0, bytes_accessed=4 * slots * cap * width, transcendentals=0
        ),
    )(lengths, events, keys, values)


def pack(side, lengths, keys, values):
    slots, cap, width = keys.shape
    return pl.pallas_call(
        functools.partial(pack_kernel, side),
        out_shape=jax.ShapeDtypeStruct((slots, cap, width), keys.dtype),
        in_specs=[SMEM, HBM, HBM],
        out_specs=VMEM,
        scratch_shapes=[pltpu.SemaphoreType.DMA((slots,))],
        compiler_params=pltpu.CompilerParams(vmem_limit_bytes=6 * 2**20),
    )(lengths, keys, values)


def cache_copies(side, offsets, keys, values, moved, kv, sems):
    half_slots = kv.shape[0] // 2
    waits = []
    for s in range(half_slots):
        j = 2 * s + side
        own = (
            pltpu.make_async_copy(keys.at[j], kv.at[s], sems.at[s]),
            pltpu.make_async_copy(values.at[j], kv.at[half_slots + s], sems.at[half_slots + s]),
        )
        traded = (
            pltpu.make_async_copy(moved.at[s], kv.at[s], sems.at[s]),
            pltpu.make_async_copy(
                moved.at[half_slots + s], kv.at[half_slots + s], sems.at[half_slots + s]
            ),
        )

        @pl.when(offsets[j] == 0)
        def _():
            for c in own:
                c.start()

        @pl.when(offsets[j] != 0)
        def _():
            for c in traded:
                c.start()

        waits.append(own)
    return waits


def attend_slots(side, lengths, offsets, b_ref, kv, waits, gated):
    half_slots, cap, width = kv.shape[0] // 2, kv.shape[1], kv.shape[2]
    new = b_ref.shape[0] // half_slots
    heads = width // HEAD
    lane_head = lax.broadcasted_iota(jnp.int32, (new, width), 1) // HEAD
    position = lax.broadcasted_iota(jnp.int32, (1, cap), 1)
    row = lax.broadcasted_iota(jnp.int32, (heads * new, new), 0) % new
    causal = row >= lax.broadcasted_iota(jnp.int32, (heads * new, new), 1)
    pair_lane = lax.broadcasted_iota(jnp.int32, (new, 2 * HEAD), 1) // HEAD

    def weigh(s):
        j = 2 * s + side
        at = slice(s * new, (s + 1) * new)
        queries = b_ref[at, 2 * width : 3 * width] * jnp.bfloat16(0.5 * HEAD**-0.5)
        fresh_keys = b_ref[at, 3 * width :]
        zero = jnp.zeros_like(queries)
        spread_q = jnp.concatenate(
            [jnp.where(lane_head == h, queries, zero) for h in range(heads)], axis=0
        )
        used = jnp.where(offsets[j] == 0, lengths[j] * BLOCK, cap)
        half = lax.dot_general(spread_q, kv[s], NT, preferred_element_type=jnp.float32)
        cached = jnp.where(position < used, half + half * jnp.tanh(half), 0.0)
        half = lax.dot_general(spread_q, fresh_keys, NT, preferred_element_type=jnp.float32)
        fresh = jnp.where(causal, half + half * jnp.tanh(half), 0.0)
        return cached.astype(jnp.bfloat16), fresh.astype(jnp.bfloat16)

    def finish(s, cached, fresh):
        at = slice(s * new, (s + 1) * new)
        gate = b_ref[at, :width].astype(jnp.float32)
        fresh_values = b_ref[at, width : 2 * width]
        total = lax.dot_general(
            cached, kv[half_slots + s], NN, preferred_element_type=jnp.float32
        )
        total = total + lax.dot_general(
            fresh, fresh_values, NN, preferred_element_type=jnp.float32
        )
        for pair in range(heads // 2):
            lanes = slice(2 * HEAD * pair, 2 * HEAD * (pair + 1))
            result = jnp.zeros((new, 2 * HEAD), jnp.float32)
            for within in range(2):
                h = 2 * pair + within
                mine = pair_lane == within
                x = jnp.where(mine, total[h * new : (h + 1) * new, lanes], 0.0)
                average = jnp.sum(x, axis=-1, keepdims=True) * (1.0 / HEAD)
                centred = jnp.where(mine, x - average, 0.0)
                spread = jnp.sum(centred * centred, axis=-1, keepdims=True) * (1.0 / HEAD)
                result = result + centred * lax.rsqrt(spread + 1e-05)
            gated[at, lanes] = (result * gate[:, lanes]).astype(jnp.bfloat16)

    for c in [pair[0] for pair in waits]:
        c.wait()
    weights = [weigh(s) for s in range(half_slots)]
    for c in [pair[1] for pair in waits]:
        c.wait()
    for s in range(half_slots):
        finish(s, *weights[s])


def project_out(gated, w_ref, out_ref, width):
    for p in range(out_ref.shape[0]):
        out_ref[p] = lax.dot_general(
            gated[...],
            w_ref[:, p * width : (p + 1) * width],
            NN,
            preferred_element_type=jnp.float32,
        ).astype(jnp.bfloat16)


def first_kernel(
    lengths, offsets, x_hbm, gain_ref, w_hbm, keys, values, moved, wo_hbm,
    out_ref, odd_hbm,
    x_ref, w_ref, wo_ref, kv, even_ref, odd_ref, gated, x_sems, w_sems, kv_sems,
):
    parts, total, width = x_ref.shape
    slots = keys.shape[0]
    new = total // slots
    features = parts * width
    chunks = x_sems.shape[0]
    rows = total // chunks
    x_copies = []
    for i in range(chunks):
        at = pl.ds(i * rows, rows)
        x_copies.append(pltpu.make_async_copy(x_hbm.at[:, at, :], x_ref.at[:, at, :], x_sems.at[i]))
    w_copy = pltpu.make_async_copy(w_hbm, w_ref, w_sems.at[0])
    wo_copy = pltpu.make_async_copy(wo_hbm, wo_ref, w_sems.at[1])
    x_copies[0].start()
    w_copy.start()
    for c in x_copies[1:]:
        c.start()
    waits = cache_copies(0, offsets, keys, values, moved, kv, kv_sems)
    wo_copy.start()
    gain = gain_ref[...]

    def normalise(i):
        x = jnp.concatenate(
            [x_ref[p, i * rows : (i + 1) * rows, :] for p in range(parts)], axis=1
        ).astype(jnp.float32)
        average = jnp.sum(x, axis=-1, keepdims=True) * (1.0 / features)
        centred = x - average
        spread = jnp.sum(centred * centred, axis=-1, keepdims=True) * (1.0 / features)
        return (centred * lax.rsqrt(spread + 1e-05) * gain).astype(jnp.bfloat16)

    for i in range(chunks):
        x_copies[i].wait()
        normed = normalise(i)
        if i == 0:
            w_copy.wait()
        half = 0.5 * lax.dot_general(normed, w_ref[...], NN, preferred_element_type=jnp.float32)
        branch = (half + half * jnp.tanh(half)).astype(jnp.bfloat16)
        for k in range(rows // new):
            j = i * (rows // new) + k
            target = odd_ref if j % 2 else even_ref
            target[(j // 2) * new : (j // 2 + 1) * new, :] = branch[k * new : (k + 1) * new, :]

    odd_copy = pltpu.make_async_copy(odd_ref, odd_hbm, w_sems.at[2])
    odd_copy.start()
    attend_slots(0, lengths, offsets, even_ref, kv, waits, gated)
    wo_copy.wait()
    project_out(gated, wo_ref, out_ref, width)
    odd_copy.wait()


def second_kernel(
    lengths, offsets, b_hbm, keys, values, moved, wo_hbm, out_ref, b_ref, wo_ref, kv, gated, sems, kv_sems
):
    width = keys.shape[2]
    waits = cache_copies(1, offsets, keys, values, moved, kv, kv_sems)
    b_copy = pltpu.make_async_copy(b_hbm, b_ref, sems.at[0])
    wo_copy = pltpu.make_async_copy(wo_hbm, wo_ref, sems.at[1])
    b_copy.start()
    wo_copy.start()
    b_copy.wait()
    attend_slots(1, lengths, offsets, b_ref, kv, waits, gated)
    wo_copy.wait()
    project_out(gated, wo_ref, out_ref, width)


def attention_flops(rows, new, cap, width):
    return 4 * rows * width * (cap + new) * (width // HEAD)


def first(lengths, offsets, x4, gain, w, keys, values, moved, w_out):
    slots, cap, width = keys.shape
    parts, total, _ = x4.shape
    half, new, wide = total // 2, total // slots, w.shape[1]
    bf16 = jnp.bfloat16
    return pl.pallas_call(
        first_kernel,
        out_shape=(
            jax.ShapeDtypeStruct((parts, half, width), bf16),
            jax.ShapeDtypeStruct((half, wide), bf16),
        ),
        in_specs=[SMEM, SMEM, ANY, VMEM, HBM, HBM, HBM, HBM, HBM],
        out_specs=(VMEM, HBM),
        scratch_shapes=[
            pltpu.VMEM(x4.shape, bf16),
            pltpu.VMEM(w.shape, bf16),
            pltpu.VMEM(w_out.shape, bf16),
            pltpu.VMEM((slots, cap, width), bf16),
            pltpu.VMEM((half, wide), bf16),
            pltpu.VMEM((half, wide), bf16),
            pltpu.VMEM((half, width), bf16),
            pltpu.SemaphoreType.DMA((4,)),
            pltpu.SemaphoreType.DMA((3,)),
            pltpu.SemaphoreType.DMA((slots,)),
        ],
        compiler_params=pltpu.CompilerParams(vmem_limit_bytes=40 * 2**20),
        cost_estimate=pl.CostEstimate(
            flops=2 * total * w.size + attention_flops(half, new, cap, width),
            bytes_accessed=2 * (w.size + x4.size) + 4 * slots * cap * width,
            transcendentals=total * wide,
        ),
    )(lengths, offsets, x4, gain, in_hbm(w), in_hbm(keys), in_hbm(values), in_hbm(moved), in_hbm(w_out))


def second(lengths, offsets, branches, keys, values, moved, w_out):
    slots, cap, width = keys.shape
    half, wide = branches.shape
    parts = w_out.shape[1] // width
    bf16 = jnp.bfloat16
    return pl.pallas_call(
        second_kernel,
        out_shape=jax.ShapeDtypeStruct((parts, half, width), bf16),
        in_specs=[SMEM, SMEM, ANY, HBM, HBM, HBM, HBM],
        out_specs=VMEM,
        scratch_shapes=[
            pltpu.VMEM(branches.shape, bf16),
            pltpu.VMEM(w_out.shape, bf16),
            pltpu.VMEM((slots, cap, width), bf16),
            pltpu.VMEM((half, width), bf16),
            pltpu.SemaphoreType.DMA((2,)),
            pltpu.SemaphoreType.DMA((slots,)),
        ],
        compiler_params=pltpu.CompilerParams(vmem_limit_bytes=40 * 2**20),
        cost_estimate=pl.CostEstimate(
            flops=attention_flops(half, 2 * half // slots, cap, width),
            bytes_accessed=4 * slots * cap * width + 2 * branches.size,
            transcendentals=half * (width // HEAD) * cap,
        ),
    )(lengths, offsets, branches, in_hbm(keys), in_hbm(values), in_hbm(moved), in_hbm(w_out))


def combine_kernel(events, even, odd, out_ref):
    parts, new, _ = even.shape
    for side, terms in enumerate((even, odd)):
        at = slice(side * new, (side + 1) * new)
        total = terms[0].astype(jnp.float32)
        for p in range(1, parts):
            total = total + terms[p].astype(jnp.float32)
        out_ref[at, :] = (events[at, :].astype(jnp.float32) + total).astype(out_ref.dtype)


def combine(slots, events, even, odd):
    rows, width = events.shape
    parts, new = even.shape[0], rows // slots
    terms = pl.BlockSpec((parts, new, width), lambda i: (0, i, 0))
    own = pl.BlockSpec((2 * new, width), lambda i: (i, 0))
    return pl.pallas_call(
        combine_kernel,
        grid=(slots // 2,),
        out_shape=jax.ShapeDtypeStruct(events.shape, events.dtype),
        in_specs=[own, terms, terms],
        out_specs=own,
        compiler_params=pltpu.CompilerParams(vmem_limit_bytes=40 * 2**20),
    )(in_hbm(events), in_hbm(even), in_hbm(odd))


def in_hbm(array):
    return pltpu.with_memory_space_constraint(array, pltpu.HBM)


def on_device(events, norm_gain, w_uvqk, w_out, cache_keys, cache_values, lengths, swap_offset):
    slots, cap, width = cache_keys.shape
    users = lax.axis_size("user")
    heads = lax.axis_size("head")

    odd_pay, spread_events = gather_pack(
        1, heads, lengths, in_hbm(events), in_hbm(cache_keys), in_hbm(cache_values)
    )
    odd = lax.ppermute(
        odd_pay, "user", [(i, (((i + 1) ^ 1) - 1) % users) for i in range(users)]
    )
    gathered = lax.all_to_all(spread_events, "head", 0, 0)
    w = w_uvqk.reshape(w_uvqk.shape[0], 4 * width)
    later_lengths, _ = lax.optimization_barrier((lengths, spread_events))
    even_pay = pack(0, later_lengths, in_hbm(cache_keys), in_hbm(cache_values))
    even = lax.ppermute(even_pay, "user", [(i, i ^ 1) for i in range(users)])

    even_part, odd_branches = first(
        lengths, swap_offset, gathered, norm_gain[None, :], w, cache_keys, cache_values, even, w_out
    )
    even_terms = lax.all_to_all(even_part, "head", 0, 0)
    odd_part = second(
        lengths, swap_offset, odd_branches, cache_keys, cache_values, odd, w_out
    )
    odd_part, even_terms = lax.optimization_barrier((odd_part, even_terms))
    odd_terms = lax.all_to_all(odd_part, "head", 0, 0)
    return combine(slots, events, even_terms, odd_terms)


def solution(mesh):
    return jax.shard_map(
        on_device,
        mesh=mesh,
        in_specs=(
            P("user", "head"),
            P(),
            P(None, None, "head"),
            P("head", None),
            P("user", None, "head"),
            P("user", None, "head"),
            P("user"),
            P("user"),
        ),
        out_specs=P("user", "head"),
        check_vma=False,
    )
```

```python
import functools

import jax
import jax.numpy as jnp
from jax import lax
from jax.experimental import pallas as pl
from jax.experimental.pallas import tpu as pltpu
from jax.sharding import PartitionSpec as P

HEAD = 64
BLOCK = 128
NT = (((1,), (1,)), ((), ()))
NN = (((1,), (0,)), ((), ()))
VMEM = pl.BlockSpec(memory_space=pltpu.VMEM)
SMEM = pl.BlockSpec(memory_space=pltpu.SMEM)
HBM = pl.BlockSpec(memory_space=pltpu.HBM)
ANY = pl.BlockSpec(memory_space=pl.ANY)


def pack_kernel(side, lengths, keys, values, *rest):
    *pays, buf, in_sems, out_sems = rest
    half_slots, cap, width = keys.shape[0] // 2, keys.shape[1], keys.shape[2]
    places = [pay.at[s] for pay in pays for s in range(pay.shape[0])]
    arrive, leave = [], []
    for s in range(half_slots):
        j = 2 * s + side
        for array, slot in ((values, half_slots + s), (keys, s)):
            arrive.append(pltpu.make_async_copy(array.at[j], buf.at[slot], in_sems.at[slot]))
            leave.append(pltpu.make_async_copy(buf.at[slot], places[slot], out_sems.at[slot]))
    for c in arrive:
        c.start()
    for i, c in enumerate(arrive):
        c.wait()
        if i % 2 == 0:
            s = i // 2
            for block in range(1, cap // BLOCK):

                @pl.when(lengths[2 * s + side] <= block)
                def _():
                    buf[half_slots + s, block * BLOCK : (block + 1) * BLOCK, :] = jnp.zeros(
                        (BLOCK, width), buf.dtype
                    )

        leave[i].start()
    for c in leave:
        c.wait()


def pack(side, pieces, lengths, keys, values):
    slots, cap, width = keys.shape
    return pl.pallas_call(
        functools.partial(pack_kernel, side),
        out_shape=[jax.ShapeDtypeStruct((slots // pieces, cap, width), keys.dtype)] * pieces,
        in_specs=[SMEM, HBM, HBM],
        out_specs=[HBM] * pieces,
        scratch_shapes=[
            pltpu.VMEM((slots, cap, width), keys.dtype),
            pltpu.SemaphoreType.DMA((slots,)),
            pltpu.SemaphoreType.DMA((slots,)),
        ],
        compiler_params=pltpu.CompilerParams(vmem_limit_bytes=6 * 2**20),
        cost_estimate=pl.CostEstimate(
            flops=0, bytes_accessed=4 * 10**6 if side else 15 * 10**6, transcendentals=0
        ),
    )(lengths, in_hbm(keys), in_hbm(values))


def project_kernel(x_any, gain_ref, w_any, b_ref, x_ref, w_ref, x_sems, w_sem):
    parts, total, width = x_ref.shape
    features = parts * width
    chunks = x_sems.shape[0]
    rows = total // chunks
    x_copies = []
    for i in range(chunks):
        at = pl.ds(i * rows, rows)
        x_copies.append(
            pltpu.make_async_copy(x_any.at[:, at, :], x_ref.at[:, at, :], x_sems.at[i])
        )
    w_copy = pltpu.make_async_copy(w_any, w_ref, w_sem.at[0])
    x_copies[0].start()
    w_copy.start()
    for c in x_copies[1:]:
        c.start()
    gain = gain_ref[...]

    def normalise(i):
        x = jnp.concatenate(
            [x_ref[p, i * rows : (i + 1) * rows, :] for p in range(parts)], axis=1
        ).astype(jnp.float32)
        average = jnp.sum(x, axis=-1, keepdims=True) * (1.0 / features)
        centred = x - average
        spread = jnp.sum(centred * centred, axis=-1, keepdims=True) * (1.0 / features)
        return (centred * lax.rsqrt(spread + 1e-05) * gain).astype(jnp.bfloat16)

    for i in range(chunks):
        x_copies[i].wait()
        normed = normalise(i)
        if i == 0:
            w_copy.wait()
        half = 0.5 * lax.dot_general(normed, w_ref[...], NN, preferred_element_type=jnp.float32)
        b_ref[i * rows : (i + 1) * rows, :] = (half + half * jnp.tanh(half)).astype(jnp.bfloat16)


def project(x4, gain, w):
    parts, total, width = x4.shape
    return pl.pallas_call(
        project_kernel,
        out_shape=jax.ShapeDtypeStruct((total, w.shape[1]), jnp.bfloat16),
        in_specs=[ANY, VMEM, ANY],
        out_specs=VMEM,
        scratch_shapes=[
            pltpu.VMEM(x4.shape, jnp.bfloat16),
            pltpu.VMEM(w.shape, jnp.bfloat16),
            pltpu.SemaphoreType.DMA((2,)),
            pltpu.SemaphoreType.DMA((1,)),
        ],
        compiler_params=pltpu.CompilerParams(vmem_limit_bytes=16 * 2**20),
        cost_estimate=pl.CostEstimate(
            flops=9 * 10**9,
            bytes_accessed=2 * (w.size + 2 * x4.size),
            transcendentals=total * w.shape[1],
        ),
    )(x4, gain, w)


def cache_copies(side, offsets, keys, values, moved_keys, moved_values, kv, sems):
    half_slots = kv.shape[0] // 2
    waits = []
    for s in range(half_slots):
        j = 2 * s + side
        own = (
            pltpu.make_async_copy(keys.at[j], kv.at[s], sems.at[s]),
            pltpu.make_async_copy(values.at[j], kv.at[half_slots + s], sems.at[half_slots + s]),
        )
        traded = (
            pltpu.make_async_copy(moved_keys.at[s], kv.at[s], sems.at[s]),
            pltpu.make_async_copy(
                moved_values.at[s], kv.at[half_slots + s], sems.at[half_slots + s]
            ),
        )

        @pl.when(offsets[j] == 0)
        def _():
            for c in own:
                c.start()

        @pl.when(offsets[j] != 0)
        def _():
            for c in traded:
                c.start()

        waits.append(own)
    return waits


def attend_slots(side, lengths, offsets, b_ref, kv, waits, gated):
    half_slots, cap, width = kv.shape[0] // 2, kv.shape[1], kv.shape[2]
    new = b_ref.shape[0] // (2 * half_slots)
    heads = width // HEAD
    lane_head = lax.broadcasted_iota(jnp.int32, (new, width), 1) // HEAD
    position = lax.broadcasted_iota(jnp.int32, (1, cap), 1)
    row = lax.broadcasted_iota(jnp.int32, (heads * new, new), 0) % new
    causal = row >= lax.broadcasted_iota(jnp.int32, (heads * new, new), 1)
    pair_lane = lax.broadcasted_iota(jnp.int32, (new, 2 * HEAD), 1) // HEAD

    def weigh(s):
        j = 2 * s + side
        at = slice(j * new, (j + 1) * new)
        queries = b_ref[at, 2 * width : 3 * width] * jnp.bfloat16(0.5 * HEAD**-0.5)
        fresh_keys = b_ref[at, 3 * width :]
        zero = jnp.zeros_like(queries)
        spread_q = jnp.concatenate(
            [jnp.where(lane_head == h, queries, zero) for h in range(heads)], axis=0
        )
        used = jnp.where(offsets[j] == 0, lengths[j] * BLOCK, cap)
        half = lax.dot_general(spread_q, kv[s], NT, preferred_element_type=jnp.float32)
        cached = jnp.where(position < used, half + half * jnp.tanh(half), 0.0)
        half = lax.dot_general(spread_q, fresh_keys, NT, preferred_element_type=jnp.float32)
        fresh = jnp.where(causal, half + half * jnp.tanh(half), 0.0)
        return cached.astype(jnp.bfloat16), fresh.astype(jnp.bfloat16)

    def finish(s, cached, fresh):
        j = 2 * s + side
        at = slice(j * new, (j + 1) * new)
        to = slice(s * new, (s + 1) * new)
        gate = b_ref[at, :width].astype(jnp.float32)
        fresh_values = b_ref[at, width : 2 * width]
        total = lax.dot_general(
            cached, kv[half_slots + s], NN, preferred_element_type=jnp.float32
        )
        total = total + lax.dot_general(
            fresh, fresh_values, NN, preferred_element_type=jnp.float32
        )
        for pair in range(heads // 2):
            lanes = slice(2 * HEAD * pair, 2 * HEAD * (pair + 1))
            result = jnp.zeros((new, 2 * HEAD), jnp.float32)
            for within in range(2):
                h = 2 * pair + within
                mine = pair_lane == within
                x = jnp.where(mine, total[h * new : (h + 1) * new, lanes], 0.0)
                average = jnp.sum(x, axis=-1, keepdims=True) * (1.0 / HEAD)
                centred = jnp.where(mine, x - average, 0.0)
                spread = jnp.sum(centred * centred, axis=-1, keepdims=True) * (1.0 / HEAD)
                result = result + centred * lax.rsqrt(spread + 1e-05)
            gated[to, lanes] = (result * gate[:, lanes]).astype(jnp.bfloat16)

    for c in [pair[0] for pair in waits]:
        c.wait()
    weights = [weigh(s) for s in range(half_slots)]
    for c in [pair[1] for pair in waits]:
        c.wait()
    for s in range(half_slots):
        finish(s, *weights[s])


def even_kernel(
    lengths, offsets, b_ref, keys, values, moved_keys, moved_values, gated, kv, kv_sems
):
    waits = cache_copies(0, offsets, keys, values, moved_keys, moved_values, kv, kv_sems)
    attend_slots(0, lengths, offsets, b_ref, kv, waits, gated)


def odd_kernel(
    lengths, offsets, b_ref, keys, values, moved, even_ref, w_any, out_ref, kv, gated, w_ref, kv_sems, w_sem
):
    parts, _, width = out_ref.shape
    half_slots = kv.shape[0] // 2
    moved_keys, moved_values = moved.at[:half_slots], moved.at[half_slots:]
    waits = cache_copies(1, offsets, keys, values, moved_keys, moved_values, kv, kv_sems)
    w_copy = pltpu.make_async_copy(w_any, w_ref, w_sem.at[0])
    w_copy.start()
    attend_slots(1, lengths, offsets, b_ref, kv, waits, gated)
    w_copy.wait()
    new = gated.shape[0] // half_slots
    for p in range(parts):
        for side, ref in enumerate((even_ref, gated)):
            block = lax.dot_general(
                ref[...],
                w_ref[:, p * width : (p + 1) * width],
                NN,
                preferred_element_type=jnp.float32,
            ).astype(jnp.bfloat16)
            for s in range(half_slots):
                j = 2 * s + side
                out_ref[p, j * new : (j + 1) * new, :] = block[s * new : (s + 1) * new, :]


def attention_cost(rows, slots, cap, width):
    return pl.CostEstimate(
        flops=4 * rows * width * (cap + rows // slots) * (width // HEAD),
        bytes_accessed=4 * slots * cap * width,
        transcendentals=rows * (width // HEAD) * cap,
    )


def attend_even(lengths, offsets, branches, keys, values, moved_keys, moved_values):
    slots, cap, width = keys.shape
    rows = branches.shape[0] // 2
    return pl.pallas_call(
        even_kernel,
        out_shape=jax.ShapeDtypeStruct((rows, width), jnp.bfloat16),
        in_specs=[SMEM, SMEM, VMEM, HBM, HBM, HBM, HBM],
        out_specs=VMEM,
        scratch_shapes=[
            pltpu.VMEM((slots, cap, width), jnp.bfloat16),
            pltpu.SemaphoreType.DMA((slots,)),
        ],
        compiler_params=pltpu.CompilerParams(vmem_limit_bytes=16 * 2**20),
        cost_estimate=pl.CostEstimate(flops=10**8, bytes_accessed=0, transcendentals=0),
    )(lengths, offsets, branches, in_hbm(keys), in_hbm(values), in_hbm(moved_keys), in_hbm(moved_values))


def attend_odd(lengths, offsets, branches, keys, values, moved, even_gated, w_out):
    slots, cap, width = keys.shape
    rows = branches.shape[0]
    parts = w_out.shape[1] // width
    return pl.pallas_call(
        odd_kernel,
        out_shape=jax.ShapeDtypeStruct((parts, rows, width), jnp.bfloat16),
        in_specs=[SMEM, SMEM, VMEM, HBM, HBM, HBM, VMEM, HBM],
        out_specs=VMEM,
        scratch_shapes=[
            pltpu.VMEM((slots, cap, width), jnp.bfloat16),
            pltpu.VMEM((rows // 2, width), jnp.bfloat16),
            pltpu.VMEM(w_out.shape, jnp.bfloat16),
            pltpu.SemaphoreType.DMA((slots,)),
            pltpu.SemaphoreType.DMA((1,)),
        ],
        compiler_params=pltpu.CompilerParams(vmem_limit_bytes=20 * 2**20),
        cost_estimate=attention_cost(rows // 2, slots // 2, cap, width),
    )(lengths, offsets, branches, in_hbm(keys), in_hbm(values), in_hbm(moved), even_gated, in_hbm(w_out))


def in_hbm(array):
    return pltpu.with_memory_space_constraint(array, pltpu.HBM)


def on_device(events, norm_gain, w_uvqk, w_out, cache_keys, cache_values, lengths, swap_offset):
    slots, cap, width = cache_keys.shape
    users = lax.axis_size("user")
    heads = lax.axis_size("head")

    (odd_pay,) = pack(1, 1, lengths, cache_keys, cache_values)
    odd = lax.ppermute(
        odd_pay, "user", [(i, (((i + 1) ^ 1) - 1) % users) for i in range(users)]
    )
    later_lengths, _ = lax.optimization_barrier((lengths, odd_pay))
    spread = jnp.broadcast_to(events[None], (heads,) + events.shape)
    gathered = lax.all_to_all(spread, "head", 0, 0)
    even = [
        lax.ppermute(pay, "user", [(i, i ^ 1) for i in range(users)])
        for pay in pack(0, 2, later_lengths, cache_keys, cache_values)
    ]

    w = w_uvqk.reshape(w_uvqk.shape[0], 4 * width)
    branches = project(gathered, norm_gain[None, :], w)
    caches = (cache_keys, cache_values)
    even_gated = attend_even(lengths, swap_offset, branches, *caches, *even)
    part = attend_odd(lengths, swap_offset, branches, *caches, odd, even_gated, w_out)
    terms = lax.all_to_all(part, "head", 0, 0)
    summed = jnp.sum(terms.astype(jnp.float32), axis=0)
    return (events.astype(jnp.float32) + summed).astype(jnp.bfloat16)


def solution(mesh):
    return jax.shard_map(
        on_device,
        mesh=mesh,
        in_specs=(
            P("user", "head"),
            P(),
            P(None, None, "head"),
            P("head", None),
            P("user", None, "head"),
            P("user", None, "head"),
            P("user"),
            P("user"),
        ),
        out_specs=P("user", "head"),
        check_vma=False,
    )
```

```python
import functools

import jax
import jax.numpy as jnp
from jax import lax
from jax.experimental import pallas as pl
from jax.experimental.pallas import tpu as pltpu
from jax.sharding import PartitionSpec as P

HEAD = 64
BLOCK = 128
NEW = 64
NT = (((1,), (1,)), ((), ()))
NN = (((1,), (0,)), ((), ()))
VMEM = pl.BlockSpec(memory_space=pltpu.VMEM)
SMEM = pl.BlockSpec(memory_space=pltpu.SMEM)
HBM = pl.BlockSpec(memory_space=pltpu.HBM)
ANY = pl.BlockSpec(memory_space=pl.ANY)


def pack_kernel(side, lengths_hbm, keys, values, *rest):
    *rest, buf, lengths, in_sems, out_sems, sem = rest
    spread = None
    if side == 1:
        events, *pays, spread, events_ref, spread_sems = rest
    else:
        pays = rest
    half_slots, cap, width = keys.shape[0] // 2, keys.shape[1], keys.shape[2]
    places = [pay.at[s] for pay in pays for s in range(pay.shape[0])]
    lengths_copy = pltpu.make_async_copy(lengths_hbm, lengths, sem.at[0])
    lengths_copy.start()
    arrive, leave = [], []
    for s in range(half_slots):
        j = 2 * s + side
        for array, slot in ((values, half_slots + s), (keys, s)):
            arrive.append(pltpu.make_async_copy(array.at[j], buf.at[slot], in_sems.at[slot]))
            leave.append(pltpu.make_async_copy(buf.at[slot], places[slot], out_sems.at[slot]))
    for c in arrive:
        c.start()
    if spread is not None:
        events_copy = pltpu.make_async_copy(events, events_ref, sem.at[1])
        events_copy.start()
    lengths_copy.wait()
    for i, c in enumerate(arrive):
        c.wait()
        if i % 2 == 0:
            s = i // 2
            for block in range(1, cap // BLOCK):

                @pl.when(lengths[2 * s + side] <= block)
                def _():
                    buf[half_slots + s, block * BLOCK : (block + 1) * BLOCK, :] = jnp.zeros(
                        (BLOCK, width), buf.dtype
                    )

        leave[i].start()
    if spread is not None:
        events_copy.wait()
        for p in range(spread.shape[0]):
            copy = pltpu.make_async_copy(events_ref, spread.at[p], spread_sems.at[p])
            copy.start()
            leave.append(copy)
    for c in leave:
        c.wait()


def pack(side, pieces, lengths, keys, values, events=None, parts=0):
    slots, cap, width = keys.shape
    operands = [in_hbm(lengths), in_hbm(keys), in_hbm(values)]
    outs = [pltpu.HBM((slots // pieces, cap, width), keys.dtype)] * pieces
    scratch = []
    if events is not None:
        operands.append(in_hbm(events))
        outs.append(pltpu.HBM((parts,) + events.shape, events.dtype))
        scratch = [pltpu.VMEM(events.shape, events.dtype), pltpu.SemaphoreType.DMA((parts,))]
    return pl.pallas_call(
        functools.partial(pack_kernel, side),
        out_shape=outs,
        in_specs=[HBM] * len(operands),
        out_specs=[HBM] * len(outs),
        scratch_shapes=scratch
        + [
            pltpu.VMEM((slots, cap, width), keys.dtype),
            pltpu.SMEM(lengths.shape, lengths.dtype),
            pltpu.SemaphoreType.DMA((slots,)),
            pltpu.SemaphoreType.DMA((slots,)),
            pltpu.SemaphoreType.DMA((2,)),
        ],
        compiler_params=pltpu.CompilerParams(vmem_limit_bytes=6 * 2**20),
        cost_estimate=pl.CostEstimate(
            flops=0, bytes_accessed=4 * 10**6 if side else 15 * 10**6, transcendentals=0
        ),
    )(*operands)


def project_kernel(x_any, gain_ref, w_hbm, even_hbm, odd_hbm, x_ref, w_ref, b_ref, x_sems, w_sem, b_sems):
    parts, total, width = x_ref.shape
    features = parts * width
    chunks = x_sems.shape[0]
    rows = total // chunks
    x_copies = []
    for i in range(chunks):
        at = pl.ds(i * rows, rows)
        x_copies.append(
            pltpu.make_async_copy(x_any.at[:, at, :], x_ref.at[:, at, :], x_sems.at[i])
        )
    w_copy = pltpu.make_async_copy(w_hbm, w_ref, w_sem.at[0])
    x_copies[0].start()
    w_copy.start()
    for c in x_copies[1:]:
        c.start()
    gain = gain_ref[...]

    def normalise(i):
        x = jnp.concatenate(
            [x_ref[p, i * rows : (i + 1) * rows, :] for p in range(parts)], axis=1
        ).astype(jnp.float32)
        average = jnp.sum(x, axis=-1, keepdims=True) * (1.0 / features)
        centred = x - average
        spread = jnp.sum(centred * centred, axis=-1, keepdims=True) * (1.0 / features)
        return (centred * lax.rsqrt(spread + 1e-05) * gain).astype(jnp.bfloat16)

    leave = []
    for i in range(chunks):
        x_copies[i].wait()
        normed = normalise(i)
        if i == 0:
            w_copy.wait()
        half = 0.5 * lax.dot_general(normed, w_ref[...], NN, preferred_element_type=jnp.float32)
        branch = (half + half * jnp.tanh(half)).astype(jnp.bfloat16)
        held = rows // (2 * NEW)
        for k in range(2 * held):
            s = i * held + k // 2
            b_ref[k % 2, s * NEW : (s + 1) * NEW, :] = branch[k * NEW : (k + 1) * NEW, :]
        for side, target in enumerate((even_hbm, odd_hbm)):
            at = pl.ds(i * held * NEW, held * NEW)
            copy = pltpu.make_async_copy(
                b_ref.at[side, at], target.at[at], b_sems.at[2 * i + side]
            )
            copy.start()
            leave.append(copy)
    for c in leave:
        c.wait()


def project(x4, gain, w):
    parts, total, width = x4.shape
    chunks, wide = 2, w.shape[1]
    out = pltpu.HBM((total // 2, wide), jnp.bfloat16)
    return pl.pallas_call(
        project_kernel,
        out_shape=(out, out),
        in_specs=[ANY, VMEM, HBM],
        out_specs=(HBM, HBM),
        scratch_shapes=[
            pltpu.VMEM(x4.shape, jnp.bfloat16),
            pltpu.VMEM(w.shape, jnp.bfloat16),
            pltpu.VMEM((2, total // 2, wide), jnp.bfloat16),
            pltpu.SemaphoreType.DMA((chunks,)),
            pltpu.SemaphoreType.DMA((1,)),
            pltpu.SemaphoreType.DMA((2 * chunks,)),
        ],
        compiler_params=pltpu.CompilerParams(vmem_limit_bytes=20 * 2**20),
        cost_estimate=pl.CostEstimate(
            flops=9 * 10**9,
            bytes_accessed=2 * (w.size + 2 * x4.size),
            transcendentals=total * wide,
        ),
    )(x4, gain, in_hbm(w))


def cache_copies(side, offsets, keys, values, moved_keys, moved_values, kv, sems):
    half_slots = kv.shape[0] // 2
    waits = []
    for s in range(half_slots):
        j = 2 * s + side
        own = (
            pltpu.make_async_copy(keys.at[j], kv.at[s], sems.at[s]),
            pltpu.make_async_copy(values.at[j], kv.at[half_slots + s], sems.at[half_slots + s]),
        )
        traded = (
            pltpu.make_async_copy(moved_keys.at[s], kv.at[s], sems.at[s]),
            pltpu.make_async_copy(
                moved_values.at[s], kv.at[half_slots + s], sems.at[half_slots + s]
            ),
        )

        waits.append((j, own, traded))
    for kind in range(2):
        for j, own, traded in waits:

            @pl.when(offsets[j] == 0)
            def _():
                own[kind].start()

            @pl.when(offsets[j] != 0)
            def _():
                traded[kind].start()

    return [own for _, own, _ in waits]


def attend_slots(side, lengths, offsets, b_ref, kv, waits, gated):
    half_slots, cap, width = kv.shape[0] // 2, kv.shape[1], kv.shape[2]
    new = b_ref.shape[0] // half_slots
    heads = width // HEAD
    lane_head = lax.broadcasted_iota(jnp.int32, (new, width), 1) // HEAD
    position = lax.broadcasted_iota(jnp.int32, (1, cap), 1)
    row = lax.broadcasted_iota(jnp.int32, (heads * new, new), 0) % new
    causal = row >= lax.broadcasted_iota(jnp.int32, (heads * new, new), 1)
    pair_lane = lax.broadcasted_iota(jnp.int32, (new, 2 * HEAD), 1) // HEAD

    def weigh(s):
        j = 2 * s + side
        at = slice(s * new, (s + 1) * new)
        queries = b_ref[at, 2 * width : 3 * width] * jnp.bfloat16(0.5 * HEAD**-0.5)
        fresh_keys = b_ref[at, 3 * width :]
        zero = jnp.zeros_like(queries)
        spread_q = jnp.concatenate(
            [jnp.where(lane_head == h, queries, zero) for h in range(heads)], axis=0
        )
        used = jnp.where(offsets[j] == 0, lengths[j] * BLOCK, cap)
        half = lax.dot_general(spread_q, kv[s], NT, preferred_element_type=jnp.float32)
        cached = jnp.where(position < used, half + half * jnp.tanh(half), 0.0)
        half = lax.dot_general(spread_q, fresh_keys, NT, preferred_element_type=jnp.float32)
        fresh = jnp.where(causal, half + half * jnp.tanh(half), 0.0)
        return cached.astype(jnp.bfloat16), fresh.astype(jnp.bfloat16)

    def finish(s, cached, fresh):
        at = slice(s * new, (s + 1) * new)
        gate = b_ref[at, :width].astype(jnp.float32)
        fresh_values = b_ref[at, width : 2 * width]
        total = lax.dot_general(
            cached, kv[half_slots + s], NN, preferred_element_type=jnp.float32
        )
        total = total + lax.dot_general(
            fresh, fresh_values, NN, preferred_element_type=jnp.float32
        )
        for pair in range(heads // 2):
            lanes = slice(2 * HEAD * pair, 2 * HEAD * (pair + 1))
            result = jnp.zeros((new, 2 * HEAD), jnp.float32)
            for within in range(2):
                h = 2 * pair + within
                mine = pair_lane == within
                x = jnp.where(mine, total[h * new : (h + 1) * new, lanes], 0.0)
                average = jnp.sum(x, axis=-1, keepdims=True) * (1.0 / HEAD)
                centred = jnp.where(mine, x - average, 0.0)
                spread = jnp.sum(centred * centred, axis=-1, keepdims=True) * (1.0 / HEAD)
                result = result + centred * lax.rsqrt(spread + 1e-05)
            gated[at, lanes] = (result * gate[:, lanes]).astype(jnp.bfloat16)

    for c in [pair[0] for pair in waits]:
        c.wait()
    weights = [weigh(s) for s in range(half_slots)]
    for c in [pair[1] for pair in waits]:
        c.wait()
    for s in range(half_slots):
        finish(s, *weights[s])


def project_out(gated, w_ref, out_ref, width):
    for p in range(out_ref.shape[0]):
        out_ref[p] = lax.dot_general(
            gated[...],
            w_ref[:, p * width : (p + 1) * width],
            NN,
            preferred_element_type=jnp.float32,
        ).astype(jnp.bfloat16)


def serve_kernel(
    side, lengths, offsets, b_hbm, keys, values, w_hbm, moved_keys, *rest
):
    moved_values = None
    if side == 0:
        moved_values, *rest = rest
    out_ref, b_ref, w_ref, kv, gated, sems, kv_sems = rest
    half_slots, width = kv.shape[0] // 2, kv.shape[2]
    if side == 1:
        moved_keys, moved_values = moved_keys.at[:half_slots], moved_keys.at[half_slots:]
    b_copy = pltpu.make_async_copy(b_hbm, b_ref, sems.at[0])
    w_copy = pltpu.make_async_copy(w_hbm, w_ref, sems.at[1])
    b_copy.start()
    waits = cache_copies(side, offsets, keys, values, moved_keys, moved_values, kv, kv_sems)
    w_copy.start()
    b_copy.wait()
    attend_slots(side, lengths, offsets, b_ref, kv, waits, gated)
    w_copy.wait()
    project_out(gated, w_ref, out_ref, width)


def serve(side, lengths, offsets, branches, keys, values, w_out, moved):
    slots, cap, width = keys.shape
    parts, rows = w_out.shape[1] // width, branches.shape[0]
    bf16 = jnp.bfloat16
    operands = [in_hbm(a) for a in (branches, keys, values, w_out)]
    operands += [in_hbm(a) for a in moved] if side else moved
    return pl.pallas_call(
        functools.partial(serve_kernel, side),
        out_shape=jax.ShapeDtypeStruct((parts, rows, width), bf16),
        in_specs=[SMEM, SMEM] + [HBM] * 4 + [HBM if side else ANY] * len(moved),
        out_specs=VMEM,
        scratch_shapes=[
            pltpu.VMEM(branches.shape, bf16),
            pltpu.VMEM(w_out.shape, bf16),
            pltpu.VMEM((slots, cap, width), bf16),
            pltpu.VMEM((rows, width), bf16),
            pltpu.SemaphoreType.DMA((2,)),
            pltpu.SemaphoreType.DMA((slots,)),
        ],
        compiler_params=pltpu.CompilerParams(vmem_limit_bytes=20 * 2**20),
        cost_estimate=pl.CostEstimate(
            flops=3 * 10**9 if side else 10**8, bytes_accessed=0, transcendentals=0
        ),
    )(lengths, offsets, *operands)


def combine_kernel(events, even, odd, out_ref):
    parts, rows, _ = even.shape
    half_slots = out_ref.shape[0] // 2 // NEW
    for j in range(2 * half_slots):
        at = slice(j * NEW, (j + 1) * NEW)
        terms_at = slice((j // 2) * NEW, (j // 2 + 1) * NEW)
        terms = odd if j % 2 else even
        total = terms[0, terms_at, :].astype(jnp.float32)
        for p in range(1, parts):
            total = total + terms[p, terms_at, :].astype(jnp.float32)
        out_ref[at, :] = (events[at, :].astype(jnp.float32) + total).astype(out_ref.dtype)


def combine(events, even, odd):
    return pl.pallas_call(
        combine_kernel,
        out_shape=jax.ShapeDtypeStruct(events.shape, events.dtype),
        in_specs=[VMEM, VMEM, VMEM],
        out_specs=VMEM,
        compiler_params=pltpu.CompilerParams(vmem_limit_bytes=6 * 2**20),
    )(events, even, odd)


def in_hbm(array):
    return pltpu.with_memory_space_constraint(array, pltpu.HBM)


def on_device(events, norm_gain, w_uvqk, w_out, cache_keys, cache_values, lengths, swap_offset):
    slots, cap, width = cache_keys.shape
    users = lax.axis_size("user")
    heads = lax.axis_size("head")
    caches = (cache_keys, cache_values)

    def to_heads(blocks):
        return lax.all_to_all(blocks, "head", 0, 0)

    odd_pay, spread = pack(1, 1, lengths, *caches, events, heads)
    across = [(i, (((i + 1) ^ 1) - 1) % users) for i in range(users)]
    odd = [lax.ppermute(odd_pay, "user", across)]
    gathered = to_heads(spread)
    later_lengths, _ = lax.optimization_barrier((lengths, odd_pay))
    within = [(i, i ^ 1) for i in range(users)]
    even = [lax.ppermute(pay, "user", within) for pay in pack(0, 2, later_lengths, *caches)]

    w = w_uvqk.reshape(w_uvqk.shape[0], 4 * width)
    even_branches, odd_branches = project(gathered, norm_gain[None, :], w)
    even_part = serve(0, lengths, swap_offset, even_branches, *caches, w_out, even)
    even_terms = to_heads(even_part)
    later_branches, _ = lax.optimization_barrier((odd_branches, even_part))
    odd_part = serve(1, lengths, swap_offset, later_branches, *caches, w_out, odd)
    odd_part, even_terms = lax.optimization_barrier((odd_part, even_terms))
    odd_terms = to_heads(odd_part)
    return combine(events, even_terms, odd_terms)


def solution(mesh):
    return jax.shard_map(
        on_device,
        mesh=mesh,
        in_specs=(
            P("user", "head"),
            P(),
            P(None, None, "head"),
            P("head", None),
            P("user", None, "head"),
            P("user", None, "head"),
            P("user"),
            P("user"),
        ),
        out_specs=P("user", "head"),
        check_vma=False,
    )
```

```python
import functools

import jax
import jax.numpy as jnp
from jax import lax
from jax.experimental import pallas as pl
from jax.experimental.pallas import tpu as pltpu
from jax.sharding import PartitionSpec as P

HEAD = 64
BLOCK = 128
NEW = 64
NT = (((1,), (1,)), ((), ()))
NN = (((1,), (0,)), ((), ()))
VMEM = pl.BlockSpec(memory_space=pltpu.VMEM)
SMEM = pl.BlockSpec(memory_space=pltpu.SMEM)
HBM = pl.BlockSpec(memory_space=pltpu.HBM)
ANY = pl.BlockSpec(memory_space=pl.ANY)


def pack_kernel(side, lengths_hbm, keys, values, *rest):
    *rest, buf, lengths, in_sems, out_sems, sem = rest
    spread = None
    if side == 1:
        events, *pays, spread, events_ref, spread_sems = rest
    else:
        pays = rest
    half_slots, cap, width = keys.shape[0] // 2, keys.shape[1], keys.shape[2]
    places = [pay.at[s] for pay in pays for s in range(pay.shape[0])]
    lengths_copy = pltpu.make_async_copy(lengths_hbm, lengths, sem.at[0])
    lengths_copy.start()
    arrive, leave = [], []
    for s in range(half_slots):
        j = 2 * s + side
        for array, slot in ((values, half_slots + s), (keys, s)):
            arrive.append(pltpu.make_async_copy(array.at[j], buf.at[slot], in_sems.at[slot]))
            leave.append(pltpu.make_async_copy(buf.at[slot], places[slot], out_sems.at[slot]))
    for c in arrive:
        c.start()
    if spread is not None:
        events_copy = pltpu.make_async_copy(events, events_ref, sem.at[1])
        events_copy.start()
    lengths_copy.wait()
    for i, c in enumerate(arrive):
        c.wait()
        if i % 2 == 0:
            s = i // 2
            for block in range(1, cap // BLOCK):

                @pl.when(lengths[2 * s + side] <= block)
                def _():
                    buf[half_slots + s, block * BLOCK : (block + 1) * BLOCK, :] = jnp.zeros(
                        (BLOCK, width), buf.dtype
                    )

        leave[i].start()
    if spread is not None:
        events_copy.wait()
        for p in range(spread.shape[0]):
            copy = pltpu.make_async_copy(events_ref, spread.at[p], spread_sems.at[p])
            copy.start()
            leave.append(copy)
    for c in leave:
        c.wait()


def pack(side, pieces, lengths, keys, values, events=None, parts=0):
    slots, cap, width = keys.shape
    operands = [in_hbm(lengths), in_hbm(keys), in_hbm(values)]
    outs = [pltpu.HBM((slots // pieces, cap, width), keys.dtype)] * pieces
    scratch = []
    if events is not None:
        operands.append(in_hbm(events))
        outs.append(pltpu.HBM((parts,) + events.shape, events.dtype))
        scratch = [pltpu.VMEM(events.shape, events.dtype), pltpu.SemaphoreType.DMA((parts,))]
    return pl.pallas_call(
        functools.partial(pack_kernel, side),
        out_shape=outs,
        in_specs=[HBM] * len(operands),
        out_specs=[HBM] * len(outs),
        scratch_shapes=scratch
        + [
            pltpu.VMEM((slots, cap, width), keys.dtype),
            pltpu.SMEM(lengths.shape, lengths.dtype),
            pltpu.SemaphoreType.DMA((slots,)),
            pltpu.SemaphoreType.DMA((slots,)),
            pltpu.SemaphoreType.DMA((2,)),
        ],
        compiler_params=pltpu.CompilerParams(vmem_limit_bytes=6 * 2**20),
        cost_estimate=pl.CostEstimate(
            flops=0, bytes_accessed=4 * 10**6 if side else 15 * 10**6, transcendentals=0
        ),
    )(*operands)


def project_kernel(x_any, gain_ref, w_hbm, even_hbm, odd_hbm, x_ref, w_ref, b_ref, x_sems, w_sem, b_sems):
    parts, total, width = x_ref.shape
    features = parts * width
    chunks = x_sems.shape[0]
    rows = total // chunks
    x_copies = []
    for i in range(chunks):
        at = pl.ds(i * rows, rows)
        x_copies.append(
            pltpu.make_async_copy(x_any.at[:, at, :], x_ref.at[:, at, :], x_sems.at[i])
        )
    w_copy = pltpu.make_async_copy(w_hbm, w_ref, w_sem.at[0])
    x_copies[0].start()
    w_copy.start()
    for c in x_copies[1:]:
        c.start()
    gain = gain_ref[...]

    def normalise(i):
        x = jnp.concatenate(
            [x_ref[p, i * rows : (i + 1) * rows, :] for p in range(parts)], axis=1
        ).astype(jnp.float32)
        average = jnp.sum(x, axis=-1, keepdims=True) * (1.0 / features)
        centred = x - average
        spread = jnp.sum(centred * centred, axis=-1, keepdims=True) * (1.0 / features)
        return (centred * lax.rsqrt(spread + 1e-05) * gain).astype(jnp.bfloat16)

    leave = []
    for i in range(chunks):
        x_copies[i].wait()
        normed = normalise(i)
        if i == 0:
            w_copy.wait()
        half = 0.5 * lax.dot_general(normed, w_ref[...], NN, preferred_element_type=jnp.float32)
        branch = (half + half * jnp.tanh(half)).astype(jnp.bfloat16)
        held = rows // (2 * NEW)
        for k in range(2 * held):
            s = i * held + k // 2
            b_ref[k % 2, s * NEW : (s + 1) * NEW, :] = branch[k * NEW : (k + 1) * NEW, :]
        for side, target in enumerate((even_hbm, odd_hbm)):
            at = pl.ds(i * held * NEW, held * NEW)
            copy = pltpu.make_async_copy(
                b_ref.at[side, at], target.at[at], b_sems.at[2 * i + side]
            )
            copy.start()
            leave.append(copy)
    for c in leave:
        c.wait()


def project(x4, gain, w):
    parts, total, width = x4.shape
    chunks, wide = 2, w.shape[1]
    out = pltpu.HBM((total // 2, wide), jnp.bfloat16)
    return pl.pallas_call(
        project_kernel,
        out_shape=(out, out),
        in_specs=[ANY, VMEM, HBM],
        out_specs=(HBM, HBM),
        scratch_shapes=[
            pltpu.VMEM(x4.shape, jnp.bfloat16),
            pltpu.VMEM(w.shape, jnp.bfloat16),
            pltpu.VMEM((2, total // 2, wide), jnp.bfloat16),
            pltpu.SemaphoreType.DMA((chunks,)),
            pltpu.SemaphoreType.DMA((1,)),
            pltpu.SemaphoreType.DMA((2 * chunks,)),
        ],
        compiler_params=pltpu.CompilerParams(vmem_limit_bytes=20 * 2**20),
        cost_estimate=pl.CostEstimate(
            flops=40 * 10**9,
            bytes_accessed=2 * (w.size + 2 * x4.size),
            transcendentals=total * wide,
        ),
    )(x4, gain, in_hbm(w))


def cache_copies(side, offsets, keys, values, moved_keys, moved_values, kv, sems):
    half_slots = kv.shape[0] // 2
    waits = []
    for s in range(half_slots):
        j = 2 * s + side
        own = (
            pltpu.make_async_copy(keys.at[j], kv.at[s], sems.at[s]),
            pltpu.make_async_copy(values.at[j], kv.at[half_slots + s], sems.at[half_slots + s]),
        )
        traded = (
            pltpu.make_async_copy(moved_keys.at[s], kv.at[s], sems.at[s]),
            pltpu.make_async_copy(
                moved_values.at[s], kv.at[half_slots + s], sems.at[half_slots + s]
            ),
        )

        waits.append((j, own, traded))
    for kind in range(2):
        for j, own, traded in waits:

            @pl.when(offsets[j] == 0)
            def _():
                own[kind].start()

            @pl.when(offsets[j] != 0)
            def _():
                traded[kind].start()

    return [own for _, own, _ in waits]


def attend_slots(side, lengths, offsets, b_ref, kv, waits, gated):
    half_slots, cap, width = kv.shape[0] // 2, kv.shape[1], kv.shape[2]
    new = b_ref.shape[0] // half_slots
    heads = width // HEAD
    lane_head = lax.broadcasted_iota(jnp.int32, (new, width), 1) // HEAD
    position = lax.broadcasted_iota(jnp.int32, (1, cap), 1)
    row = lax.broadcasted_iota(jnp.int32, (heads * new, new), 0) % new
    causal = row >= lax.broadcasted_iota(jnp.int32, (heads * new, new), 1)
    pair_lane = lax.broadcasted_iota(jnp.int32, (new, 2 * HEAD), 1) // HEAD

    def weigh(s):
        j = 2 * s + side
        at = slice(s * new, (s + 1) * new)
        queries = b_ref[at, 2 * width : 3 * width] * jnp.bfloat16(0.5 * HEAD**-0.5)
        fresh_keys = b_ref[at, 3 * width :]
        zero = jnp.zeros_like(queries)
        spread_q = jnp.concatenate(
            [jnp.where(lane_head == h, queries, zero) for h in range(heads)], axis=0
        )
        used = jnp.where(offsets[j] == 0, lengths[j] * BLOCK, cap)
        half = lax.dot_general(spread_q, kv[s], NT, preferred_element_type=jnp.float32)
        cached = jnp.where(position < used, half + half * jnp.tanh(half), 0.0)
        half = lax.dot_general(spread_q, fresh_keys, NT, preferred_element_type=jnp.float32)
        fresh = jnp.where(causal, half + half * jnp.tanh(half), 0.0)
        return cached.astype(jnp.bfloat16), fresh.astype(jnp.bfloat16)

    def finish(s, cached, fresh):
        at = slice(s * new, (s + 1) * new)
        gate = b_ref[at, :width].astype(jnp.float32)
        fresh_values = b_ref[at, width : 2 * width]
        total = lax.dot_general(
            cached, kv[half_slots + s], NN, preferred_element_type=jnp.float32
        )
        total = total + lax.dot_general(
            fresh, fresh_values, NN, preferred_element_type=jnp.float32
        )
        for pair in range(heads // 2):
            lanes = slice(2 * HEAD * pair, 2 * HEAD * (pair + 1))
            result = jnp.zeros((new, 2 * HEAD), jnp.float32)
            for within in range(2):
                h = 2 * pair + within
                mine = pair_lane == within
                x = jnp.where(mine, total[h * new : (h + 1) * new, lanes], 0.0)
                average = jnp.sum(x, axis=-1, keepdims=True) * (1.0 / HEAD)
                centred = jnp.where(mine, x - average, 0.0)
                spread = jnp.sum(centred * centred, axis=-1, keepdims=True) * (1.0 / HEAD)
                result = result + centred * lax.rsqrt(spread + 1e-05)
            gated[at, lanes] = (result * gate[:, lanes]).astype(jnp.bfloat16)

    for c in [pair[0] for pair in waits]:
        c.wait()
    weights = [weigh(s) for s in range(half_slots)]
    for c in [pair[1] for pair in waits]:
        c.wait()
    for s in range(half_slots):
        finish(s, *weights[s])


def project_out(gated, w_ref, out_ref, width):
    for p in range(out_ref.shape[0]):
        out_ref[p] = lax.dot_general(
            gated[...],
            w_ref[:, p * width : (p + 1) * width],
            NN,
            preferred_element_type=jnp.float32,
        ).astype(jnp.bfloat16)


def serve_kernel(
    side, lengths, offsets, b_hbm, keys, values, w_hbm, moved_keys, *rest
):
    moved_values = None
    if side == 0:
        moved_values, *rest = rest
    out_ref, b_ref, w_ref, kv, gated, sems, kv_sems = rest
    half_slots, width = kv.shape[0] // 2, kv.shape[2]
    if side == 1:
        moved_keys, moved_values = moved_keys.at[:half_slots], moved_keys.at[half_slots:]
    b_copy = pltpu.make_async_copy(b_hbm, b_ref, sems.at[0])
    w_copy = pltpu.make_async_copy(w_hbm, w_ref, sems.at[1])
    b_copy.start()
    waits = cache_copies(side, offsets, keys, values, moved_keys, moved_values, kv, kv_sems)
    w_copy.start()
    b_copy.wait()
    attend_slots(side, lengths, offsets, b_ref, kv, waits, gated)
    w_copy.wait()
    project_out(gated, w_ref, out_ref, width)


def serve(side, lengths, offsets, branches, keys, values, w_out, moved):
    slots, cap, width = keys.shape
    parts, rows = w_out.shape[1] // width, branches.shape[0]
    bf16 = jnp.bfloat16
    operands = [in_hbm(a) for a in (branches, keys, values, w_out)]
    operands += [in_hbm(a) for a in moved] if side else moved
    return pl.pallas_call(
        functools.partial(serve_kernel, side),
        out_shape=jax.ShapeDtypeStruct((parts, rows, width), bf16),
        in_specs=[SMEM, SMEM] + [HBM] * 4 + [HBM if side else ANY] * len(moved),
        out_specs=VMEM,
        scratch_shapes=[
            pltpu.VMEM(branches.shape, bf16),
            pltpu.VMEM(w_out.shape, bf16),
            pltpu.VMEM((slots, cap, width), bf16),
            pltpu.VMEM((rows, width), bf16),
            pltpu.SemaphoreType.DMA((2,)),
            pltpu.SemaphoreType.DMA((slots,)),
        ],
        compiler_params=pltpu.CompilerParams(vmem_limit_bytes=20 * 2**20),
        cost_estimate=pl.CostEstimate(
            flops=3 * 10**9 if side else 10**8, bytes_accessed=0, transcendentals=0
        ),
    )(lengths, offsets, *operands)


def combine_kernel(events, even, odd, out_ref):
    parts, rows, _ = even.shape
    half_slots = out_ref.shape[0] // 2 // NEW
    for j in range(2 * half_slots):
        at = slice(j * NEW, (j + 1) * NEW)
        terms_at = slice((j // 2) * NEW, (j // 2 + 1) * NEW)
        terms = odd if j % 2 else even
        total = terms[0, terms_at, :].astype(jnp.float32)
        for p in range(1, parts):
            total = total + terms[p, terms_at, :].astype(jnp.float32)
        out_ref[at, :] = (events[at, :].astype(jnp.float32) + total).astype(out_ref.dtype)


def combine(events, even, odd):
    return pl.pallas_call(
        combine_kernel,
        out_shape=jax.ShapeDtypeStruct(events.shape, events.dtype),
        in_specs=[VMEM, VMEM, VMEM],
        out_specs=VMEM,
        compiler_params=pltpu.CompilerParams(vmem_limit_bytes=6 * 2**20),
    )(events, even, odd)


def in_hbm(array):
    return pltpu.with_memory_space_constraint(array, pltpu.HBM)


def on_device(events, norm_gain, w_uvqk, w_out, cache_keys, cache_values, lengths, swap_offset):
    slots, cap, width = cache_keys.shape
    users = lax.axis_size("user")
    heads = lax.axis_size("head")
    caches = (cache_keys, cache_values)

    def to_heads(blocks):
        return lax.all_to_all(blocks, "head", 0, 0)

    odd_pay, spread = pack(1, 1, lengths, *caches, events, heads)
    across = [(i, (((i + 1) ^ 1) - 1) % users) for i in range(users)]
    odd = [lax.ppermute(odd_pay, "user", across)]
    gathered = to_heads(spread)
    later_lengths, _ = lax.optimization_barrier((lengths, odd_pay))
    within = [(i, i ^ 1) for i in range(users)]
    even = [lax.ppermute(pay, "user", within) for pay in pack(0, 2, later_lengths, *caches)]

    w = w_uvqk.reshape(w_uvqk.shape[0], 4 * width)
    even_branches, odd_branches = project(gathered, norm_gain[None, :], w)
    even_part = serve(0, lengths, swap_offset, even_branches, *caches, w_out, even)
    even_terms = to_heads(even_part)
    later_branches, _ = lax.optimization_barrier((odd_branches, even_part))
    odd_part = serve(1, lengths, swap_offset, later_branches, *caches, w_out, odd)
    odd_part, even_terms = lax.optimization_barrier((odd_part, even_terms))
    odd_terms = to_heads(odd_part)
    return combine(events, even_terms, odd_terms)


def solution(mesh):
    return jax.shard_map(
        on_device,
        mesh=mesh,
        in_specs=(
            P("user", "head"),
            P(),
            P(None, None, "head"),
            P("head", None),
            P("user", None, "head"),
            P("user", None, "head"),
            P("user"),
            P("user"),
        ),
        out_specs=P("user", "head"),
        check_vma=False,
    )
```

```python
import functools

import jax
import jax.numpy as jnp
from jax import lax
from jax.experimental import pallas as pl
from jax.experimental.pallas import tpu as pltpu
from jax.sharding import PartitionSpec as P

HEAD = 64
BLOCK = 128
NEW = 64
NT = (((1,), (1,)), ((), ()))
NN = (((1,), (0,)), ((), ()))
VMEM = pl.BlockSpec(memory_space=pltpu.VMEM)
SMEM = pl.BlockSpec(memory_space=pltpu.SMEM)
HBM = pl.BlockSpec(memory_space=pltpu.HBM)
ANY = pl.BlockSpec(memory_space=pl.ANY)


def pack_kernel(side, lengths_hbm, keys, values, *rest):
    *rest, buf, lengths, in_sems, out_sems, sem = rest
    spread = None
    if side == 1:
        events, *pays, spread, events_ref, spread_sems = rest
    else:
        pays = rest
    half_slots, cap, width = keys.shape[0] // 2, keys.shape[1], keys.shape[2]
    places = [pay.at[s] for pay in pays for s in range(pay.shape[0])]
    lengths_copy = pltpu.make_async_copy(lengths_hbm, lengths, sem.at[0])
    lengths_copy.start()
    arrive, leave = [], []
    for s in range(half_slots):
        j = 2 * s + side
        for array, slot in ((values, half_slots + s), (keys, s)):
            arrive.append(pltpu.make_async_copy(array.at[j], buf.at[slot], in_sems.at[slot]))
            leave.append(pltpu.make_async_copy(buf.at[slot], places[slot], out_sems.at[slot]))
    for c in arrive:
        c.start()
    if spread is not None:
        events_copy = pltpu.make_async_copy(events, events_ref, sem.at[1])
        events_copy.start()
    lengths_copy.wait()
    for i, c in enumerate(arrive):
        c.wait()
        if i % 2 == 0:
            s = i // 2
            for block in range(1, cap // BLOCK):

                @pl.when(lengths[2 * s + side] <= block)
                def _():
                    buf[half_slots + s, block * BLOCK : (block + 1) * BLOCK, :] = jnp.zeros(
                        (BLOCK, width), buf.dtype
                    )

        leave[i].start()
    if spread is not None:
        events_copy.wait()
        for p in range(spread.shape[0]):
            copy = pltpu.make_async_copy(events_ref, spread.at[p], spread_sems.at[p])
            copy.start()
            leave.append(copy)
    for c in leave:
        c.wait()


def pack(side, pieces, lengths, keys, values, events=None, parts=0):
    slots, cap, width = keys.shape
    operands = [in_hbm(lengths), in_hbm(keys), in_hbm(values)]
    outs = [pltpu.HBM((slots // pieces, cap, width), keys.dtype)] * pieces
    scratch = []
    if events is not None:
        operands.append(in_hbm(events))
        outs.append(pltpu.HBM((parts,) + events.shape, events.dtype))
        scratch = [pltpu.VMEM(events.shape, events.dtype), pltpu.SemaphoreType.DMA((parts,))]
    return pl.pallas_call(
        functools.partial(pack_kernel, side),
        out_shape=outs,
        in_specs=[HBM] * len(operands),
        out_specs=[HBM] * len(outs),
        scratch_shapes=scratch
        + [
            pltpu.VMEM((slots, cap, width), keys.dtype),
            pltpu.SMEM(lengths.shape, lengths.dtype),
            pltpu.SemaphoreType.DMA((slots,)),
            pltpu.SemaphoreType.DMA((slots,)),
            pltpu.SemaphoreType.DMA((2,)),
        ],
        compiler_params=pltpu.CompilerParams(vmem_limit_bytes=6 * 2**20),
        cost_estimate=pl.CostEstimate(
            flops=0, bytes_accessed=4 * 10**6 if side else 15 * 10**6, transcendentals=0
        ),
    )(*operands)


def cache_copies(side, offsets, keys, values, moved_keys, moved_values, kv, sems):
    half_slots = kv.shape[0] // 2
    waits = []
    for s in range(half_slots):
        j = 2 * s + side
        own = (
            pltpu.make_async_copy(keys.at[j], kv.at[s], sems.at[s]),
            pltpu.make_async_copy(values.at[j], kv.at[half_slots + s], sems.at[half_slots + s]),
        )
        traded = (
            pltpu.make_async_copy(moved_keys.at[s], kv.at[s], sems.at[s]),
            pltpu.make_async_copy(
                moved_values.at[s], kv.at[half_slots + s], sems.at[half_slots + s]
            ),
        )

        waits.append((j, own, traded))
    for kind in range(2):
        for j, own, traded in waits:

            @pl.when(offsets[j] == 0)
            def _():
                own[kind].start()

            @pl.when(offsets[j] != 0)
            def _():
                traded[kind].start()

    return [c for _, own, _ in waits for c in own]


def attend_slots(side, lengths, offsets, b_ref, kv, gated):
    half_slots, cap, width = kv.shape[0] // 2, kv.shape[1], kv.shape[2]
    new = b_ref.shape[0] // half_slots
    heads = width // HEAD
    lane_head = lax.broadcasted_iota(jnp.int32, (new, width), 1) // HEAD
    position = lax.broadcasted_iota(jnp.int32, (1, cap), 1)
    row = lax.broadcasted_iota(jnp.int32, (heads * new, new), 0) % new
    causal = row >= lax.broadcasted_iota(jnp.int32, (heads * new, new), 1)
    pair_lane = lax.broadcasted_iota(jnp.int32, (new, 2 * HEAD), 1) // HEAD

    def weigh(s):
        j = 2 * s + side
        at = slice(s * new, (s + 1) * new)
        queries = b_ref[at, 2 * width : 3 * width] * jnp.bfloat16(0.5 * HEAD**-0.5)
        fresh_keys = b_ref[at, 3 * width :]
        zero = jnp.zeros_like(queries)
        spread_q = jnp.concatenate(
            [jnp.where(lane_head == h, queries, zero) for h in range(heads)], axis=0
        )
        used = jnp.where(offsets[j] == 0, lengths[j] * BLOCK, cap)
        half = lax.dot_general(spread_q, kv[s], NT, preferred_element_type=jnp.float32)
        cached = jnp.where(position < used, half + half * jnp.tanh(half), 0.0)
        half = lax.dot_general(spread_q, fresh_keys, NT, preferred_element_type=jnp.float32)
        fresh = jnp.where(causal, half + half * jnp.tanh(half), 0.0)
        return cached.astype(jnp.bfloat16), fresh.astype(jnp.bfloat16)

    def finish(s, cached, fresh):
        at = slice(s * new, (s + 1) * new)
        gate = b_ref[at, :width].astype(jnp.float32)
        fresh_values = b_ref[at, width : 2 * width]
        total = lax.dot_general(
            cached, kv[half_slots + s], NN, preferred_element_type=jnp.float32
        )
        total = total + lax.dot_general(
            fresh, fresh_values, NN, preferred_element_type=jnp.float32
        )
        for pair in range(heads // 2):
            lanes = slice(2 * HEAD * pair, 2 * HEAD * (pair + 1))
            result = jnp.zeros((new, 2 * HEAD), jnp.float32)
            for within in range(2):
                h = 2 * pair + within
                mine = pair_lane == within
                x = jnp.where(mine, total[h * new : (h + 1) * new, lanes], 0.0)
                average = jnp.sum(x, axis=-1, keepdims=True) * (1.0 / HEAD)
                centred = jnp.where(mine, x - average, 0.0)
                spread = jnp.sum(centred * centred, axis=-1, keepdims=True) * (1.0 / HEAD)
                result = result + centred * lax.rsqrt(spread + 1e-05)
            gated[at, lanes] = (result * gate[:, lanes]).astype(jnp.bfloat16)

    weights = [weigh(s) for s in range(half_slots)]
    for s in range(half_slots):
        finish(s, *weights[s])


def project_out(gated, w_ref, out_ref, width):
    for p in range(out_ref.shape[0]):
        out_ref[p] = lax.dot_general(
            gated[...],
            w_ref[:, p * width : (p + 1) * width],
            NN,
            preferred_element_type=jnp.float32,
        ).astype(jnp.bfloat16)


def first_kernel(
    lengths, offsets, x_any, gain_ref, w_hbm, keys, values, wo_hbm, moved_keys, moved_values,
    out_ref, odd_hbm,
    x_ref, w_ref, wo_ref, kv, normed_ref, even_ref, odd_ref, gated, sems, kv_sems,
):
    parts, total, width = x_ref.shape
    features = parts * width
    x_copy = pltpu.make_async_copy(x_any, x_ref, sems.at[0])
    rest = [
        pltpu.make_async_copy(w_hbm, w_ref, sems.at[1]),
        pltpu.make_async_copy(wo_hbm, wo_ref, sems.at[2]),
    ]
    for c in [x_copy] + rest:
        c.start()
    rest += cache_copies(0, offsets, keys, values, moved_keys, moved_values, kv, kv_sems)
    x_copy.wait()
    x = jnp.concatenate([x_ref[p] for p in range(parts)], axis=1).astype(jnp.float32)
    average = jnp.sum(x, axis=-1, keepdims=True) * (1.0 / features)
    centred = x - average
    spread = jnp.sum(centred * centred, axis=-1, keepdims=True) * (1.0 / features)
    normed = centred * lax.rsqrt(spread + 1e-05) * gain_ref[...]
    normed_ref[...] = normed.astype(jnp.bfloat16)

    for c in rest:
        c.wait()
    half = 0.5 * lax.dot_general(
        normed_ref[...], w_ref[...], NN, preferred_element_type=jnp.float32
    )
    branch = (half + half * jnp.tanh(half)).astype(jnp.bfloat16)
    for j in range(total // NEW):
        target = odd_ref if j % 2 else even_ref
        target[(j // 2) * NEW : (j // 2 + 1) * NEW, :] = branch[j * NEW : (j + 1) * NEW, :]

    odd_copy = pltpu.make_async_copy(odd_ref, odd_hbm, sems.at[3])
    odd_copy.start()
    attend_slots(0, lengths, offsets, even_ref, kv, gated)
    project_out(gated, wo_ref, out_ref, width)
    odd_copy.wait()


def second_kernel(
    lengths, offsets, b_hbm, keys, values, w_hbm, moved, out_ref, b_ref, w_ref, kv, gated, sems, kv_sems
):
    half_slots, width = kv.shape[0] // 2, kv.shape[2]
    copies = [
        pltpu.make_async_copy(b_hbm, b_ref, sems.at[0]),
        pltpu.make_async_copy(w_hbm, w_ref, sems.at[1]),
    ]
    for c in copies:
        c.start()
    moved_keys, moved_values = moved.at[:half_slots], moved.at[half_slots:]
    copies += cache_copies(1, offsets, keys, values, moved_keys, moved_values, kv, kv_sems)
    for c in copies:
        c.wait()
    attend_slots(1, lengths, offsets, b_ref, kv, gated)
    project_out(gated, w_ref, out_ref, width)


def first(lengths, offsets, x4, gain, w, keys, values, w_out, moved):
    slots, cap, width = keys.shape
    parts, total, _ = x4.shape
    half, wide = total // 2, w.shape[1]
    bf16 = jnp.bfloat16
    return pl.pallas_call(
        first_kernel,
        out_shape=(jax.ShapeDtypeStruct((parts, half, width), bf16), pltpu.HBM((half, wide), bf16)),
        in_specs=[SMEM, SMEM, ANY, VMEM, HBM, HBM, HBM, HBM, ANY, ANY],
        out_specs=(VMEM, HBM),
        scratch_shapes=[
            pltpu.VMEM(x4.shape, bf16),
            pltpu.VMEM(w.shape, bf16),
            pltpu.VMEM(w_out.shape, bf16),
            pltpu.VMEM((slots, cap, width), bf16),
            pltpu.VMEM((total, parts * width), bf16),
            pltpu.VMEM((half, wide), bf16),
            pltpu.VMEM((half, wide), bf16),
            pltpu.VMEM((half, width), bf16),
            pltpu.SemaphoreType.DMA((4,)),
            pltpu.SemaphoreType.DMA((slots,)),
        ],
        compiler_params=pltpu.CompilerParams(vmem_limit_bytes=28 * 2**20),
        cost_estimate=pl.CostEstimate(flops=10**8, bytes_accessed=0, transcendentals=0),
    )(lengths, offsets, x4, gain, in_hbm(w), in_hbm(keys), in_hbm(values), in_hbm(w_out), *moved)


def second(lengths, offsets, branches, keys, values, w_out, moved):
    slots, cap, width = keys.shape
    parts, rows = w_out.shape[1] // width, branches.shape[0]
    bf16 = jnp.bfloat16
    operands = [in_hbm(a) for a in (branches, keys, values, w_out, moved)]
    return pl.pallas_call(
        second_kernel,
        out_shape=jax.ShapeDtypeStruct((parts, rows, width), bf16),
        in_specs=[SMEM, SMEM] + [HBM] * len(operands),
        out_specs=VMEM,
        scratch_shapes=[
            pltpu.VMEM(branches.shape, bf16),
            pltpu.VMEM(w_out.shape, bf16),
            pltpu.VMEM((slots, cap, width), bf16),
            pltpu.VMEM((rows, width), bf16),
            pltpu.SemaphoreType.DMA((2,)),
            pltpu.SemaphoreType.DMA((slots,)),
        ],
        compiler_params=pltpu.CompilerParams(vmem_limit_bytes=20 * 2**20),
        cost_estimate=pl.CostEstimate(flops=3 * 10**9, bytes_accessed=0, transcendentals=0),
    )(lengths, offsets, *operands)


def gate_kernel(x_any, gain_ref, out_ref):
    del x_any
    out_ref[...] = gain_ref[...]


def gain_after(x4, gain):
    return pl.pallas_call(
        gate_kernel,
        out_shape=jax.ShapeDtypeStruct(gain.shape, gain.dtype),
        in_specs=[ANY, VMEM],
        out_specs=VMEM,
        cost_estimate=pl.CostEstimate(flops=9 * 10**9, bytes_accessed=0, transcendentals=0),
    )(x4, gain)


def combine_kernel(events, even, odd, out_ref):
    parts, rows, _ = even.shape
    half_slots = out_ref.shape[0] // 2 // NEW
    for j in range(2 * half_slots):
        at = slice(j * NEW, (j + 1) * NEW)
        terms_at = slice((j // 2) * NEW, (j // 2 + 1) * NEW)
        terms = odd if j % 2 else even
        total = terms[0, terms_at, :].astype(jnp.float32)
        for p in range(1, parts):
            total = total + terms[p, terms_at, :].astype(jnp.float32)
        out_ref[at, :] = (events[at, :].astype(jnp.float32) + total).astype(out_ref.dtype)


def combine(events, even, odd):
    return pl.pallas_call(
        combine_kernel,
        out_shape=jax.ShapeDtypeStruct(events.shape, events.dtype),
        in_specs=[VMEM, VMEM, VMEM],
        out_specs=VMEM,
        compiler_params=pltpu.CompilerParams(vmem_limit_bytes=6 * 2**20),
    )(events, even, odd)


def in_hbm(array):
    return pltpu.with_memory_space_constraint(array, pltpu.HBM)


def on_device(events, norm_gain, w_uvqk, w_out, cache_keys, cache_values, lengths, swap_offset):
    slots, cap, width = cache_keys.shape
    users = lax.axis_size("user")
    heads = lax.axis_size("head")
    caches = (cache_keys, cache_values)

    def to_heads(blocks):
        return lax.all_to_all(blocks, "head", 0, 0)

    odd_pay, spread = pack(1, 1, lengths, *caches, events, heads)
    across = [(i, (((i + 1) ^ 1) - 1) % users) for i in range(users)]
    odd = lax.ppermute(odd_pay, "user", across)
    gathered = to_heads(spread)
    later_lengths, _ = lax.optimization_barrier((lengths, odd_pay))
    within = [(i, i ^ 1) for i in range(users)]
    even = [lax.ppermute(pay, "user", within) for pay in pack(0, 2, later_lengths, *caches)]

    w = w_uvqk.reshape(w_uvqk.shape[0], 4 * width)
    gain = gain_after(gathered, norm_gain[None, :])
    even_part, odd_branches = first(
        lengths, swap_offset, gathered, gain, w, *caches, w_out, even
    )
    even_terms = to_heads(even_part)
    odd_part = second(lengths, swap_offset, odd_branches, *caches, w_out, odd)
    odd_part, even_terms = lax.optimization_barrier((odd_part, even_terms))
    odd_terms = to_heads(odd_part)
    return combine(events, even_terms, odd_terms)


def solution(mesh):
    return jax.shard_map(
        on_device,
        mesh=mesh,
        in_specs=(
            P("user", "head"),
            P(),
            P(None, None, "head"),
            P("head", None),
            P("user", None, "head"),
            P("user", None, "head"),
            P("user"),
            P("user"),
        ),
        out_specs=P("user", "head"),
        check_vma=False,
    )
```

```python
import functools

import jax
import jax.numpy as jnp
from jax import lax
from jax.experimental import pallas as pl
from jax.experimental.pallas import tpu as pltpu
from jax.sharding import PartitionSpec as P

HEAD = 64
BLOCK = 128
NEW = 64
NT = (((1,), (1,)), ((), ()))
NN = (((1,), (0,)), ((), ()))
VMEM = pl.BlockSpec(memory_space=pltpu.VMEM)
SMEM = pl.BlockSpec(memory_space=pltpu.SMEM)
HBM = pl.BlockSpec(memory_space=pltpu.HBM)
ANY = pl.BlockSpec(memory_space=pl.ANY)


def pack_kernel(side, lengths_hbm, keys, values, *rest):
    *rest, buf, lengths, in_sems, out_sems, sem = rest
    spread = None
    if side == 1:
        events, *pays, spread, events_ref, spread_sems = rest
    else:
        pays = rest
    half_slots, cap, width = keys.shape[0] // 2, keys.shape[1], keys.shape[2]
    places = [pay.at[s] for pay in pays for s in range(pay.shape[0])]
    lengths_copy = pltpu.make_async_copy(lengths_hbm, lengths, sem.at[0])
    lengths_copy.start()
    arrive, leave = [], []
    for s in range(half_slots):
        j = 2 * s + side
        for array, slot in ((values, half_slots + s), (keys, s)):
            arrive.append(pltpu.make_async_copy(array.at[j], buf.at[slot], in_sems.at[slot]))
            leave.append(pltpu.make_async_copy(buf.at[slot], places[slot], out_sems.at[slot]))
    for c in arrive:
        c.start()
    if spread is not None:
        events_copy = pltpu.make_async_copy(events, events_ref, sem.at[1])
        events_copy.start()
    lengths_copy.wait()
    for i, c in enumerate(arrive):
        c.wait()
        if i % 2 == 0:
            s = i // 2
            for block in range(1, cap // BLOCK):

                @pl.when(lengths[2 * s + side] <= block)
                def _():
                    buf[half_slots + s, block * BLOCK : (block + 1) * BLOCK, :] = jnp.zeros(
                        (BLOCK, width), buf.dtype
                    )

        leave[i].start()
    if spread is not None:
        events_copy.wait()
        for p in range(spread.shape[0]):
            copy = pltpu.make_async_copy(events_ref, spread.at[p], spread_sems.at[p])
            copy.start()
            leave.append(copy)
    for c in leave:
        c.wait()


def pack(side, pieces, lengths, keys, values, events=None, parts=0):
    slots, cap, width = keys.shape
    operands = [in_hbm(lengths), in_hbm(keys), in_hbm(values)]
    outs = [pltpu.HBM((slots // pieces, cap, width), keys.dtype)] * pieces
    scratch = []
    if events is not None:
        operands.append(in_hbm(events))
        outs.append(pltpu.HBM((parts,) + events.shape, events.dtype))
        scratch = [pltpu.VMEM(events.shape, events.dtype), pltpu.SemaphoreType.DMA((parts,))]
    return pl.pallas_call(
        functools.partial(pack_kernel, side),
        out_shape=outs,
        in_specs=[HBM] * len(operands),
        out_specs=[HBM] * len(outs),
        scratch_shapes=scratch
        + [
            pltpu.VMEM((slots, cap, width), keys.dtype),
            pltpu.SMEM(lengths.shape, lengths.dtype),
            pltpu.SemaphoreType.DMA((slots,)),
            pltpu.SemaphoreType.DMA((slots,)),
            pltpu.SemaphoreType.DMA((2,)),
        ],
        compiler_params=pltpu.CompilerParams(vmem_limit_bytes=6 * 2**20),
        cost_estimate=pl.CostEstimate(
            flops=0, bytes_accessed=4 * 10**6 if side else 15 * 10**6, transcendentals=0
        ),
    )(*operands)


def cache_copies(side, offsets, keys, values, moved_keys, moved_values, kv, sems):
    half_slots = kv.shape[0] // 2
    waits = []
    for s in range(half_slots):
        j = 2 * s + side
        own = (
            pltpu.make_async_copy(keys.at[j], kv.at[s], sems.at[s]),
            pltpu.make_async_copy(values.at[j], kv.at[half_slots + s], sems.at[half_slots + s]),
        )
        traded = (
            pltpu.make_async_copy(moved_keys.at[s], kv.at[s], sems.at[s]),
            pltpu.make_async_copy(
                moved_values.at[s], kv.at[half_slots + s], sems.at[half_slots + s]
            ),
        )

        waits.append((j, own, traded))
    for kind in range(2):
        for j, own, traded in waits:

            @pl.when(offsets[j] == 0)
            def _():
                own[kind].start()

            @pl.when(offsets[j] != 0)
            def _():
                traded[kind].start()

    return [c for _, own, _ in waits for c in own]


def attend_slots(side, lengths, offsets, b_ref, kv, gated):
    half_slots, cap, width = kv.shape[0] // 2, kv.shape[1], kv.shape[2]
    new = b_ref.shape[0] // half_slots
    heads = width // HEAD
    lane_head = lax.broadcasted_iota(jnp.int32, (new, width), 1) // HEAD
    position = lax.broadcasted_iota(jnp.int32, (1, cap), 1)
    row = lax.broadcasted_iota(jnp.int32, (heads * new, new), 0) % new
    causal = row >= lax.broadcasted_iota(jnp.int32, (heads * new, new), 1)
    pair_lane = lax.broadcasted_iota(jnp.int32, (new, 2 * HEAD), 1) // HEAD

    def weigh(s):
        j = 2 * s + side
        at = slice(s * new, (s + 1) * new)
        queries = b_ref[at, 2 * width : 3 * width] * jnp.bfloat16(0.5 * HEAD**-0.5)
        fresh_keys = b_ref[at, 3 * width :]
        zero = jnp.zeros_like(queries)
        spread_q = jnp.concatenate(
            [jnp.where(lane_head == h, queries, zero) for h in range(heads)], axis=0
        )
        used = jnp.where(offsets[j] == 0, lengths[j] * BLOCK, cap)
        half = lax.dot_general(spread_q, kv[s], NT, preferred_element_type=jnp.float32)
        cached = jnp.where(position < used, half + half * jnp.tanh(half), 0.0)
        half = lax.dot_general(spread_q, fresh_keys, NT, preferred_element_type=jnp.float32)
        fresh = jnp.where(causal, half + half * jnp.tanh(half), 0.0)
        return cached.astype(jnp.bfloat16), fresh.astype(jnp.bfloat16)

    def finish(s, cached, fresh):
        at = slice(s * new, (s + 1) * new)
        gate = b_ref[at, :width].astype(jnp.float32)
        fresh_values = b_ref[at, width : 2 * width]
        total = lax.dot_general(
            cached, kv[half_slots + s], NN, preferred_element_type=jnp.float32
        )
        total = total + lax.dot_general(
            fresh, fresh_values, NN, preferred_element_type=jnp.float32
        )
        for pair in range(heads // 2):
            lanes = slice(2 * HEAD * pair, 2 * HEAD * (pair + 1))
            result = jnp.zeros((new, 2 * HEAD), jnp.float32)
            for within in range(2):
                h = 2 * pair + within
                mine = pair_lane == within
                x = jnp.where(mine, total[h * new : (h + 1) * new, lanes], 0.0)
                average = jnp.sum(x, axis=-1, keepdims=True) * (1.0 / HEAD)
                centred = jnp.where(mine, x - average, 0.0)
                spread = jnp.sum(centred * centred, axis=-1, keepdims=True) * (1.0 / HEAD)
                result = result + centred * lax.rsqrt(spread + 1e-05)
            gated[at, lanes] = (result * gate[:, lanes]).astype(jnp.bfloat16)

    weights = [weigh(s) for s in range(half_slots)]
    for s in range(half_slots):
        finish(s, *weights[s])


def first_kernel(
    lengths, offsets, x_any, gain_ref, w_hbm, keys, values, wo_hbm, moved_keys, moved_values,
    out_hbm, odd_hbm,
    x_ref, w_ref, wo_ref, kv, normed_ref, even_ref, odd_ref, gated, out_ref, sems, kv_sems, out_sems,
):
    parts, total, width = x_ref.shape
    features = parts * width
    x_copy = pltpu.make_async_copy(x_any, x_ref, sems.at[0])
    rest = [
        pltpu.make_async_copy(w_hbm, w_ref, sems.at[1]),
        pltpu.make_async_copy(wo_hbm, wo_ref, sems.at[2]),
    ]
    for c in [x_copy] + rest:
        c.start()
    rest += cache_copies(0, offsets, keys, values, moved_keys, moved_values, kv, kv_sems)
    x_copy.wait()
    x = jnp.concatenate([x_ref[p] for p in range(parts)], axis=1).astype(jnp.float32)
    average = jnp.sum(x, axis=-1, keepdims=True) * (1.0 / features)
    centred = x - average
    spread = jnp.sum(centred * centred, axis=-1, keepdims=True) * (1.0 / features)
    normed = centred * lax.rsqrt(spread + 1e-05) * gain_ref[...]
    normed_ref[...] = normed.astype(jnp.bfloat16)

    for c in rest:
        c.wait()
    half = 0.5 * lax.dot_general(
        normed_ref[...], w_ref[...], NN, preferred_element_type=jnp.float32
    )
    branch = (half + half * jnp.tanh(half)).astype(jnp.bfloat16)
    for j in range(total // NEW):
        target = odd_ref if j % 2 else even_ref
        target[(j // 2) * NEW : (j // 2 + 1) * NEW, :] = branch[j * NEW : (j + 1) * NEW, :]

    odd_copy = pltpu.make_async_copy(odd_ref, odd_hbm, sems.at[3])
    odd_copy.start()
    attend_slots(0, lengths, offsets, even_ref, kv, gated)
    leave = [odd_copy]
    for p in range(parts):
        out_ref[p] = lax.dot_general(
            gated[...],
            wo_ref[:, p * width : (p + 1) * width],
            NN,
            preferred_element_type=jnp.float32,
        ).astype(jnp.bfloat16)
        leave.append(pltpu.make_async_copy(out_ref.at[p], out_hbm.at[p], out_sems.at[p]))
        leave[-1].start()
    for c in leave:
        c.wait()


def second_kernel(
    lengths, offsets, head, b_hbm, keys, values, w_hbm, moved, *rest
):
    *outs, b_ref, w_ref, kv, gated, sems, kv_sems = rest
    parts, half_slots, width = len(outs), kv.shape[0] // 2, kv.shape[2]
    copies = [
        pltpu.make_async_copy(b_hbm, b_ref, sems.at[0]),
        pltpu.make_async_copy(w_hbm, w_ref, sems.at[1]),
    ]
    for c in copies:
        c.start()
    moved_keys, moved_values = moved.at[:half_slots], moved.at[half_slots:]
    copies += cache_copies(1, offsets, keys, values, moved_keys, moved_values, kv, kv_sems)
    for c in copies:
        c.wait()
    attend_slots(1, lengths, offsets, b_ref, kv, gated)
    for distance, out_ref in enumerate(outs):
        target = lax.rem(head[0] + distance, parts)
        at = pl.ds(pl.multiple_of(target * width, width), width)
        out_ref[...] = lax.dot_general(
            gated[...], w_ref[:, at], NN, preferred_element_type=jnp.float32
        ).astype(jnp.bfloat16)


def first(lengths, offsets, x4, gain, w, keys, values, w_out, moved):
    slots, cap, width = keys.shape
    parts, total, _ = x4.shape
    half, wide = total // 2, w.shape[1]
    bf16 = jnp.bfloat16
    return pl.pallas_call(
        first_kernel,
        out_shape=(pltpu.HBM((parts, half, width), bf16), pltpu.HBM((half, wide), bf16)),
        in_specs=[SMEM, SMEM, ANY, VMEM, HBM, HBM, HBM, HBM, ANY, ANY],
        out_specs=(HBM, HBM),
        scratch_shapes=[
            pltpu.VMEM(x4.shape, bf16),
            pltpu.VMEM(w.shape, bf16),
            pltpu.VMEM(w_out.shape, bf16),
            pltpu.VMEM((slots, cap, width), bf16),
            pltpu.VMEM((total, parts * width), bf16),
            pltpu.VMEM((half, wide), bf16),
            pltpu.VMEM((half, wide), bf16),
            pltpu.VMEM((half, width), bf16),
            pltpu.VMEM((parts, half, width), bf16),
            pltpu.SemaphoreType.DMA((4,)),
            pltpu.SemaphoreType.DMA((slots,)),
            pltpu.SemaphoreType.DMA((parts,)),
        ],
        compiler_params=pltpu.CompilerParams(vmem_limit_bytes=28 * 2**20),
        cost_estimate=pl.CostEstimate(flops=10**8, bytes_accessed=0, transcendentals=0),
    )(lengths, offsets, x4, gain, in_hbm(w), in_hbm(keys), in_hbm(values), in_hbm(w_out), *moved)


def second(lengths, offsets, head, branches, keys, values, w_out, moved):
    slots, cap, width = keys.shape
    parts, rows = w_out.shape[1] // width, branches.shape[0]
    bf16 = jnp.bfloat16
    operands = [in_hbm(a) for a in (branches, keys, values, w_out, moved)]
    return pl.pallas_call(
        second_kernel,
        out_shape=[jax.ShapeDtypeStruct((rows, width), bf16)] * parts,
        in_specs=[SMEM, SMEM, SMEM] + [HBM] * len(operands),
        out_specs=[VMEM] * parts,
        scratch_shapes=[
            pltpu.VMEM(branches.shape, bf16),
            pltpu.VMEM(w_out.shape, bf16),
            pltpu.VMEM((slots, cap, width), bf16),
            pltpu.VMEM((rows, width), bf16),
            pltpu.SemaphoreType.DMA((2,)),
            pltpu.SemaphoreType.DMA((slots,)),
        ],
        compiler_params=pltpu.CompilerParams(vmem_limit_bytes=20 * 2**20),
        cost_estimate=pl.CostEstimate(flops=3 * 10**9, bytes_accessed=0, transcendentals=0),
    )(lengths, offsets, head, *operands)


def gate_kernel(x_any, gain_ref, out_ref):
    del x_any
    out_ref[...] = gain_ref[...]


def gain_after(x4, gain):
    return pl.pallas_call(
        gate_kernel,
        out_shape=jax.ShapeDtypeStruct(gain.shape, gain.dtype),
        in_specs=[ANY, VMEM],
        out_specs=VMEM,
        compiler_params=pltpu.CompilerParams(vmem_limit_bytes=2**20),
        cost_estimate=pl.CostEstimate(flops=9 * 10**9, bytes_accessed=0, transcendentals=0),
    )(x4, gain)


def combine_kernel(events, even, *rest):
    *odd, out_ref = rest
    even = [even.at[p] for p in range(even.shape[0])]
    for j in range(out_ref.shape[0] // NEW):
        at = slice(j * NEW, (j + 1) * NEW)
        terms_at = slice((j // 2) * NEW, (j // 2 + 1) * NEW)
        terms = odd if j % 2 else even
        total = terms[0][terms_at, :].astype(jnp.float32)
        for term in terms[1:]:
            total = total + term[terms_at, :].astype(jnp.float32)
        out_ref[at, :] = (events[at, :].astype(jnp.float32) + total).astype(out_ref.dtype)


def combine(events, even, odd):
    return pl.pallas_call(
        combine_kernel,
        out_shape=jax.ShapeDtypeStruct(events.shape, events.dtype),
        in_specs=[VMEM] * (2 + len(odd)),
        out_specs=VMEM,
        compiler_params=pltpu.CompilerParams(vmem_limit_bytes=6 * 2**20),
    )(events, even, *odd)


def in_hbm(array):
    return pltpu.with_memory_space_constraint(array, pltpu.HBM)


def on_device(events, norm_gain, w_uvqk, w_out, cache_keys, cache_values, lengths, swap_offset):
    slots, cap, width = cache_keys.shape
    users = lax.axis_size("user")
    heads = lax.axis_size("head")
    caches = (cache_keys, cache_values)

    def to_heads(blocks):
        return lax.all_to_all(blocks, "head", 0, 0)

    odd_pay, spread = pack(1, 1, lengths, *caches, events, heads)
    across = [(i, (((i + 1) ^ 1) - 1) % users) for i in range(users)]
    odd = lax.ppermute(odd_pay, "user", across)
    gathered = to_heads(spread)
    later_lengths, _ = lax.optimization_barrier((lengths, odd_pay))
    within = [(i, i ^ 1) for i in range(users)]
    even = [lax.ppermute(pay, "user", within) for pay in pack(0, 2, later_lengths, *caches)]

    w = w_uvqk.reshape(w_uvqk.shape[0], 4 * width)
    gain = gain_after(gathered, norm_gain[None, :])
    even_part, odd_branches = first(
        lengths, swap_offset, gathered, gain, w, *caches, w_out, even
    )
    even_terms = to_heads(even_part)
    head = lax.axis_index("head").astype(jnp.int32)[None]
    odd_terms = list(
        second(lengths, swap_offset, head, odd_branches, *caches, w_out, odd)
    )
    for distance in range(1, heads):
        ahead = [(h, (h + distance) % heads) for h in range(heads)]
        odd_terms[distance] = lax.ppermute(odd_terms[distance], "head", ahead)
    return combine(events, even_terms, odd_terms)


def solution(mesh):
    return jax.shard_map(
        on_device,
        mesh=mesh,
        in_specs=(
            P("user", "head"),
            P(),
            P(None, None, "head"),
            P("head", None),
            P("user", None, "head"),
            P("user", None, "head"),
            P("user"),
            P("user"),
        ),
        out_specs=P("user", "head"),
        check_vma=False,
    )
```

```python
import functools

import jax
import jax.numpy as jnp
from jax import lax
from jax.experimental import pallas as pl
from jax.experimental.pallas import tpu as pltpu
from jax.sharding import PartitionSpec as P

HEAD = 64
BLOCK = 128
NEW = 64
NT = (((1,), (1,)), ((), ()))
NN = (((1,), (0,)), ((), ()))
VMEM = pl.BlockSpec(memory_space=pltpu.VMEM)
SMEM = pl.BlockSpec(memory_space=pltpu.SMEM)
HBM = pl.BlockSpec(memory_space=pltpu.HBM)
ANY = pl.BlockSpec(memory_space=pl.ANY)


def pack_kernel(side, lengths_hbm, keys, values, *rest):
    *rest, buf, lengths, in_sems, out_sems, sem = rest
    spread = None
    if side == 1:
        events, *pays, spread, events_ref, spread_sems = rest
    else:
        pays = rest
    half_slots, cap, width = keys.shape[0] // 2, keys.shape[1], keys.shape[2]
    places = [pay.at[s] for pay in pays for s in range(pay.shape[0])]
    lengths_copy = pltpu.make_async_copy(lengths_hbm, lengths, sem.at[0])
    lengths_copy.start()
    arrive, leave = [], []
    for s in range(half_slots):
        j = 2 * s + side
        for array, slot in ((values, half_slots + s), (keys, s)):
            arrive.append(pltpu.make_async_copy(array.at[j], buf.at[slot], in_sems.at[slot]))
            leave.append(pltpu.make_async_copy(buf.at[slot], places[slot], out_sems.at[slot]))
    for c in arrive:
        c.start()
    if spread is not None:
        events_copy = pltpu.make_async_copy(events, events_ref, sem.at[1])
        events_copy.start()
    lengths_copy.wait()
    for i, c in enumerate(arrive):
        c.wait()
        if i % 2 == 0:
            s = i // 2
            for block in range(1, cap // BLOCK):

                @pl.when(lengths[2 * s + side] <= block)
                def _():
                    buf[half_slots + s, block * BLOCK : (block + 1) * BLOCK, :] = jnp.zeros(
                        (BLOCK, width), buf.dtype
                    )

        leave[i].start()
    if spread is not None:
        events_copy.wait()
        for p in range(spread.shape[0]):
            copy = pltpu.make_async_copy(events_ref, spread.at[p], spread_sems.at[p])
            copy.start()
            leave.append(copy)
    for c in leave:
        c.wait()


def pack(side, pieces, lengths, keys, values, events=None, parts=0):
    slots, cap, width = keys.shape
    operands = [in_hbm(lengths), in_hbm(keys), in_hbm(values)]
    outs = [pltpu.HBM((slots // pieces, cap, width), keys.dtype)] * pieces
    scratch = []
    if events is not None:
        operands.append(in_hbm(events))
        outs.append(pltpu.HBM((parts,) + events.shape, events.dtype))
        scratch = [pltpu.VMEM(events.shape, events.dtype), pltpu.SemaphoreType.DMA((parts,))]
    return pl.pallas_call(
        functools.partial(pack_kernel, side),
        out_shape=outs,
        in_specs=[HBM] * len(operands),
        out_specs=[HBM] * len(outs),
        scratch_shapes=scratch
        + [
            pltpu.VMEM((slots, cap, width), keys.dtype),
            pltpu.SMEM(lengths.shape, lengths.dtype),
            pltpu.SemaphoreType.DMA((slots,)),
            pltpu.SemaphoreType.DMA((slots,)),
            pltpu.SemaphoreType.DMA((2,)),
        ],
        compiler_params=pltpu.CompilerParams(vmem_limit_bytes=6 * 2**20),
        cost_estimate=pl.CostEstimate(
            flops=0, bytes_accessed=4 * 10**6 if side else 15 * 10**6, transcendentals=0
        ),
    )(*operands)


def cache_copies(side, offsets, keys, values, moved_keys, moved_values, kv, sems):
    half_slots = kv.shape[0] // 2
    waits = []
    for s in range(half_slots):
        j = 2 * s + side
        own = (
            pltpu.make_async_copy(keys.at[j], kv.at[s], sems.at[s]),
            pltpu.make_async_copy(values.at[j], kv.at[half_slots + s], sems.at[half_slots + s]),
        )
        traded = (
            pltpu.make_async_copy(moved_keys.at[s], kv.at[s], sems.at[s]),
            pltpu.make_async_copy(
                moved_values.at[s], kv.at[half_slots + s], sems.at[half_slots + s]
            ),
        )

        waits.append((j, own, traded))
    for kind in range(2):
        for j, own, traded in waits:

            @pl.when(offsets[j] == 0)
            def _():
                own[kind].start()

            @pl.when(offsets[j] != 0)
            def _():
                traded[kind].start()

    return [c for _, own, _ in waits for c in own]


def attend_slots(side, lengths, offsets, b_ref, kv, gated):
    half_slots, cap, width = kv.shape[0] // 2, kv.shape[1], kv.shape[2]
    new = b_ref.shape[0] // half_slots
    heads = width // HEAD
    lane_head = lax.broadcasted_iota(jnp.int32, (new, width), 1) // HEAD
    position = lax.broadcasted_iota(jnp.int32, (1, cap), 1)
    row = lax.broadcasted_iota(jnp.int32, (heads * new, new), 0) % new
    causal = row >= lax.broadcasted_iota(jnp.int32, (heads * new, new), 1)
    pair_lane = lax.broadcasted_iota(jnp.int32, (new, 2 * HEAD), 1) // HEAD

    def weigh(s):
        j = 2 * s + side
        at = slice(s * new, (s + 1) * new)
        queries = b_ref[at, 2 * width : 3 * width] * jnp.bfloat16(0.5 * HEAD**-0.5)
        fresh_keys = b_ref[at, 3 * width :]
        zero = jnp.zeros_like(queries)
        spread_q = jnp.concatenate(
            [jnp.where(lane_head == h, queries, zero) for h in range(heads)], axis=0
        )
        used = jnp.where(offsets[j] == 0, lengths[j] * BLOCK, cap)
        half = lax.dot_general(spread_q, kv[s], NT, preferred_element_type=jnp.float32)
        cached = jnp.where(position < used, half + half * jnp.tanh(half), 0.0)
        half = lax.dot_general(spread_q, fresh_keys, NT, preferred_element_type=jnp.float32)
        fresh = jnp.where(causal, half + half * jnp.tanh(half), 0.0)
        return cached.astype(jnp.bfloat16), fresh.astype(jnp.bfloat16)

    def finish(s, cached, fresh):
        at = slice(s * new, (s + 1) * new)
        gate = b_ref[at, :width].astype(jnp.float32)
        fresh_values = b_ref[at, width : 2 * width]
        total = lax.dot_general(
            cached, kv[half_slots + s], NN, preferred_element_type=jnp.float32
        )
        total = total + lax.dot_general(
            fresh, fresh_values, NN, preferred_element_type=jnp.float32
        )
        for pair in range(heads // 2):
            lanes = slice(2 * HEAD * pair, 2 * HEAD * (pair + 1))
            result = jnp.zeros((new, 2 * HEAD), jnp.float32)
            for within in range(2):
                h = 2 * pair + within
                mine = pair_lane == within
                x = jnp.where(mine, total[h * new : (h + 1) * new, lanes], 0.0)
                average = jnp.sum(x, axis=-1, keepdims=True) * (1.0 / HEAD)
                centred = jnp.where(mine, x - average, 0.0)
                spread = jnp.sum(centred * centred, axis=-1, keepdims=True) * (1.0 / HEAD)
                result = result + centred * lax.rsqrt(spread + 1e-05)
            gated[at, lanes] = (result * gate[:, lanes]).astype(jnp.bfloat16)

    weights = [weigh(s) for s in range(half_slots)]
    for s in range(half_slots):
        finish(s, *weights[s])


def project_out(gated, w_ref, out_ref, width):
    for p in range(out_ref.shape[0]):
        out_ref[p] = lax.dot_general(
            gated[...],
            w_ref[:, p * width : (p + 1) * width],
            NN,
            preferred_element_type=jnp.float32,
        ).astype(jnp.bfloat16)


def first_kernel(
    lengths_hbm, offsets_hbm, x_any, gain_ref, w_hbm, keys, values, wo_hbm, moved_keys, moved_values,
    out_hbm, odd_hbm,
    x_ref, w_ref, wo_ref, kv, normed_ref, even_ref, odd_ref, gated, out_ref, lengths, offsets,
    sems, kv_sems, out_sems,
):
    parts, total, width = x_ref.shape
    features = parts * width
    x_copy = pltpu.make_async_copy(x_any, x_ref, sems.at[0])
    rest = [
        pltpu.make_async_copy(w_hbm, w_ref, sems.at[1]),
        pltpu.make_async_copy(wo_hbm, wo_ref, sems.at[2]),
    ]
    layout = [
        pltpu.make_async_copy(offsets_hbm, offsets, sems.at[4]),
        pltpu.make_async_copy(lengths_hbm, lengths, sems.at[5]),
    ]
    for c in layout + [x_copy] + rest:
        c.start()
    for c in layout:
        c.wait()
    rest += cache_copies(0, offsets, keys, values, moved_keys, moved_values, kv, kv_sems)
    x_copy.wait()
    x = jnp.concatenate([x_ref[p] for p in range(parts)], axis=1).astype(jnp.float32)
    average = jnp.sum(x, axis=-1, keepdims=True) * (1.0 / features)
    centred = x - average
    spread = jnp.sum(centred * centred, axis=-1, keepdims=True) * (1.0 / features)
    normed = centred * lax.rsqrt(spread + 1e-05) * gain_ref[...]
    normed_ref[...] = normed.astype(jnp.bfloat16)

    for c in rest:
        c.wait()
    half = 0.5 * lax.dot_general(
        normed_ref[...], w_ref[...], NN, preferred_element_type=jnp.float32
    )
    branch = (half + half * jnp.tanh(half)).astype(jnp.bfloat16)
    for j in range(total // NEW):
        target = odd_ref if j % 2 else even_ref
        target[(j // 2) * NEW : (j // 2 + 1) * NEW, :] = branch[j * NEW : (j + 1) * NEW, :]

    odd_copy = pltpu.make_async_copy(odd_ref, odd_hbm, sems.at[3])
    odd_copy.start()
    attend_slots(0, lengths, offsets, even_ref, kv, gated)
    leave = [odd_copy]
    for p in range(parts):
        out_ref[p] = lax.dot_general(
            gated[...],
            wo_ref[:, p * width : (p + 1) * width],
            NN,
            preferred_element_type=jnp.float32,
        ).astype(jnp.bfloat16)
        leave.append(pltpu.make_async_copy(out_ref.at[p], out_hbm.at[p], out_sems.at[p]))
        leave[-1].start()
    for c in leave:
        c.wait()


def second_kernel(
    lengths, offsets, b_hbm, keys, values, w_hbm, moved, out_ref, b_ref, w_ref, kv, gated, sems, kv_sems
):
    half_slots, width = kv.shape[0] // 2, kv.shape[2]
    copies = [
        pltpu.make_async_copy(b_hbm, b_ref, sems.at[0]),
        pltpu.make_async_copy(w_hbm, w_ref, sems.at[1]),
    ]
    for c in copies:
        c.start()
    moved_keys, moved_values = moved.at[:half_slots], moved.at[half_slots:]
    copies += cache_copies(1, offsets, keys, values, moved_keys, moved_values, kv, kv_sems)
    for c in copies:
        c.wait()
    attend_slots(1, lengths, offsets, b_ref, kv, gated)
    project_out(gated, w_ref, out_ref, width)


def first(lengths, offsets, x4, gain, w, keys, values, w_out, moved):
    slots, cap, width = keys.shape
    parts, total, _ = x4.shape
    half, wide = total // 2, w.shape[1]
    bf16 = jnp.bfloat16
    return pl.pallas_call(
        first_kernel,
        out_shape=(pltpu.HBM((parts, half, width), bf16), pltpu.HBM((half, wide), bf16)),
        in_specs=[HBM, HBM, ANY, VMEM, HBM, HBM, HBM, HBM, ANY, ANY],
        out_specs=(HBM, HBM),
        scratch_shapes=[
            pltpu.VMEM(x4.shape, bf16),
            pltpu.VMEM(w.shape, bf16),
            pltpu.VMEM(w_out.shape, bf16),
            pltpu.VMEM((slots, cap, width), bf16),
            pltpu.VMEM((total, parts * width), bf16),
            pltpu.VMEM((half, wide), bf16),
            pltpu.VMEM((half, wide), bf16),
            pltpu.VMEM((half, width), bf16),
            pltpu.VMEM((parts, half, width), bf16),
            pltpu.SMEM(lengths.shape, lengths.dtype),
            pltpu.SMEM(offsets.shape, offsets.dtype),
            pltpu.SemaphoreType.DMA((6,)),
            pltpu.SemaphoreType.DMA((slots,)),
            pltpu.SemaphoreType.DMA((parts,)),
        ],
        compiler_params=pltpu.CompilerParams(vmem_limit_bytes=28 * 2**20),
        cost_estimate=pl.CostEstimate(flops=10**8, bytes_accessed=0, transcendentals=0),
    )(in_hbm(lengths), in_hbm(offsets), x4, gain, in_hbm(w), in_hbm(keys), in_hbm(values), in_hbm(w_out), *moved)


def second(lengths, offsets, branches, keys, values, w_out, moved):
    slots, cap, width = keys.shape
    parts, rows = w_out.shape[1] // width, branches.shape[0]
    bf16 = jnp.bfloat16
    operands = [in_hbm(a) for a in (branches, keys, values, w_out, moved)]
    return pl.pallas_call(
        second_kernel,
        out_shape=jax.ShapeDtypeStruct((parts, rows, width), bf16),
        in_specs=[SMEM, SMEM] + [HBM] * len(operands),
        out_specs=VMEM,
        scratch_shapes=[
            pltpu.VMEM(branches.shape, bf16),
            pltpu.VMEM(w_out.shape, bf16),
            pltpu.VMEM((slots, cap, width), bf16),
            pltpu.VMEM((rows, width), bf16),
            pltpu.SemaphoreType.DMA((2,)),
            pltpu.SemaphoreType.DMA((slots,)),
        ],
        compiler_params=pltpu.CompilerParams(vmem_limit_bytes=20 * 2**20),
        cost_estimate=pl.CostEstimate(flops=3 * 10**9, bytes_accessed=0, transcendentals=0),
    )(lengths, offsets, *operands)


def gate_kernel(x_any, gain_ref, out_ref):
    del x_any
    out_ref[...] = gain_ref[...]


def gain_after(x4, gain):
    return pl.pallas_call(
        gate_kernel,
        out_shape=jax.ShapeDtypeStruct(gain.shape, gain.dtype),
        in_specs=[ANY, VMEM],
        out_specs=VMEM,
        compiler_params=pltpu.CompilerParams(vmem_limit_bytes=2**20),
        cost_estimate=pl.CostEstimate(flops=9 * 10**9, bytes_accessed=0, transcendentals=0),
    )(x4, gain)


def combine_kernel(events, even, odd, out_ref):
    parts, rows, _ = even.shape
    half_slots = out_ref.shape[0] // 2 // NEW
    for j in range(2 * half_slots):
        at = slice(j * NEW, (j + 1) * NEW)
        terms_at = slice((j // 2) * NEW, (j // 2 + 1) * NEW)
        terms = odd if j % 2 else even
        total = terms[0, terms_at, :].astype(jnp.float32)
        for p in range(1, parts):
            total = total + terms[p, terms_at, :].astype(jnp.float32)
        out_ref[at, :] = (events[at, :].astype(jnp.float32) + total).astype(out_ref.dtype)


def combine(events, even, odd):
    return pl.pallas_call(
        combine_kernel,
        out_shape=jax.ShapeDtypeStruct(events.shape, events.dtype),
        in_specs=[VMEM, VMEM, VMEM],
        out_specs=VMEM,
        compiler_params=pltpu.CompilerParams(vmem_limit_bytes=6 * 2**20),
    )(events, even, odd)


def in_hbm(array):
    return pltpu.with_memory_space_constraint(array, pltpu.HBM)


def on_device(events, norm_gain, w_uvqk, w_out, cache_keys, cache_values, lengths, swap_offset):
    slots, cap, width = cache_keys.shape
    users = lax.axis_size("user")
    heads = lax.axis_size("head")
    caches = (cache_keys, cache_values)

    def to_heads(blocks):
        return lax.all_to_all(blocks, "head", 0, 0)

    odd_pay, spread = pack(1, 1, lengths, *caches, events, heads)
    across = [(i, (((i + 1) ^ 1) - 1) % users) for i in range(users)]
    odd = lax.ppermute(odd_pay, "user", across)
    gathered = to_heads(spread)
    later_lengths, _ = lax.optimization_barrier((lengths, odd_pay))
    within = [(i, i ^ 1) for i in range(users)]
    even = [lax.ppermute(pay, "user", within) for pay in pack(0, 2, later_lengths, *caches)]

    w = w_uvqk.reshape(w_uvqk.shape[0], 4 * width)
    gain = gain_after(gathered, norm_gain[None, :])
    even_part, odd_branches = first(
        lengths, swap_offset, gathered, gain, w, *caches, w_out, even
    )
    even_terms = to_heads(even_part)
    odd_part = second(lengths, swap_offset, odd_branches, *caches, w_out, odd)
    odd_part, even_terms = lax.optimization_barrier((odd_part, even_terms))
    odd_terms = to_heads(odd_part)
    return combine(events, even_terms, odd_terms)


def solution(mesh):
    return jax.shard_map(
        on_device,
        mesh=mesh,
        in_specs=(
            P("user", "head"),
            P(),
            P(None, None, "head"),
            P("head", None),
            P("user", None, "head"),
            P("user", None, "head"),
            P("user"),
            P("user"),
        ),
        out_specs=P("user", "head"),
        check_vma=False,
    )
```

```python
import functools

import jax
import jax.numpy as jnp
from jax import lax
from jax.experimental import pallas as pl
from jax.experimental.pallas import tpu as pltpu
from jax.sharding import PartitionSpec as P

HEAD = 64
BLOCK = 128
NEW = 64
NT = (((1,), (1,)), ((), ()))
NN = (((1,), (0,)), ((), ()))
VMEM = pl.BlockSpec(memory_space=pltpu.VMEM)
SMEM = pl.BlockSpec(memory_space=pltpu.SMEM)
HBM = pl.BlockSpec(memory_space=pltpu.HBM)
ANY = pl.BlockSpec(memory_space=pl.ANY)


def pack_kernel(side, lengths_hbm, keys, values, *rest):
    *rest, buf, lengths, in_sems, out_sems, sem = rest
    spread = None
    if side == 1:
        events, *pays, spread, events_ref, spread_sems = rest
    else:
        pays = rest
    half_slots, cap, width = keys.shape[0] // 2, keys.shape[1], keys.shape[2]
    places = [pay.at[s] for pay in pays for s in range(pay.shape[0])]
    lengths_copy = pltpu.make_async_copy(lengths_hbm, lengths, sem.at[0])
    lengths_copy.start()
    arrive, leave = [], []
    for s in range(half_slots):
        j = 2 * s + side
        for array, slot in ((values, half_slots + s), (keys, s)):
            arrive.append(pltpu.make_async_copy(array.at[j], buf.at[slot], in_sems.at[slot]))
            leave.append(pltpu.make_async_copy(buf.at[slot], places[slot], out_sems.at[slot]))
    for c in arrive:
        c.start()
    if spread is not None:
        events_copy = pltpu.make_async_copy(events, events_ref, sem.at[1])
        events_copy.start()
    lengths_copy.wait()
    for i, c in enumerate(arrive):
        c.wait()
        if i % 2 == 0:
            s = i // 2
            for block in range(1, cap // BLOCK):

                @pl.when(lengths[2 * s + side] <= block)
                def _():
                    buf[half_slots + s, block * BLOCK : (block + 1) * BLOCK, :] = jnp.zeros(
                        (BLOCK, width), buf.dtype
                    )

        leave[i].start()
    if spread is not None:
        events_copy.wait()
        for p in range(spread.shape[0]):
            copy = pltpu.make_async_copy(events_ref, spread.at[p], spread_sems.at[p])
            copy.start()
            leave.append(copy)
    for c in leave:
        c.wait()


def pack(side, pieces, lengths, keys, values, events=None, parts=0):
    slots, cap, width = keys.shape
    operands = [in_hbm(lengths), in_hbm(keys), in_hbm(values)]
    outs = [pltpu.HBM((slots // pieces, cap, width), keys.dtype)] * pieces
    scratch = []
    if events is not None:
        operands.append(in_hbm(events))
        outs.append(pltpu.HBM((parts,) + events.shape, events.dtype))
        scratch = [pltpu.VMEM(events.shape, events.dtype), pltpu.SemaphoreType.DMA((parts,))]
    return pl.pallas_call(
        functools.partial(pack_kernel, side),
        out_shape=outs,
        in_specs=[HBM] * len(operands),
        out_specs=[HBM] * len(outs),
        scratch_shapes=scratch
        + [
            pltpu.VMEM((slots, cap, width), keys.dtype),
            pltpu.SMEM(lengths.shape, lengths.dtype),
            pltpu.SemaphoreType.DMA((slots,)),
            pltpu.SemaphoreType.DMA((slots,)),
            pltpu.SemaphoreType.DMA((2,)),
        ],
        compiler_params=pltpu.CompilerParams(vmem_limit_bytes=6 * 2**20),
        cost_estimate=pl.CostEstimate(
            flops=0, bytes_accessed=4 * 10**6 if side else 15 * 10**6, transcendentals=0
        ),
    )(*operands)


def cache_copies(side, offsets, keys, values, moved_keys, moved_values, kv, sems):
    half_slots = kv.shape[0] // 2
    waits = []
    for s in range(half_slots):
        j = 2 * s + side
        own = (
            pltpu.make_async_copy(keys.at[j], kv.at[s], sems.at[s]),
            pltpu.make_async_copy(values.at[j], kv.at[half_slots + s], sems.at[half_slots + s]),
        )
        traded = (
            pltpu.make_async_copy(moved_keys.at[s], kv.at[s], sems.at[s]),
            pltpu.make_async_copy(
                moved_values.at[s], kv.at[half_slots + s], sems.at[half_slots + s]
            ),
        )

        waits.append((j, own, traded))
    for kind in range(2):
        for j, own, traded in waits:

            @pl.when(offsets[j] == 0)
            def _():
                own[kind].start()

            @pl.when(offsets[j] != 0)
            def _():
                traded[kind].start()

    return [c for _, own, _ in waits for c in own]


def attend_slots(side, lengths, offsets, b_ref, kv, gated):
    half_slots, cap, width = kv.shape[0] // 2, kv.shape[1], kv.shape[2]
    new = b_ref.shape[0] // half_slots
    heads = width // HEAD
    lane_head = lax.broadcasted_iota(jnp.int32, (new, width), 1) // HEAD
    position = lax.broadcasted_iota(jnp.int32, (1, cap), 1)
    row = lax.broadcasted_iota(jnp.int32, (heads * new, new), 0) % new
    causal = row >= lax.broadcasted_iota(jnp.int32, (heads * new, new), 1)
    pair_lane = lax.broadcasted_iota(jnp.int32, (new, 2 * HEAD), 1) // HEAD

    def weigh(s):
        j = 2 * s + side
        at = slice(s * new, (s + 1) * new)
        queries = b_ref[at, 2 * width : 3 * width] * jnp.bfloat16(0.5 * HEAD**-0.5)
        fresh_keys = b_ref[at, 3 * width :]
        zero = jnp.zeros_like(queries)
        spread_q = jnp.concatenate(
            [jnp.where(lane_head == h, queries, zero) for h in range(heads)], axis=0
        )
        used = jnp.where(offsets[j] == 0, lengths[j] * BLOCK, cap)
        half = lax.dot_general(spread_q, kv[s], NT, preferred_element_type=jnp.float32)
        cached = jnp.where(position < used, half + half * jnp.tanh(half), 0.0)
        half = lax.dot_general(spread_q, fresh_keys, NT, preferred_element_type=jnp.float32)
        fresh = jnp.where(causal, half + half * jnp.tanh(half), 0.0)
        return cached.astype(jnp.bfloat16), fresh.astype(jnp.bfloat16)

    def finish(s, cached, fresh):
        at = slice(s * new, (s + 1) * new)
        gate = b_ref[at, :width].astype(jnp.float32)
        fresh_values = b_ref[at, width : 2 * width]
        total = lax.dot_general(
            cached, kv[half_slots + s], NN, preferred_element_type=jnp.float32
        )
        total = total + lax.dot_general(
            fresh, fresh_values, NN, preferred_element_type=jnp.float32
        )
        for pair in range(heads // 2):
            lanes = slice(2 * HEAD * pair, 2 * HEAD * (pair + 1))
            result = jnp.zeros((new, 2 * HEAD), jnp.float32)
            for within in range(2):
                h = 2 * pair + within
                mine = pair_lane == within
                x = jnp.where(mine, total[h * new : (h + 1) * new, lanes], 0.0)
                average = jnp.sum(x, axis=-1, keepdims=True) * (1.0 / HEAD)
                centred = jnp.where(mine, x - average, 0.0)
                spread = jnp.sum(centred * centred, axis=-1, keepdims=True) * (1.0 / HEAD)
                result = result + centred * lax.rsqrt(spread + 1e-05)
            gated[at, lanes] = (result * gate[:, lanes]).astype(jnp.bfloat16)

    weights = [weigh(s) for s in range(half_slots)]
    for s in range(half_slots):
        finish(s, *weights[s])


def project_out(gated, w_ref, out_ref, width):
    for p in range(out_ref.shape[0]):
        out_ref[p] = lax.dot_general(
            gated[...],
            w_ref[:, p * width : (p + 1) * width],
            NN,
            preferred_element_type=jnp.float32,
        ).astype(jnp.bfloat16)


def first_kernel(
    lengths_hbm, offsets_hbm, x_any, gain_ref, w_hbm, keys, values, wo_hbm, moved_keys, moved_values,
    out_hbm, late_hbm, odd_hbm,
    x_ref, w_ref, wo_ref, kv, normed_ref, even_ref, odd_ref, gated, out_ref, lengths, offsets,
    sems, kv_sems, out_sems,
):
    parts, total, width = x_ref.shape
    features = parts * width
    x_copy = pltpu.make_async_copy(x_any, x_ref, sems.at[0])
    rest = [
        pltpu.make_async_copy(w_hbm, w_ref, sems.at[1]),
        pltpu.make_async_copy(wo_hbm, wo_ref, sems.at[2]),
    ]
    layout = [
        pltpu.make_async_copy(offsets_hbm, offsets, sems.at[4]),
        pltpu.make_async_copy(lengths_hbm, lengths, sems.at[5]),
    ]
    for c in layout + [x_copy] + rest:
        c.start()
    for c in layout:
        c.wait()
    rest += cache_copies(0, offsets, keys, values, moved_keys, moved_values, kv, kv_sems)
    x_copy.wait()
    x = jnp.concatenate([x_ref[p] for p in range(parts)], axis=1).astype(jnp.float32)
    average = jnp.sum(x, axis=-1, keepdims=True) * (1.0 / features)
    centred = x - average
    spread = jnp.sum(centred * centred, axis=-1, keepdims=True) * (1.0 / features)
    normed = centred * lax.rsqrt(spread + 1e-05) * gain_ref[...]
    normed_ref[...] = normed.astype(jnp.bfloat16)

    for c in rest:
        c.wait()
    half = 0.5 * lax.dot_general(
        normed_ref[...], w_ref[...], NN, preferred_element_type=jnp.float32
    )
    branch = (half + half * jnp.tanh(half)).astype(jnp.bfloat16)
    for j in range(total // NEW):
        target = odd_ref if j % 2 else even_ref
        target[(j // 2) * NEW : (j // 2 + 1) * NEW, :] = branch[j * NEW : (j + 1) * NEW, :]

    odd_copy = pltpu.make_async_copy(odd_ref, odd_hbm, sems.at[3])
    odd_copy.start()
    attend_slots(0, lengths, offsets, even_ref, kv, gated)
    early = out_ref.shape[1]
    leave = [odd_copy, pltpu.make_async_copy(gated.at[early:], late_hbm, sems.at[6])]
    leave[-1].start()
    for p in range(parts):
        out_ref[p] = lax.dot_general(
            gated[:early, :],
            wo_ref[:, p * width : (p + 1) * width],
            NN,
            preferred_element_type=jnp.float32,
        ).astype(jnp.bfloat16)
        leave.append(pltpu.make_async_copy(out_ref.at[p], out_hbm.at[p], out_sems.at[p]))
        leave[-1].start()
    for c in leave:
        c.wait()


def second_kernel(
    lengths, offsets, b_hbm, keys, values, w_hbm, late_hbm, moved,
    out_ref, b_ref, w_ref, kv, gated, sems, kv_sems,
):
    half_slots, width = kv.shape[0] // 2, kv.shape[2]
    copies = [
        pltpu.make_async_copy(b_hbm, b_ref, sems.at[0]),
        pltpu.make_async_copy(w_hbm, w_ref, sems.at[1]),
        pltpu.make_async_copy(late_hbm, gated.at[: late_hbm.shape[0]], sems.at[2]),
    ]
    for c in copies:
        c.start()
    moved_keys, moved_values = moved.at[:half_slots], moved.at[half_slots:]
    copies += cache_copies(1, offsets, keys, values, moved_keys, moved_values, kv, kv_sems)
    for c in copies:
        c.wait()
    attend_slots(1, lengths, offsets, b_ref, kv, gated.at[late_hbm.shape[0] :])
    project_out(gated, w_ref, out_ref, width)


def first(lengths, offsets, x4, gain, w, keys, values, w_out, moved):
    slots, cap, width = keys.shape
    parts, total, _ = x4.shape
    half, wide = total // 2, w.shape[1]
    bf16 = jnp.bfloat16
    return pl.pallas_call(
        first_kernel,
        out_shape=(
            pltpu.HBM((parts, half // 2, width), bf16),
            pltpu.HBM((half // 2, width), bf16),
            pltpu.HBM((half, wide), bf16),
        ),
        in_specs=[HBM, HBM, ANY, VMEM, HBM, HBM, HBM, HBM, ANY, ANY],
        out_specs=(HBM, HBM, HBM),
        scratch_shapes=[
            pltpu.VMEM(x4.shape, bf16),
            pltpu.VMEM(w.shape, bf16),
            pltpu.VMEM(w_out.shape, bf16),
            pltpu.VMEM((slots, cap, width), bf16),
            pltpu.VMEM((total, parts * width), bf16),
            pltpu.VMEM((half, wide), bf16),
            pltpu.VMEM((half, wide), bf16),
            pltpu.VMEM((half, width), bf16),
            pltpu.VMEM((parts, half // 2, width), bf16),
            pltpu.SMEM(lengths.shape, lengths.dtype),
            pltpu.SMEM(offsets.shape, offsets.dtype),
            pltpu.SemaphoreType.DMA((7,)),
            pltpu.SemaphoreType.DMA((slots,)),
            pltpu.SemaphoreType.DMA((parts,)),
        ],
        compiler_params=pltpu.CompilerParams(vmem_limit_bytes=28 * 2**20),
        cost_estimate=pl.CostEstimate(flops=10**8, bytes_accessed=0, transcendentals=0),
    )(in_hbm(lengths), in_hbm(offsets), x4, gain, in_hbm(w), in_hbm(keys), in_hbm(values), in_hbm(w_out), *moved)


def second(lengths, offsets, branches, late, keys, values, w_out, moved):
    slots, cap, width = keys.shape
    parts, rows = w_out.shape[1] // width, late.shape[0] + branches.shape[0]
    bf16 = jnp.bfloat16
    operands = [in_hbm(a) for a in (branches, keys, values, w_out, late, moved)]
    return pl.pallas_call(
        second_kernel,
        out_shape=jax.ShapeDtypeStruct((parts, rows, width), bf16),
        in_specs=[SMEM, SMEM] + [HBM] * len(operands),
        out_specs=VMEM,
        scratch_shapes=[
            pltpu.VMEM(branches.shape, bf16),
            pltpu.VMEM(w_out.shape, bf16),
            pltpu.VMEM((slots, cap, width), bf16),
            pltpu.VMEM((rows, width), bf16),
            pltpu.SemaphoreType.DMA((3,)),
            pltpu.SemaphoreType.DMA((slots,)),
        ],
        compiler_params=pltpu.CompilerParams(vmem_limit_bytes=20 * 2**20),
        cost_estimate=pl.CostEstimate(flops=3 * 10**9, bytes_accessed=0, transcendentals=0),
    )(lengths, offsets, *operands)


def gate_kernel(x_any, gain_ref, out_ref):
    del x_any
    out_ref[...] = gain_ref[...]


def gain_after(x4, gain):
    return pl.pallas_call(
        gate_kernel,
        out_shape=jax.ShapeDtypeStruct(gain.shape, gain.dtype),
        in_specs=[ANY, VMEM],
        out_specs=VMEM,
        compiler_params=pltpu.CompilerParams(vmem_limit_bytes=2**20),
        cost_estimate=pl.CostEstimate(flops=9 * 10**9, bytes_accessed=0, transcendentals=0),
    )(x4, gain)


def combine_kernel(events, early, late, out_ref):
    parts, early_rows, _ = early.shape
    for j in range(out_ref.shape[0] // NEW):
        at = slice(j * NEW, (j + 1) * NEW)
        terms, start = early, j // 2 * NEW
        if j % 2:
            terms, start = late, start + late.shape[1] - out_ref.shape[0] // 2
        elif start >= early_rows:
            terms, start = late, start - early_rows
        total = terms[0, start : start + NEW, :].astype(jnp.float32)
        for p in range(1, parts):
            total = total + terms[p, start : start + NEW, :].astype(jnp.float32)
        out_ref[at, :] = (events[at, :].astype(jnp.float32) + total).astype(out_ref.dtype)


def combine(events, early, late):
    return pl.pallas_call(
        combine_kernel,
        out_shape=jax.ShapeDtypeStruct(events.shape, events.dtype),
        in_specs=[VMEM, VMEM, VMEM],
        out_specs=VMEM,
        compiler_params=pltpu.CompilerParams(vmem_limit_bytes=6 * 2**20),
    )(events, early, late)


def in_hbm(array):
    return pltpu.with_memory_space_constraint(array, pltpu.HBM)


def on_device(events, norm_gain, w_uvqk, w_out, cache_keys, cache_values, lengths, swap_offset):
    slots, cap, width = cache_keys.shape
    users = lax.axis_size("user")
    heads = lax.axis_size("head")
    caches = (cache_keys, cache_values)

    def to_heads(blocks):
        return lax.all_to_all(blocks, "head", 0, 0)

    odd_pay, spread = pack(1, 1, lengths, *caches, events, heads)
    across = [(i, (((i + 1) ^ 1) - 1) % users) for i in range(users)]
    odd = lax.ppermute(odd_pay, "user", across)
    gathered = to_heads(spread)
    later_lengths, _ = lax.optimization_barrier((lengths, odd_pay))
    within = [(i, i ^ 1) for i in range(users)]
    even = [lax.ppermute(pay, "user", within) for pay in pack(0, 2, later_lengths, *caches)]

    w = w_uvqk.reshape(w_uvqk.shape[0], 4 * width)
    gain = gain_after(gathered, norm_gain[None, :])
    early_part, late_gated, odd_branches = first(
        lengths, swap_offset, gathered, gain, w, *caches, w_out, even
    )
    early_terms = to_heads(early_part)
    late_part = second(lengths, swap_offset, odd_branches, late_gated, *caches, w_out, odd)
    late_part, early_terms = lax.optimization_barrier((late_part, early_terms))
    late_terms = to_heads(late_part)
    return combine(events, early_terms, late_terms)


def solution(mesh):
    return jax.shard_map(
        on_device,
        mesh=mesh,
        in_specs=(
            P("user", "head"),
            P(),
            P(None, None, "head"),
            P("head", None),
            P("user", None, "head"),
            P("user", None, "head"),
            P("user"),
            P("user"),
        ),
        out_specs=P("user", "head"),
        check_vma=False,
    )
```

```python
import functools

import jax
import jax.numpy as jnp
from jax import lax
from jax.experimental import pallas as pl
from jax.experimental.pallas import tpu as pltpu
from jax.sharding import PartitionSpec as P

HEAD = 64
BLOCK = 128
NEW = 64
NT = (((1,), (1,)), ((), ()))
NN = (((1,), (0,)), ((), ()))
VMEM = pl.BlockSpec(memory_space=pltpu.VMEM)
SMEM = pl.BlockSpec(memory_space=pltpu.SMEM)
HBM = pl.BlockSpec(memory_space=pltpu.HBM)
ANY = pl.BlockSpec(memory_space=pl.ANY)


def pack_kernel(side, lengths_hbm, keys, values, *rest):
    *rest, buf, lengths, in_sems, out_sems, sem = rest
    spread = None
    if side == 1:
        events, *pays, spread, events_ref, spread_sems = rest
    else:
        pays = rest
    half_slots, cap, width = keys.shape[0] // 2, keys.shape[1], keys.shape[2]
    places = [pay.at[s] for pay in pays for s in range(pay.shape[0])]
    lengths_copy = pltpu.make_async_copy(lengths_hbm, lengths, sem.at[0])
    lengths_copy.start()
    arrive, leave = [], []
    for s in range(half_slots):
        j = 2 * s + side
        for array, slot in ((values, half_slots + s), (keys, s)):
            arrive.append(pltpu.make_async_copy(array.at[j], buf.at[slot], in_sems.at[slot]))
            leave.append(pltpu.make_async_copy(buf.at[slot], places[slot], out_sems.at[slot]))
    for c in arrive:
        c.start()
    if spread is not None:
        events_copy = pltpu.make_async_copy(events, events_ref, sem.at[1])
        events_copy.start()
    lengths_copy.wait()
    for i, c in enumerate(arrive):
        c.wait()
        if i % 2 == 0:
            s = i // 2
            for block in range(1, cap // BLOCK):

                @pl.when(lengths[2 * s + side] <= block)
                def _():
                    buf[half_slots + s, block * BLOCK : (block + 1) * BLOCK, :] = jnp.zeros(
                        (BLOCK, width), buf.dtype
                    )

        leave[i].start()
    if spread is not None:
        events_copy.wait()
        for p in range(spread.shape[0]):
            copy = pltpu.make_async_copy(events_ref, spread.at[p], spread_sems.at[p])
            copy.start()
            leave.append(copy)
    for c in leave:
        c.wait()


def pack(side, pieces, lengths, keys, values, events=None, parts=0):
    slots, cap, width = keys.shape
    operands = [in_hbm(lengths), in_hbm(keys), in_hbm(values)]
    outs = [pltpu.HBM((slots // pieces, cap, width), keys.dtype)] * pieces
    scratch = []
    if events is not None:
        operands.append(in_hbm(events))
        outs.append(pltpu.HBM((parts,) + events.shape, events.dtype))
        scratch = [pltpu.VMEM(events.shape, events.dtype), pltpu.SemaphoreType.DMA((parts,))]
    return pl.pallas_call(
        functools.partial(pack_kernel, side),
        out_shape=outs,
        in_specs=[HBM] * len(operands),
        out_specs=[HBM] * len(outs),
        scratch_shapes=scratch
        + [
            pltpu.VMEM((slots, cap, width), keys.dtype),
            pltpu.SMEM(lengths.shape, lengths.dtype),
            pltpu.SemaphoreType.DMA((slots,)),
            pltpu.SemaphoreType.DMA((slots,)),
            pltpu.SemaphoreType.DMA((2,)),
        ],
        compiler_params=pltpu.CompilerParams(vmem_limit_bytes=6 * 2**20),
        cost_estimate=pl.CostEstimate(
            flops=0, bytes_accessed=4 * 10**6 if side else 15 * 10**6, transcendentals=0
        ),
    )(*operands)


def cache_copies(side, offsets, keys, values, moved_keys, moved_values, kv, sems):
    half_slots = kv.shape[0] // 2
    waits = []
    for s in range(half_slots):
        j = 2 * s + side
        own = (
            pltpu.make_async_copy(keys.at[j], kv.at[s], sems.at[s]),
            pltpu.make_async_copy(values.at[j], kv.at[half_slots + s], sems.at[half_slots + s]),
        )
        traded = (
            pltpu.make_async_copy(moved_keys.at[s], kv.at[s], sems.at[s]),
            pltpu.make_async_copy(
                moved_values.at[s], kv.at[half_slots + s], sems.at[half_slots + s]
            ),
        )

        waits.append((j, own, traded))
    for kind in range(2):
        for j, own, traded in waits:

            @pl.when(offsets[j] == 0)
            def _():
                own[kind].start()

            @pl.when(offsets[j] != 0)
            def _():
                traded[kind].start()

    return [c for _, own, _ in waits for c in own]


def attend_slots(side, lengths, offsets, b_ref, kv, gated):
    half_slots, cap, width = kv.shape[0] // 2, kv.shape[1], kv.shape[2]
    new = b_ref.shape[0] // half_slots
    heads = width // HEAD
    lane_head = lax.broadcasted_iota(jnp.int32, (new, width), 1) // HEAD
    position = lax.broadcasted_iota(jnp.int32, (1, cap), 1)
    row = lax.broadcasted_iota(jnp.int32, (heads * new, new), 0) % new
    causal = row >= lax.broadcasted_iota(jnp.int32, (heads * new, new), 1)
    pair_lane = lax.broadcasted_iota(jnp.int32, (new, 2 * HEAD), 1) // HEAD

    def weigh(s):
        j = 2 * s + side
        at = slice(s * new, (s + 1) * new)
        queries = b_ref[at, 2 * width : 3 * width] * jnp.bfloat16(0.5 * HEAD**-0.5)
        fresh_keys = b_ref[at, 3 * width :]
        zero = jnp.zeros_like(queries)
        spread_q = jnp.concatenate(
            [jnp.where(lane_head == h, queries, zero) for h in range(heads)], axis=0
        )
        used = jnp.where(offsets[j] == 0, lengths[j] * BLOCK, cap)
        half = lax.dot_general(spread_q, kv[s], NT, preferred_element_type=jnp.float32)
        cached = jnp.where(position < used, half + half * jnp.tanh(half), 0.0)
        half = lax.dot_general(spread_q, fresh_keys, NT, preferred_element_type=jnp.float32)
        fresh = jnp.where(causal, half + half * jnp.tanh(half), 0.0)
        return cached.astype(jnp.bfloat16), fresh.astype(jnp.bfloat16)

    def finish(s, cached, fresh):
        at = slice(s * new, (s + 1) * new)
        gate = b_ref[at, :width].astype(jnp.float32)
        fresh_values = b_ref[at, width : 2 * width]
        total = lax.dot_general(
            cached, kv[half_slots + s], NN, preferred_element_type=jnp.float32
        )
        total = total + lax.dot_general(
            fresh, fresh_values, NN, preferred_element_type=jnp.float32
        )
        for pair in range(heads // 2):
            lanes = slice(2 * HEAD * pair, 2 * HEAD * (pair + 1))
            result = jnp.zeros((new, 2 * HEAD), jnp.float32)
            for within in range(2):
                h = 2 * pair + within
                mine = pair_lane == within
                x = jnp.where(mine, total[h * new : (h + 1) * new, lanes], 0.0)
                average = jnp.sum(x, axis=-1, keepdims=True) * (1.0 / HEAD)
                centred = jnp.where(mine, x - average, 0.0)
                spread = jnp.sum(centred * centred, axis=-1, keepdims=True) * (1.0 / HEAD)
                result = result + centred * lax.rsqrt(spread + 1e-05)
            gated[at, lanes] = (result * gate[:, lanes]).astype(jnp.bfloat16)

    weights = [weigh(s) for s in range(half_slots)]
    for s in range(half_slots):
        finish(s, *weights[s])


def project_out(gated, w_ref, out_ref, width):
    for p in range(out_ref.shape[0]):
        out_ref[p] = lax.dot_general(
            gated[...],
            w_ref[:, p * width : (p + 1) * width],
            NN,
            preferred_element_type=jnp.float32,
        ).astype(jnp.bfloat16)


def first_kernel(
    lengths_hbm, offsets_hbm, x_any, gain_ref, w_hbm, keys, values, wo_hbm, moved_keys, moved_values,
    out_hbm, odd_hbm,
    x_ref, w_ref, wo_ref, kv, normed_ref, even_ref, odd_ref, gated, out_ref, lengths, offsets,
    sems, kv_sems, out_sems,
):
    parts, total, width = x_ref.shape
    features = parts * width
    x_copy = pltpu.make_async_copy(x_any, x_ref, sems.at[0])
    rest = [
        pltpu.make_async_copy(w_hbm, w_ref, sems.at[1]),
        pltpu.make_async_copy(wo_hbm, wo_ref, sems.at[2]),
    ]
    layout = [
        pltpu.make_async_copy(offsets_hbm, offsets, sems.at[4]),
        pltpu.make_async_copy(lengths_hbm, lengths, sems.at[5]),
    ]
    for c in layout + [x_copy] + rest:
        c.start()
    for c in layout:
        c.wait()
    rest += cache_copies(0, offsets, keys, values, moved_keys, moved_values, kv, kv_sems)
    x_copy.wait()
    x = jnp.concatenate([x_ref[p] for p in range(parts)], axis=1).astype(jnp.float32)
    average = jnp.sum(x, axis=-1, keepdims=True) * (1.0 / features)
    centred = x - average
    spread = jnp.sum(centred * centred, axis=-1, keepdims=True) * (1.0 / features)
    normed = centred * lax.rsqrt(spread + 1e-05) * gain_ref[...]
    normed_ref[...] = normed.astype(jnp.bfloat16)

    for c in rest:
        c.wait()
    half = 0.5 * lax.dot_general(
        normed_ref[...], w_ref[...], NN, preferred_element_type=jnp.float32
    )
    branch = (half + half * jnp.tanh(half)).astype(jnp.bfloat16)
    for j in range(total // NEW):
        target = odd_ref if j % 2 else even_ref
        target[(j // 2) * NEW : (j // 2 + 1) * NEW, :] = branch[j * NEW : (j + 1) * NEW, :]

    odd_copy = pltpu.make_async_copy(odd_ref, odd_hbm, sems.at[3])
    odd_copy.start()
    attend_slots(0, lengths, offsets, even_ref, kv, gated)
    leave = [odd_copy]
    for p in range(parts):
        out_ref[p] = lax.dot_general(
            gated[...],
            wo_ref[:, p * width : (p + 1) * width],
            NN,
            preferred_element_type=jnp.float32,
        ).astype(jnp.bfloat16)
        leave.append(pltpu.make_async_copy(out_ref.at[p], out_hbm.at[p], out_sems.at[p]))
        leave[-1].start()
    for c in leave:
        c.wait()


def second_kernel(
    lengths, offsets, b_hbm, keys, values, w_hbm, moved, out_ref, b_ref, w_ref, kv, gated, sems, kv_sems
):
    half_slots, width = kv.shape[0] // 2, kv.shape[2]
    copies = [
        pltpu.make_async_copy(b_hbm, b_ref, sems.at[0]),
        pltpu.make_async_copy(w_hbm, w_ref, sems.at[1]),
    ]
    for c in copies:
        c.start()
    moved_keys, moved_values = moved.at[:half_slots], moved.at[half_slots:]
    copies += cache_copies(1, offsets, keys, values, moved_keys, moved_values, kv, kv_sems)
    for c in copies:
        c.wait()
    attend_slots(1, lengths, offsets, b_ref, kv, gated)
    project_out(gated, w_ref, out_ref, width)


def first(lengths, offsets, x4, gain, w, keys, values, w_out, moved):
    slots, cap, width = keys.shape
    parts, total, _ = x4.shape
    half, wide = total // 2, w.shape[1]
    bf16 = jnp.bfloat16
    return pl.pallas_call(
        first_kernel,
        out_shape=(pltpu.HBM((parts, half, width), bf16), pltpu.HBM((half, wide), bf16)),
        in_specs=[HBM, HBM, ANY, VMEM, HBM, HBM, HBM, HBM, ANY, ANY],
        out_specs=(HBM, HBM),
        scratch_shapes=[
            pltpu.VMEM(x4.shape, bf16),
            pltpu.VMEM(w.shape, bf16),
            pltpu.VMEM(w_out.shape, bf16),
            pltpu.VMEM((slots, cap, width), bf16),
            pltpu.VMEM((total, parts * width), bf16),
            pltpu.VMEM((half, wide), bf16),
            pltpu.VMEM((half, wide), bf16),
            pltpu.VMEM((half, width), bf16),
            pltpu.VMEM((parts, half, width), bf16),
            pltpu.SMEM(lengths.shape, lengths.dtype),
            pltpu.SMEM(offsets.shape, offsets.dtype),
            pltpu.SemaphoreType.DMA((6,)),
            pltpu.SemaphoreType.DMA((slots,)),
            pltpu.SemaphoreType.DMA((parts,)),
        ],
        compiler_params=pltpu.CompilerParams(vmem_limit_bytes=28 * 2**20),
        cost_estimate=pl.CostEstimate(flops=10**8, bytes_accessed=0, transcendentals=0),
    )(in_hbm(lengths), in_hbm(offsets), x4, gain, in_hbm(w), in_hbm(keys), in_hbm(values), in_hbm(w_out), *moved)


def second(lengths, offsets, branches, keys, values, w_out, moved):
    slots, cap, width = keys.shape
    parts, rows = w_out.shape[1] // width, branches.shape[0]
    bf16 = jnp.bfloat16
    operands = [in_hbm(a) for a in (branches, keys, values, w_out, moved)]
    return pl.pallas_call(
        second_kernel,
        out_shape=jax.ShapeDtypeStruct((parts, rows, width), bf16),
        in_specs=[SMEM, SMEM] + [HBM] * len(operands),
        out_specs=VMEM,
        scratch_shapes=[
            pltpu.VMEM(branches.shape, bf16),
            pltpu.VMEM(w_out.shape, bf16),
            pltpu.VMEM((slots, cap, width), bf16),
            pltpu.VMEM((rows, width), bf16),
            pltpu.SemaphoreType.DMA((2,)),
            pltpu.SemaphoreType.DMA((slots,)),
        ],
        compiler_params=pltpu.CompilerParams(vmem_limit_bytes=20 * 2**20),
        cost_estimate=pl.CostEstimate(flops=3 * 10**9, bytes_accessed=0, transcendentals=0),
    )(lengths, offsets, *operands)


def gate_kernel(x_any, gain_ref, out_ref):
    del x_any
    out_ref[...] = gain_ref[...]


def gain_after(x4, gain):
    return pl.pallas_call(
        gate_kernel,
        out_shape=jax.ShapeDtypeStruct(gain.shape, gain.dtype),
        in_specs=[ANY, VMEM],
        out_specs=VMEM,
        compiler_params=pltpu.CompilerParams(vmem_limit_bytes=2**20),
        cost_estimate=pl.CostEstimate(flops=40 * 10**9, bytes_accessed=0, transcendentals=0),
    )(x4, gain)


def combine_kernel(events, even, odd, out_ref):
    parts, rows, _ = even.shape
    half_slots = out_ref.shape[0] // 2 // NEW
    for j in range(2 * half_slots):
        at = slice(j * NEW, (j + 1) * NEW)
        terms_at = slice((j // 2) * NEW, (j // 2 + 1) * NEW)
        terms = odd if j % 2 else even
        total = terms[0, terms_at, :].astype(jnp.float32)
        for p in range(1, parts):
            total = total + terms[p, terms_at, :].astype(jnp.float32)
        out_ref[at, :] = (events[at, :].astype(jnp.float32) + total).astype(out_ref.dtype)


def combine(events, even, odd):
    return pl.pallas_call(
        combine_kernel,
        out_shape=jax.ShapeDtypeStruct(events.shape, events.dtype),
        in_specs=[VMEM, VMEM, VMEM],
        out_specs=VMEM,
        compiler_params=pltpu.CompilerParams(vmem_limit_bytes=6 * 2**20),
    )(events, even, odd)


def in_hbm(array):
    return pltpu.with_memory_space_constraint(array, pltpu.HBM)


def on_device(events, norm_gain, w_uvqk, w_out, cache_keys, cache_values, lengths, swap_offset):
    slots, cap, width = cache_keys.shape
    users = lax.axis_size("user")
    heads = lax.axis_size("head")
    caches = (cache_keys, cache_values)

    def to_heads(blocks):
        return lax.all_to_all(blocks, "head", 0, 0)

    odd_pay, spread = pack(1, 1, lengths, *caches, events, heads)
    across = [(i, (((i + 1) ^ 1) - 1) % users) for i in range(users)]
    odd = lax.ppermute(odd_pay, "user", across)
    gathered = to_heads(spread)
    later_lengths, _ = lax.optimization_barrier((lengths, odd_pay))
    within = [(i, i ^ 1) for i in range(users)]
    even = [lax.ppermute(pay, "user", within) for pay in pack(0, 2, later_lengths, *caches)]

    w = w_uvqk.reshape(w_uvqk.shape[0], 4 * width)
    gain = gain_after(gathered, norm_gain[None, :])
    even_part, odd_branches = first(
        lengths, swap_offset, gathered, gain, w, *caches, w_out, even
    )
    even_terms = to_heads(even_part)
    odd_part = second(lengths, swap_offset, odd_branches, *caches, w_out, odd)
    odd_part, even_terms = lax.optimization_barrier((odd_part, even_terms))
    odd_terms = to_heads(odd_part)
    return combine(events, even_terms, odd_terms)


def solution(mesh):
    return jax.shard_map(
        on_device,
        mesh=mesh,
        in_specs=(
            P("user", "head"),
            P(),
            P(None, None, "head"),
            P("head", None),
            P("user", None, "head"),
            P("user", None, "head"),
            P("user"),
            P("user"),
        ),
        out_specs=P("user", "head"),
        check_vma=False,
    )
```

```python
import functools

import jax
import jax.numpy as jnp
from jax import lax
from jax.experimental import pallas as pl
from jax.experimental.pallas import tpu as pltpu
from jax.sharding import PartitionSpec as P

HEAD = 64
BLOCK = 128
NEW = 64
NT = (((1,), (1,)), ((), ()))
NN = (((1,), (0,)), ((), ()))
VMEM = pl.BlockSpec(memory_space=pltpu.VMEM)
SMEM = pl.BlockSpec(memory_space=pltpu.SMEM)
HBM = pl.BlockSpec(memory_space=pltpu.HBM)
ANY = pl.BlockSpec(memory_space=pl.ANY)


def pack_kernel(side, lengths_hbm, keys, values, *rest):
    *rest, buf, lengths, in_sems, out_sems, sem = rest
    spread = None
    if side == 1:
        events, *pays, spread, events_ref, spread_sems = rest
    else:
        pays = rest
    half_slots, cap, width = keys.shape[0] // 2, keys.shape[1], keys.shape[2]
    places = [pay.at[s] for pay in pays for s in range(pay.shape[0])]
    lengths_copy = pltpu.make_async_copy(lengths_hbm, lengths, sem.at[0])
    lengths_copy.start()
    arrive, leave = [], []
    for s in range(half_slots):
        j = 2 * s + side
        for array, slot in ((values, half_slots + s), (keys, s)):
            arrive.append(pltpu.make_async_copy(array.at[j], buf.at[slot], in_sems.at[slot]))
            leave.append(pltpu.make_async_copy(buf.at[slot], places[slot], out_sems.at[slot]))
    for c in arrive:
        c.start()
    if spread is not None:
        events_copy = pltpu.make_async_copy(events, events_ref, sem.at[1])
        events_copy.start()
    lengths_copy.wait()
    for i, c in enumerate(arrive):
        c.wait()
        if i % 2 == 0:
            s = i // 2
            for block in range(1, cap // BLOCK):

                @pl.when(lengths[2 * s + side] <= block)
                def _():
                    buf[half_slots + s, block * BLOCK : (block + 1) * BLOCK, :] = jnp.zeros(
                        (BLOCK, width), buf.dtype
                    )

        leave[i].start()
    if spread is not None:
        events_copy.wait()
        for p in range(spread.shape[0]):
            copy = pltpu.make_async_copy(events_ref, spread.at[p], spread_sems.at[p])
            copy.start()
            leave.append(copy)
    for c in leave:
        c.wait()


def pack(side, pieces, lengths, keys, values, events=None, parts=0):
    slots, cap, width = keys.shape
    operands = [in_hbm(lengths), in_hbm(keys), in_hbm(values)]
    outs = [pltpu.HBM((slots // pieces, cap, width), keys.dtype)] * pieces
    scratch = []
    if events is not None:
        operands.append(in_hbm(events))
        outs.append(pltpu.HBM((parts,) + events.shape, events.dtype))
        scratch = [pltpu.VMEM(events.shape, events.dtype), pltpu.SemaphoreType.DMA((parts,))]
    return pl.pallas_call(
        functools.partial(pack_kernel, side),
        out_shape=outs,
        in_specs=[HBM] * len(operands),
        out_specs=[HBM] * len(outs),
        scratch_shapes=scratch
        + [
            pltpu.VMEM((slots, cap, width), keys.dtype),
            pltpu.SMEM(lengths.shape, lengths.dtype),
            pltpu.SemaphoreType.DMA((slots,)),
            pltpu.SemaphoreType.DMA((slots,)),
            pltpu.SemaphoreType.DMA((2,)),
        ],
        compiler_params=pltpu.CompilerParams(vmem_limit_bytes=6 * 2**20),
        cost_estimate=pl.CostEstimate(
            flops=0, bytes_accessed=4 * 10**6 if side else 15 * 10**6, transcendentals=0
        ),
    )(*operands)


def cache_copies(side, offsets, keys, values, moved_keys, moved_values, kv, sems):
    half_slots = kv.shape[0] // 2
    waits = []
    for s in range(half_slots):
        j = 2 * s + side
        own = (
            pltpu.make_async_copy(keys.at[j], kv.at[s], sems.at[s]),
            pltpu.make_async_copy(values.at[j], kv.at[half_slots + s], sems.at[half_slots + s]),
        )
        traded = (
            pltpu.make_async_copy(moved_keys.at[s], kv.at[s], sems.at[s]),
            pltpu.make_async_copy(
                moved_values.at[s], kv.at[half_slots + s], sems.at[half_slots + s]
            ),
        )

        waits.append((j, own, traded))
    for kind in range(2):
        for j, own, traded in waits:

            @pl.when(offsets[j] == 0)
            def _():
                own[kind].start()

            @pl.when(offsets[j] != 0)
            def _():
                traded[kind].start()

    return [c for _, own, _ in waits for c in own]


def attend_slots(side, lengths, offsets, b_ref, kv, gated):
    half_slots, cap, width = kv.shape[0] // 2, kv.shape[1], kv.shape[2]
    new = b_ref.shape[0] // half_slots
    heads = width // HEAD
    lane_head = lax.broadcasted_iota(jnp.int32, (new, width), 1) // HEAD
    position = lax.broadcasted_iota(jnp.int32, (1, cap), 1)
    row = lax.broadcasted_iota(jnp.int32, (heads * new, new), 0) % new
    causal = row >= lax.broadcasted_iota(jnp.int32, (heads * new, new), 1)
    pair_lane = lax.broadcasted_iota(jnp.int32, (new, 2 * HEAD), 1) // HEAD

    def weigh(s):
        j = 2 * s + side
        at = slice(s * new, (s + 1) * new)
        queries = b_ref[at, 2 * width : 3 * width] * jnp.bfloat16(0.5 * HEAD**-0.5)
        fresh_keys = b_ref[at, 3 * width :]
        zero = jnp.zeros_like(queries)
        spread_q = jnp.concatenate(
            [jnp.where(lane_head == h, queries, zero) for h in range(heads)], axis=0
        )
        used = jnp.where(offsets[j] == 0, lengths[j] * BLOCK, cap)
        half = lax.dot_general(spread_q, kv[s], NT, preferred_element_type=jnp.float32)
        cached = jnp.where(position < used, half + half * jnp.tanh(half), 0.0)
        half = lax.dot_general(spread_q, fresh_keys, NT, preferred_element_type=jnp.float32)
        fresh = jnp.where(causal, half + half * jnp.tanh(half), 0.0)
        return cached.astype(jnp.bfloat16), fresh.astype(jnp.bfloat16)

    def finish(s, cached, fresh):
        at = slice(s * new, (s + 1) * new)
        gate = b_ref[at, :width].astype(jnp.float32)
        fresh_values = b_ref[at, width : 2 * width]
        total = lax.dot_general(
            cached, kv[half_slots + s], NN, preferred_element_type=jnp.float32
        )
        total = total + lax.dot_general(
            fresh, fresh_values, NN, preferred_element_type=jnp.float32
        )
        for pair in range(heads // 2):
            lanes = slice(2 * HEAD * pair, 2 * HEAD * (pair + 1))
            result = jnp.zeros((new, 2 * HEAD), jnp.float32)
            for within in range(2):
                h = 2 * pair + within
                mine = pair_lane == within
                x = jnp.where(mine, total[h * new : (h + 1) * new, lanes], 0.0)
                average = jnp.sum(x, axis=-1, keepdims=True) * (1.0 / HEAD)
                centred = jnp.where(mine, x - average, 0.0)
                spread = jnp.sum(centred * centred, axis=-1, keepdims=True) * (1.0 / HEAD)
                result = result + centred * lax.rsqrt(spread + 1e-05)
            gated[at, lanes] = (result * gate[:, lanes]).astype(jnp.bfloat16)

    weights = [weigh(s) for s in range(half_slots)]
    for s in range(half_slots):
        finish(s, *weights[s])


def project_out(gated, w_ref, out_ref, width):
    for p in range(out_ref.shape[0]):
        out_ref[p] = lax.dot_general(
            gated[...],
            w_ref[:, p * width : (p + 1) * width],
            NN,
            preferred_element_type=jnp.float32,
        ).astype(jnp.bfloat16)


def first_kernel(
    lengths_hbm, offsets_hbm, x_any, gain_ref, w_hbm, keys, values, wo_hbm, moved,
    out_hbm, odd_hbm,
    x_ref, w_ref, wo_ref, kv, normed_ref, even_ref, odd_ref, gated, out_ref, lengths, offsets,
    sems, kv_sems, out_sems,
):
    parts, total, width = x_ref.shape
    features = parts * width
    x_copy = pltpu.make_async_copy(x_any, x_ref, sems.at[0])
    rest = [
        pltpu.make_async_copy(w_hbm, w_ref, sems.at[1]),
        pltpu.make_async_copy(wo_hbm, wo_ref, sems.at[2]),
    ]
    layout = [
        pltpu.make_async_copy(offsets_hbm, offsets, sems.at[4]),
        pltpu.make_async_copy(lengths_hbm, lengths, sems.at[5]),
    ]
    for c in layout + [x_copy] + rest:
        c.start()
    for c in layout:
        c.wait()
    half_slots = kv.shape[0] // 2
    moved_keys, moved_values = moved.at[:half_slots], moved.at[half_slots:]
    rest += cache_copies(0, offsets, keys, values, moved_keys, moved_values, kv, kv_sems)
    x_copy.wait()
    x = jnp.concatenate([x_ref[p] for p in range(parts)], axis=1).astype(jnp.float32)
    average = jnp.sum(x, axis=-1, keepdims=True) * (1.0 / features)
    centred = x - average
    spread = jnp.sum(centred * centred, axis=-1, keepdims=True) * (1.0 / features)
    normed = centred * lax.rsqrt(spread + 1e-05) * gain_ref[...]
    normed_ref[...] = normed.astype(jnp.bfloat16)

    for c in rest:
        c.wait()
    half = 0.5 * lax.dot_general(
        normed_ref[...], w_ref[...], NN, preferred_element_type=jnp.float32
    )
    branch = (half + half * jnp.tanh(half)).astype(jnp.bfloat16)
    for j in range(total // NEW):
        target = odd_ref if j % 2 else even_ref
        target[(j // 2) * NEW : (j // 2 + 1) * NEW, :] = branch[j * NEW : (j + 1) * NEW, :]

    odd_copy = pltpu.make_async_copy(odd_ref, odd_hbm, sems.at[3])
    odd_copy.start()
    attend_slots(0, lengths, offsets, even_ref, kv, gated)
    leave = [odd_copy]
    for p in range(parts):
        out_ref[p] = lax.dot_general(
            gated[...],
            wo_ref[:, p * width : (p + 1) * width],
            NN,
            preferred_element_type=jnp.float32,
        ).astype(jnp.bfloat16)
        leave.append(pltpu.make_async_copy(out_ref.at[p], out_hbm.at[p], out_sems.at[p]))
        leave[-1].start()
    for c in leave:
        c.wait()


def second_kernel(
    lengths, offsets, b_hbm, keys, values, w_hbm, moved, out_ref, b_ref, w_ref, kv, gated, sems, kv_sems
):
    half_slots, width = kv.shape[0] // 2, kv.shape[2]
    copies = [
        pltpu.make_async_copy(b_hbm, b_ref, sems.at[0]),
        pltpu.make_async_copy(w_hbm, w_ref, sems.at[1]),
    ]
    for c in copies:
        c.start()
    moved_keys, moved_values = moved.at[:half_slots], moved.at[half_slots:]
    copies += cache_copies(1, offsets, keys, values, moved_keys, moved_values, kv, kv_sems)
    for c in copies:
        c.wait()
    attend_slots(1, lengths, offsets, b_ref, kv, gated)
    project_out(gated, w_ref, out_ref, width)


def first(lengths, offsets, x4, gain, w, keys, values, w_out, moved):
    slots, cap, width = keys.shape
    parts, total, _ = x4.shape
    half, wide = total // 2, w.shape[1]
    bf16 = jnp.bfloat16
    return pl.pallas_call(
        first_kernel,
        out_shape=(pltpu.HBM((parts, half, width), bf16), pltpu.HBM((half, wide), bf16)),
        in_specs=[HBM, HBM, ANY, VMEM, HBM, HBM, HBM, HBM, ANY],
        out_specs=(HBM, HBM),
        scratch_shapes=[
            pltpu.VMEM(x4.shape, bf16),
            pltpu.VMEM(w.shape, bf16),
            pltpu.VMEM(w_out.shape, bf16),
            pltpu.VMEM((slots, cap, width), bf16),
            pltpu.VMEM((total, parts * width), bf16),
            pltpu.VMEM((half, wide), bf16),
            pltpu.VMEM((half, wide), bf16),
            pltpu.VMEM((half, width), bf16),
            pltpu.VMEM((parts, half, width), bf16),
            pltpu.SMEM(lengths.shape, lengths.dtype),
            pltpu.SMEM(offsets.shape, offsets.dtype),
            pltpu.SemaphoreType.DMA((6,)),
            pltpu.SemaphoreType.DMA((slots,)),
            pltpu.SemaphoreType.DMA((parts,)),
        ],
        compiler_params=pltpu.CompilerParams(vmem_limit_bytes=28 * 2**20),
        cost_estimate=pl.CostEstimate(flops=10**8, bytes_accessed=0, transcendentals=0),
    )(in_hbm(lengths), in_hbm(offsets), x4, gain, in_hbm(w), in_hbm(keys), in_hbm(values), in_hbm(w_out), moved)


def second(lengths, offsets, branches, keys, values, w_out, moved):
    slots, cap, width = keys.shape
    parts, rows = w_out.shape[1] // width, branches.shape[0]
    bf16 = jnp.bfloat16
    operands = [in_hbm(a) for a in (branches, keys, values, w_out, moved)]
    return pl.pallas_call(
        second_kernel,
        out_shape=jax.ShapeDtypeStruct((parts, rows, width), bf16),
        in_specs=[SMEM, SMEM] + [HBM] * len(operands),
        out_specs=VMEM,
        scratch_shapes=[
            pltpu.VMEM(branches.shape, bf16),
            pltpu.VMEM(w_out.shape, bf16),
            pltpu.VMEM((slots, cap, width), bf16),
            pltpu.VMEM((rows, width), bf16),
            pltpu.SemaphoreType.DMA((2,)),
            pltpu.SemaphoreType.DMA((slots,)),
        ],
        compiler_params=pltpu.CompilerParams(vmem_limit_bytes=20 * 2**20),
        cost_estimate=pl.CostEstimate(flops=3 * 10**9, bytes_accessed=0, transcendentals=0),
    )(lengths, offsets, *operands)


def gate_kernel(x_any, gain_ref, out_ref):
    del x_any
    out_ref[...] = gain_ref[...]


def gain_after(x4, gain):
    return pl.pallas_call(
        gate_kernel,
        out_shape=jax.ShapeDtypeStruct(gain.shape, gain.dtype),
        in_specs=[ANY, VMEM],
        out_specs=VMEM,
        compiler_params=pltpu.CompilerParams(vmem_limit_bytes=2**20),
        cost_estimate=pl.CostEstimate(flops=40 * 10**9, bytes_accessed=0, transcendentals=0),
    )(x4, gain)


def combine_kernel(events, even, odd, out_ref):
    parts, rows, _ = even.shape
    half_slots = out_ref.shape[0] // 2 // NEW
    for j in range(2 * half_slots):
        at = slice(j * NEW, (j + 1) * NEW)
        terms_at = slice((j // 2) * NEW, (j // 2 + 1) * NEW)
        terms = odd if j % 2 else even
        total = terms[0, terms_at, :].astype(jnp.float32)
        for p in range(1, parts):
            total = total + terms[p, terms_at, :].astype(jnp.float32)
        out_ref[at, :] = (events[at, :].astype(jnp.float32) + total).astype(out_ref.dtype)


def combine(events, even, odd):
    return pl.pallas_call(
        combine_kernel,
        out_shape=jax.ShapeDtypeStruct(events.shape, events.dtype),
        in_specs=[VMEM, VMEM, VMEM],
        out_specs=VMEM,
        compiler_params=pltpu.CompilerParams(vmem_limit_bytes=6 * 2**20),
    )(events, even, odd)


def in_hbm(array):
    return pltpu.with_memory_space_constraint(array, pltpu.HBM)


def on_device(events, norm_gain, w_uvqk, w_out, cache_keys, cache_values, lengths, swap_offset):
    slots, cap, width = cache_keys.shape
    users = lax.axis_size("user")
    heads = lax.axis_size("head")
    caches = (cache_keys, cache_values)

    def to_heads(blocks):
        return lax.all_to_all(blocks, "head", 0, 0)

    odd_pay, spread = pack(1, 1, lengths, *caches, events, heads)
    across = [(i, (((i + 1) ^ 1) - 1) % users) for i in range(users)]
    odd = lax.ppermute(odd_pay, "user", across)
    gathered = to_heads(spread)
    later_lengths, _ = lax.optimization_barrier((lengths, odd_pay))
    within = [(i, i ^ 1) for i in range(users)]
    (even_pay,) = pack(0, 1, later_lengths, *caches)
    even = lax.ppermute(even_pay, "user", within)

    w = w_uvqk.reshape(w_uvqk.shape[0], 4 * width)
    gain = gain_after(gathered, norm_gain[None, :])
    even_part, odd_branches = first(
        lengths, swap_offset, gathered, gain, w, *caches, w_out, even
    )
    even_terms = to_heads(even_part)
    odd_part = second(lengths, swap_offset, odd_branches, *caches, w_out, odd)
    odd_part, even_terms = lax.optimization_barrier((odd_part, even_terms))
    odd_terms = to_heads(odd_part)
    return combine(events, even_terms, odd_terms)


def solution(mesh):
    return jax.shard_map(
        on_device,
        mesh=mesh,
        in_specs=(
            P("user", "head"),
            P(),
            P(None, None, "head"),
            P("head", None),
            P("user", None, "head"),
            P("user", None, "head"),
            P("user"),
            P("user"),
        ),
        out_specs=P("user", "head"),
        check_vma=False,
    )
```

```python
import functools

import jax
import jax.numpy as jnp
from jax import lax
from jax.experimental import pallas as pl
from jax.experimental.pallas import tpu as pltpu
from jax.sharding import PartitionSpec as P

HEAD = 64
BLOCK = 128
NEW = 64
NT = (((1,), (1,)), ((), ()))
NN = (((1,), (0,)), ((), ()))
VMEM = pl.BlockSpec(memory_space=pltpu.VMEM)
SMEM = pl.BlockSpec(memory_space=pltpu.SMEM)
HBM = pl.BlockSpec(memory_space=pltpu.HBM)
ANY = pl.BlockSpec(memory_space=pl.ANY)


def pack_kernel(side, lengths_hbm, keys, values, *rest):
    *rest, buf, lengths, in_sems, out_sems, sem = rest
    spread = None
    if side == 1:
        events, *pays, spread, events_ref, spread_sems = rest
    else:
        pays = rest
    half_slots, cap, width = keys.shape[0] // 2, keys.shape[1], keys.shape[2]
    places = [pay.at[s] for pay in pays for s in range(pay.shape[0])]
    lengths_copy = pltpu.make_async_copy(lengths_hbm, lengths, sem.at[0])
    lengths_copy.start()
    arrive, leave = [], []
    for s in range(half_slots):
        j = 2 * s + side
        for array, slot in ((values, half_slots + s), (keys, s)):
            arrive.append(pltpu.make_async_copy(array.at[j], buf.at[slot], in_sems.at[slot]))
            leave.append(pltpu.make_async_copy(buf.at[slot], places[slot], out_sems.at[slot]))
    for c in arrive:
        c.start()
    if spread is not None:
        events_copy = pltpu.make_async_copy(events, events_ref, sem.at[1])
        events_copy.start()
    lengths_copy.wait()
    for i, c in enumerate(arrive):
        c.wait()
        if i % 2 == 0:
            s = i // 2
            for block in range(1, cap // BLOCK):

                @pl.when(lengths[2 * s + side] <= block)
                def _():
                    buf[half_slots + s, block * BLOCK : (block + 1) * BLOCK, :] = jnp.zeros(
                        (BLOCK, width), buf.dtype
                    )

        leave[i].start()
    if spread is not None:
        events_copy.wait()
        for p in range(spread.shape[0]):
            copy = pltpu.make_async_copy(events_ref, spread.at[p], spread_sems.at[p])
            copy.start()
            leave.append(copy)
    for c in leave:
        c.wait()


def pack(side, pieces, lengths, keys, values, events=None, parts=0):
    slots, cap, width = keys.shape
    operands = [in_hbm(lengths), in_hbm(keys), in_hbm(values)]
    outs = [pltpu.HBM((slots // pieces, cap, width), keys.dtype)] * pieces
    scratch = []
    if events is not None:
        operands.append(in_hbm(events))
        outs.append(pltpu.HBM((parts,) + events.shape, events.dtype))
        scratch = [pltpu.VMEM(events.shape, events.dtype), pltpu.SemaphoreType.DMA((parts,))]
    return pl.pallas_call(
        functools.partial(pack_kernel, side),
        out_shape=outs,
        in_specs=[HBM] * len(operands),
        out_specs=[HBM] * len(outs),
        scratch_shapes=scratch
        + [
            pltpu.VMEM((slots, cap, width), keys.dtype),
            pltpu.SMEM(lengths.shape, lengths.dtype),
            pltpu.SemaphoreType.DMA((slots,)),
            pltpu.SemaphoreType.DMA((slots,)),
            pltpu.SemaphoreType.DMA((2,)),
        ],
        compiler_params=pltpu.CompilerParams(vmem_limit_bytes=6 * 2**20),
        cost_estimate=pl.CostEstimate(
            flops=0, bytes_accessed=4 * 10**6 if side else 15 * 10**6, transcendentals=0
        ),
    )(*operands)


def cache_copies(side, offsets, keys, values, moved_keys, moved_values, kv, sems):
    half_slots = kv.shape[0] // 2
    waits = []
    for s in range(half_slots):
        j = 2 * s + side
        own = (
            pltpu.make_async_copy(keys.at[j], kv.at[s], sems.at[s]),
            pltpu.make_async_copy(values.at[j], kv.at[half_slots + s], sems.at[half_slots + s]),
        )
        traded = (
            pltpu.make_async_copy(moved_keys.at[s], kv.at[s], sems.at[s]),
            pltpu.make_async_copy(
                moved_values.at[s], kv.at[half_slots + s], sems.at[half_slots + s]
            ),
        )

        waits.append((j, own, traded))
    for kind in range(2):
        for j, own, traded in waits:

            @pl.when(offsets[j] == 0)
            def _():
                own[kind].start()

            @pl.when(offsets[j] != 0)
            def _():
                traded[kind].start()

    return [c for _, own, _ in waits for c in own]


def attend_slots(side, lengths, offsets, b_ref, kv, gated):
    half_slots, cap, width = kv.shape[0] // 2, kv.shape[1], kv.shape[2]
    new = b_ref.shape[0] // half_slots
    heads = width // HEAD
    lane_head = lax.broadcasted_iota(jnp.int32, (new, width), 1) // HEAD
    position = lax.broadcasted_iota(jnp.int32, (1, cap), 1)
    row = lax.broadcasted_iota(jnp.int32, (heads * new, new), 0) % new
    causal = row >= lax.broadcasted_iota(jnp.int32, (heads * new, new), 1)
    pair_lane = lax.broadcasted_iota(jnp.int32, (new, 2 * HEAD), 1) // HEAD

    def weigh(s):
        j = 2 * s + side
        at = slice(s * new, (s + 1) * new)
        queries = b_ref[at, 2 * width : 3 * width] * jnp.bfloat16(0.5 * HEAD**-0.5)
        fresh_keys = b_ref[at, 3 * width :]
        zero = jnp.zeros_like(queries)
        spread_q = jnp.concatenate(
            [jnp.where(lane_head == h, queries, zero) for h in range(heads)], axis=0
        )
        used = jnp.where(offsets[j] == 0, lengths[j] * BLOCK, cap)
        half = lax.dot_general(spread_q, kv[s], NT, preferred_element_type=jnp.float32)
        cached = jnp.where(position < used, half + half * jnp.tanh(half), 0.0)
        half = lax.dot_general(spread_q, fresh_keys, NT, preferred_element_type=jnp.float32)
        fresh = jnp.where(causal, half + half * jnp.tanh(half), 0.0)
        return cached.astype(jnp.bfloat16), fresh.astype(jnp.bfloat16)

    def finish(s, cached, fresh):
        at = slice(s * new, (s + 1) * new)
        gate = b_ref[at, :width].astype(jnp.float32)
        fresh_values = b_ref[at, width : 2 * width]
        total = lax.dot_general(
            cached, kv[half_slots + s], NN, preferred_element_type=jnp.float32
        )
        total = total + lax.dot_general(
            fresh, fresh_values, NN, preferred_element_type=jnp.float32
        )
        for pair in range(heads // 2):
            lanes = slice(2 * HEAD * pair, 2 * HEAD * (pair + 1))
            result = jnp.zeros((new, 2 * HEAD), jnp.float32)
            for within in range(2):
                h = 2 * pair + within
                mine = pair_lane == within
                x = jnp.where(mine, total[h * new : (h + 1) * new, lanes], 0.0)
                average = jnp.sum(x, axis=-1, keepdims=True) * (1.0 / HEAD)
                centred = jnp.where(mine, x - average, 0.0)
                spread = jnp.sum(centred * centred, axis=-1, keepdims=True) * (1.0 / HEAD)
                result = result + centred * lax.rsqrt(spread + 1e-05)
            gated[at, lanes] = (result * gate[:, lanes]).astype(jnp.bfloat16)

    weights = [weigh(s) for s in range(half_slots)]
    for s in range(half_slots):
        finish(s, *weights[s])


def project_out(gated, w_ref, out_ref, width):
    for p in range(out_ref.shape[0]):
        out_ref[p] = lax.dot_general(
            gated[...],
            w_ref[:, p * width : (p + 1) * width],
            NN,
            preferred_element_type=jnp.float32,
        ).astype(jnp.bfloat16)


def first_kernel(
    lengths_hbm, offsets_hbm, x_any, gain_ref, w_hbm, keys, values, wo_hbm, moved,
    out_hbm, odd_hbm,
    x_ref, w_ref, wo_ref, kv, normed_ref, even_ref, odd_ref, gated, out_ref, lengths, offsets,
    sems, kv_sems, out_sems,
):
    parts, total, width = x_ref.shape
    features = parts * width
    x_copy = pltpu.make_async_copy(x_any, x_ref, sems.at[0])
    rest = [
        pltpu.make_async_copy(w_hbm, w_ref, sems.at[1]),
        pltpu.make_async_copy(wo_hbm, wo_ref, sems.at[2]),
    ]
    layout = [
        pltpu.make_async_copy(offsets_hbm, offsets, sems.at[4]),
        pltpu.make_async_copy(lengths_hbm, lengths, sems.at[5]),
    ]
    for c in layout + [x_copy] + rest:
        c.start()
    for c in layout:
        c.wait()
    half_slots = kv.shape[0] // 2
    moved_keys, moved_values = moved.at[:half_slots], moved.at[half_slots:]
    rest += cache_copies(0, offsets, keys, values, moved_keys, moved_values, kv, kv_sems)
    x_copy.wait()
    x = jnp.concatenate([x_ref[p] for p in range(parts)], axis=1).astype(jnp.float32)
    average = jnp.sum(x, axis=-1, keepdims=True) * (1.0 / features)
    centred = x - average
    spread = jnp.sum(centred * centred, axis=-1, keepdims=True) * (1.0 / features)
    normed = centred * lax.rsqrt(spread + 1e-05) * gain_ref[...]
    normed_ref[...] = normed.astype(jnp.bfloat16)

    for c in rest:
        c.wait()
    half = 0.5 * lax.dot_general(
        normed_ref[...], w_ref[...], NN, preferred_element_type=jnp.float32
    )
    branch = (half + half * jnp.tanh(half)).astype(jnp.bfloat16)
    for j in range(total // NEW):
        target = odd_ref if j % 2 else even_ref
        target[(j // 2) * NEW : (j // 2 + 1) * NEW, :] = branch[j * NEW : (j + 1) * NEW, :]

    odd_copy = pltpu.make_async_copy(odd_ref, odd_hbm, sems.at[3])
    odd_copy.start()
    attend_slots(0, lengths, offsets, even_ref, kv, gated)
    leave = [odd_copy]
    for p in range(parts):
        out_ref[p] = lax.dot_general(
            gated[...],
            wo_ref[:, p * width : (p + 1) * width],
            NN,
            preferred_element_type=jnp.float32,
        ).astype(jnp.bfloat16)
        leave.append(pltpu.make_async_copy(out_ref.at[p], out_hbm.at[p], out_sems.at[p]))
        leave[-1].start()
    for c in leave:
        c.wait()


def second_kernel(
    lengths, offsets, b_hbm, keys, values, w_hbm, moved, out_ref, b_ref, w_ref, kv, gated, sems, kv_sems
):
    half_slots, width = kv.shape[0] // 2, kv.shape[2]
    copies = [
        pltpu.make_async_copy(b_hbm, b_ref, sems.at[0]),
        pltpu.make_async_copy(w_hbm, w_ref, sems.at[1]),
    ]
    for c in copies:
        c.start()
    moved_keys, moved_values = moved.at[:half_slots], moved.at[half_slots:]
    copies += cache_copies(1, offsets, keys, values, moved_keys, moved_values, kv, kv_sems)
    for c in copies:
        c.wait()
    attend_slots(1, lengths, offsets, b_ref, kv, gated)
    project_out(gated, w_ref, out_ref, width)


def first(lengths, offsets, x4, gain, w, keys, values, w_out, moved):
    slots, cap, width = keys.shape
    parts, total, _ = x4.shape
    half, wide = total // 2, w.shape[1]
    bf16 = jnp.bfloat16
    return pl.pallas_call(
        first_kernel,
        out_shape=(pltpu.HBM((parts, half, width), bf16), pltpu.HBM((half, wide), bf16)),
        in_specs=[HBM, HBM, ANY, VMEM, HBM, HBM, HBM, HBM, ANY],
        out_specs=(HBM, HBM),
        scratch_shapes=[
            pltpu.VMEM(x4.shape, bf16),
            pltpu.VMEM(w.shape, bf16),
            pltpu.VMEM(w_out.shape, bf16),
            pltpu.VMEM((slots, cap, width), bf16),
            pltpu.VMEM((total, parts * width), bf16),
            pltpu.VMEM((half, wide), bf16),
            pltpu.VMEM((half, wide), bf16),
            pltpu.VMEM((half, width), bf16),
            pltpu.VMEM((parts, half, width), bf16),
            pltpu.SMEM(lengths.shape, lengths.dtype),
            pltpu.SMEM(offsets.shape, offsets.dtype),
            pltpu.SemaphoreType.DMA((6,)),
            pltpu.SemaphoreType.DMA((slots,)),
            pltpu.SemaphoreType.DMA((parts,)),
        ],
        compiler_params=pltpu.CompilerParams(vmem_limit_bytes=28 * 2**20),
        cost_estimate=pl.CostEstimate(flops=10**8, bytes_accessed=0, transcendentals=0),
    )(in_hbm(lengths), in_hbm(offsets), x4, gain, in_hbm(w), in_hbm(keys), in_hbm(values), in_hbm(w_out), moved)


def second(lengths, offsets, branches, keys, values, w_out, moved):
    slots, cap, width = keys.shape
    parts, rows = w_out.shape[1] // width, branches.shape[0]
    bf16 = jnp.bfloat16
    operands = [in_hbm(a) for a in (branches, keys, values, w_out, moved)]
    return pl.pallas_call(
        second_kernel,
        out_shape=jax.ShapeDtypeStruct((parts, rows, width), bf16),
        in_specs=[SMEM, SMEM] + [HBM] * len(operands),
        out_specs=VMEM,
        scratch_shapes=[
            pltpu.VMEM(branches.shape, bf16),
            pltpu.VMEM(w_out.shape, bf16),
            pltpu.VMEM((slots, cap, width), bf16),
            pltpu.VMEM((rows, width), bf16),
            pltpu.SemaphoreType.DMA((2,)),
            pltpu.SemaphoreType.DMA((slots,)),
        ],
        compiler_params=pltpu.CompilerParams(vmem_limit_bytes=20 * 2**20),
        cost_estimate=pl.CostEstimate(flops=3 * 10**9, bytes_accessed=0, transcendentals=0),
    )(lengths, offsets, *operands)


def gate_kernel(x_any, gain_ref, out_ref):
    del x_any
    out_ref[...] = gain_ref[...]


def gain_after(x4, gain):
    return pl.pallas_call(
        gate_kernel,
        out_shape=jax.ShapeDtypeStruct(gain.shape, gain.dtype),
        in_specs=[ANY, VMEM],
        out_specs=VMEM,
        compiler_params=pltpu.CompilerParams(vmem_limit_bytes=2**20),
        cost_estimate=pl.CostEstimate(flops=40 * 10**9, bytes_accessed=0, transcendentals=0),
    )(x4, gain)


def combine_kernel(events, even, odd, out_hbm, out_ref, sems):
    parts = even.shape[0]
    chunks = sems.shape[0]
    rows = out_ref.shape[0] // chunks
    leave = []
    for chunk in range(chunks):
        for j in range(chunk * rows // NEW, (chunk + 1) * rows // NEW):
            at = slice(j * NEW, (j + 1) * NEW)
            terms_at = slice((j // 2) * NEW, (j // 2 + 1) * NEW)
            terms = odd if j % 2 else even
            total = terms[0, terms_at, :].astype(jnp.float32)
            for p in range(1, parts):
                total = total + terms[p, terms_at, :].astype(jnp.float32)
            out_ref[at, :] = (events[at, :].astype(jnp.float32) + total).astype(out_ref.dtype)
        at = pl.ds(chunk * rows, rows)
        leave.append(pltpu.make_async_copy(out_ref.at[at], out_hbm.at[at], sems.at[chunk]))
        leave[-1].start()
    for c in leave:
        c.wait()


def combine(events, even, odd):
    return pl.pallas_call(
        combine_kernel,
        out_shape=jax.ShapeDtypeStruct(events.shape, events.dtype),
        in_specs=[VMEM, VMEM, VMEM],
        out_specs=HBM,
        scratch_shapes=[
            pltpu.VMEM(events.shape, events.dtype),
            pltpu.SemaphoreType.DMA((4,)),
        ],
        compiler_params=pltpu.CompilerParams(vmem_limit_bytes=6 * 2**20),
    )(events, even, odd)


def in_hbm(array):
    return pltpu.with_memory_space_constraint(array, pltpu.HBM)


def on_device(events, norm_gain, w_uvqk, w_out, cache_keys, cache_values, lengths, swap_offset):
    slots, cap, width = cache_keys.shape
    users = lax.axis_size("user")
    heads = lax.axis_size("head")
    caches = (cache_keys, cache_values)

    def to_heads(blocks):
        return lax.all_to_all(blocks, "head", 0, 0)

    odd_pay, spread = pack(1, 1, lengths, *caches, events, heads)
    across = [(i, (((i + 1) ^ 1) - 1) % users) for i in range(users)]
    odd = lax.ppermute(odd_pay, "user", across)
    gathered = to_heads(spread)
    later_lengths, _ = lax.optimization_barrier((lengths, odd_pay))
    within = [(i, i ^ 1) for i in range(users)]
    (even_pay,) = pack(0, 1, later_lengths, *caches)
    even = lax.ppermute(even_pay, "user", within)

    w = w_uvqk.reshape(w_uvqk.shape[0], 4 * width)
    gain = gain_after(gathered, norm_gain[None, :])
    even_part, odd_branches = first(
        lengths, swap_offset, gathered, gain, w, *caches, w_out, even
    )
    even_terms = to_heads(even_part)
    odd_part = second(lengths, swap_offset, odd_branches, *caches, w_out, odd)
    odd_part, even_terms = lax.optimization_barrier((odd_part, even_terms))
    odd_terms = to_heads(odd_part)
    return combine(events, even_terms, odd_terms)


def solution(mesh):
    return jax.shard_map(
        on_device,
        mesh=mesh,
        in_specs=(
            P("user", "head"),
            P(),
            P(None, None, "head"),
            P("head", None),
            P("user", None, "head"),
            P("user", None, "head"),
            P("user"),
            P("user"),
        ),
        out_specs=P("user", "head"),
        check_vma=False,
    )
```
